32 devices in a mesh: dp: 8 (over z, x), img: 4 (over y, core).
Axes of the slice: x: 2, y: 2, z: 4, core: 2. Of those that a mesh axis runs over, the one named last changes fastest.
Arguments:
- tokens: bfloat16 [4, 448, 56, 512], P('img', 'dp'), may hold values from -6 to 6
- regional: bfloat16 [4, 512, 512], P('img', 'dp'), may hold values from -6 to 6
- pad_mask: int32 [4, 448, 56], P('img', 'dp'), may hold values from 0 to 1, as said below
- keep_mask: int32 [4, 8], P('img'), may hold values 0 or 1
- window_slot: int32 [4, 512], P('img'), may hold values from 0 to 511, as said below
- ln1_gain: float32 [512], replicated, may hold values from 0.5 to 1.5
- ln1_bias: float32 [512], replicated, may hold values from -1.75 to 1.75
- w_qkv: bfloat16 [512, 1536], replicated, may hold values from -0.25 to 0.25
- bias_q: float32 [512], replicated, may hold values from -1.75 to 1.75
- bias_v: float32 [512], replicated, may hold values from -1.75 to 1.75
- w_out: bfloat16 [512, 512], replicated, may hold values from -1 to 1
- bias_out: float32 [512], replicated, may hold values from -1.75 to 1.75
- ln2_gain: float32 [512], replicated, may hold values from 0.5 to 1.5
- ln2_bias: float32 [512], replicated, may hold values from -1.75 to 1.75
- w_fc1: bfloat16 [512, 2048], replicated, may hold values from -0.25 to 0.25
- bias_fc1: float32 [2048], replicated, may hold values from -3 to 3
- w_fc2: bfloat16 [2048, 512], replicated, may hold values from -0.125 to 0.125
- bias_fc2: float32 [512], replicated, may hold values from -1.75 to 1.75
- cot_local: bfloat16 [4, 512, 49, 512], P('img', 'dp'), may hold values from -6 to 6
- cot_regional: bfloat16 [4, 512, 512], P('img', 'dp'), may hold values from -6 to 6
Outputs:
- out_local: bfloat16 [4, 512, 49, 512], P('img', 'dp')
- out_regional: bfloat16 [4, 512, 512], P('img', 'dp')
- grad_tokens: bfloat16 [4, 448, 56, 512], P('img', 'dp')
- grad_regional: bfloat16 [4, 512, 512], P('img', 'dp')
- grad_ln1_gain: float32 [512], replicated
- grad_ln1_bias: float32 [512], replicated
- grad_w_qkv: float32 [512, 1536], replicated
- grad_bias_q: float32 [512], replicated
- grad_bias_v: float32 [512], replicated
- grad_w_out: float32 [512, 512], replicated
- grad_bias_out: float32 [512], replicated
- grad_ln2_gain: float32 [512], replicated
- grad_ln2_bias: float32 [512], replicated
- grad_w_fc1: float32 [512, 2048], replicated
- grad_bias_fc1: float32 [2048], replicated
- grad_w_fc2: float32 [2048, 512], replicated
- grad_bias_fc2: float32 [512], replicated
The draws below stay inside these ranges and needn't reach their ends.
Inputs may be any that keep to these rules, and one draw needn't show every extreme that they name: `pad_mask`: image i of a group holds rows i * 56 to (i + 1) * 56 - 1; its live patches form a top-left rectangle of more than 7 rows and more than 7 columns. Each group's row is a permutation. Window w lies on device w // 64 of dp and goes to slot window_slot[w] on device window_slot[w] // 64; every device sends exactly 8 windows to each device it sends to, never more.
All inputs are finite; a program needn't handle non-finite values. No bound on the sum of `keep_mask` on one device may be relied on, other than what follows from the above.
Results may differ from the reference program's by a relative error of at most 0.02.
Values may be sent and summed in bfloat16 or wider, within the bound.
No kernel may reach another device: no remote copies, remote signals or barrier semaphores. Data moves between devices by JAX's collectives and lax.ppermute only.
A program may use at most 320 MiB of HBM per device.

```python
import jax
import jax.numpy as jnp
from jax import lax

D = 512
HEADS = 16
HDIM = 32
MLP = 2048
WIN_SIDE = 7
REG_SIDE = 8
WIN_DEV = 64
WIN = 49
SIDE = 56
REGIONS = 64
GROUPS = 4
NWIN_GRP = 512
IMGS_GRP = 8
ROWS_GRP = 448
CAP = 8


def draw_pad_mask(key, part):
    key = jax.random.fold_in(key, 11)
    high_key, wide_key = jax.random.split(key)
    heights = jax.random.randint(high_key, (GROUPS, IMGS_GRP), WIN_SIDE + 1, SIDE + 1)
    widths = jax.random.randint(wide_key, (GROUPS, IMGS_GRP), WIN_SIDE + 1, SIDE + 1)
    positions = jnp.arange(SIDE)
    inside = (positions[None, None, :, None] < heights[:, :, None, None]) & (positions[None, None, None, :] < widths[:, :, None, None])
    return inside.reshape(GROUPS, ROWS_GRP, SIDE).astype(jnp.int32)


def draw_window_slot(key, part):
    key = jax.random.fold_in(key, 23)
    devices = NWIN_GRP // WIN_DEV
    spread = min(WIN_DEV, devices)

    def one_group(group_key):
        offset_key, send_key, take_key = jax.random.split(group_key, 3)
        offsets = jax.random.permutation(offset_key, devices)[:spread]
        sender = jax.vmap(lambda inner_key: jax.random.permutation(inner_key, WIN_DEV))(jax.random.split(send_key, devices))
        receiver_order = jax.vmap(lambda inner_key: jax.random.permutation(inner_key, WIN_DEV))(jax.random.split(take_key, devices))
        offset_index = sender % spread
        copy_index = sender // spread
        source = jnp.arange(devices)[:, None]
        target = (source + offsets[offset_index]) % devices
        slot_index = receiver_order[target, offset_index * CAP + copy_index]
        return (target * WIN_DEV + slot_index).reshape(NWIN_GRP).astype(jnp.int32)
    return jax.vmap(one_group)(jax.random.split(key, GROUPS))


def with_ends(drawn, stream_key, low, high):
    extent = drawn.shape
    place = [jax.random.randint(jax.random.fold_in(stream_key, axis), (), 0, extent[axis]) for axis in range(len(extent))]
    drawn = drawn.at[tuple(place)].set(low)
    longest = extent.index(max(extent))
    place[longest] = (place[longest] + 1) % extent[longest]
    return drawn.at[tuple(place)].set(high)


def level_of(own_key, extent, cuts, low, top_value):
    loudness = 1.0
    for axis_at, shards_of in cuts:
        steps = jax.random.uniform(jax.random.fold_in(jax.random.fold_in(own_key, 6), axis_at), (shards_of,), jnp.float32, low / len(cuts), top_value / len(cuts))
        loudness = loudness * jnp.repeat(jnp.exp(steps), extent[axis_at] // shards_of).reshape((-1,) + (1,) * (len(extent) - 1 - axis_at))
    return loudness


def bell_draw(rng, shape, deviation, most, pieces=(), kind=jnp.bfloat16):
    gain = level_of(rng, shape, pieces, -0.22, 0.18) if pieces else 1.0
    entries = jax.random.normal(rng, shape, jnp.float32) * deviation * gain
    return jnp.minimum(jnp.maximum(entries, -most), most).astype(kind)


def setup_inputs(seed: int = 0) -> dict:
    seeds = jax.random.split(jax.random.key(seed), 21)
    return {
        "tokens": bell_draw(seeds[0], (GROUPS, ROWS_GRP, SIDE, D), 1.0, 6.0, ((0, 4), (1, 8))),
        "regional": bell_draw(seeds[1], (GROUPS, NWIN_GRP, D), 1.0, 6.0, ((0, 4), (1, 8))),
        "pad_mask": draw_pad_mask(jax.random.fold_in(seeds[20], 71), 0),
        "keep_mask": with_ends((jax.random.randint(seeds[3], (GROUPS, IMGS_GRP), 0, 4) < 3).astype(jnp.int32), jax.random.fold_in(seeds[3], 1), 0, 1),
        "window_slot": draw_window_slot(jax.random.fold_in(seeds[20], 71), 0),
        "ln1_gain": jnp.clip(jax.random.uniform(seeds[5], (D,), jnp.float32, 0.5, 1.5), 0.5, 1.5),
        "ln1_bias": bell_draw(seeds[6], (D,), 0.3, 1.75, (), jnp.float32),
        "w_qkv": bell_draw(seeds[7], (D, 3 * D), D ** -0.5, 0.25),
        "bias_q": bell_draw(seeds[8], (D,), 0.3, 1.75, (), jnp.float32),
        "bias_v": bell_draw(seeds[9], (D,), 0.3, 1.75, (), jnp.float32),
        "w_out": bell_draw(seeds[10], (D, D), (D // 16) ** -0.5, 1.0),
        "bias_out": bell_draw(seeds[11], (D,), 0.3, 1.75, (), jnp.float32),
        "ln2_gain": jnp.clip(jax.random.uniform(seeds[12], (D,), jnp.float32, 0.5, 1.5), 0.5, 1.5),
        "ln2_bias": bell_draw(seeds[13], (D,), 0.3, 1.75, (), jnp.float32),
        "w_fc1": bell_draw(seeds[14], (D, MLP), D ** -0.5, 0.25),
        "bias_fc1": bell_draw(seeds[15], (MLP,), 0.5, 3.0, (), jnp.float32),
        "w_fc2": bell_draw(seeds[16], (MLP, D), MLP ** -0.5, 0.125),
        "bias_fc2": bell_draw(seeds[17], (D,), 0.3, 1.75, (), jnp.float32),
        "cot_local": bell_draw(seeds[18], (GROUPS, NWIN_GRP, WIN, D), 1.0, 6.0, ((0, 4), (1, 8))),
        "cot_regional": bell_draw(seeds[19], (GROUPS, NWIN_GRP, D), 1.0, 6.0, ((0, 4), (1, 8))),
    }


norm_eps = 1e-05
survive = 0.9
highest = lax.Precision.HIGHEST

@jax.custom_vjp
def low(v):
    return lax.optimization_barrier(v.astype(jnp.bfloat16)).astype(jnp.float32)

@jax.custom_vjp
def low_back(v):
    return v

def low_keep(v):
    return (low(v), None)

def low_pass(kept, grad):
    return (grad,)

def back_keep(v):
    return (v, None)

def back_low(kept, grad):
    return (low(grad),)
low.defvjp(low_keep, low_pass)
low_back.defvjp(back_keep, back_low)

def layer_norm(values, scale_gain, shift_bias):
    centered = values - lax.optimization_barrier(jnp.mean(values, axis=-1, keepdims=True))
    spread = lax.optimization_barrier(jnp.mean(centered * centered, axis=-1, keepdims=True))
    return centered * lax.rsqrt(spread + norm_eps) * scale_gain + shift_bias

def project(values, matrix):
    return jnp.einsum('...i,ij->...j', values, matrix, precision=highest)

def split_heads(values):
    return values.reshape(values.shape[:-1] + (HEADS, HDIM))

def attention_branch(normed, allowed, params):
    w_qkv, bias_q, bias_v, w_out, bias_out = params
    combined = project(normed, w_qkv)
    queries = split_heads(low(low_back(combined[..., :D] + bias_q)))
    key_heads = split_heads(low(low_back(combined[..., D:2 * D])))
    values = split_heads(low(low_back(combined[..., 2 * D:] + bias_v)))
    scores = low_back(jnp.einsum('bqhe,bkhe->bhqk', queries, key_heads, precision=highest) * HDIM ** (-0.5))
    attn_probs = low(jax.nn.softmax(jnp.where(allowed, scores, -1e+30), axis=-1))
    mixed_heads = jnp.einsum('bhqk,bkhe->bqhe', attn_probs, values, precision=highest)
    mixed_rows = low(low_back(mixed_heads.reshape(mixed_heads.shape[:-2] + (D,))))
    return low_back(project(mixed_rows, w_out) + bias_out)

def image_layer(weights, windows, regional, live_tokens, keep_scale):
    ln1_gain, ln1_bias, w_qkv, bias_q, bias_v, w_out, bias_out, ln2_gain, ln2_bias, w_fc1, bias_fc1, w_fc2, bias_fc2 = weights
    attn_params = (w_qkv, bias_q, bias_v, w_out, bias_out)
    region_live = live_tokens[:, 0]
    normed = low(layer_norm(regional, ln1_gain, ln1_bias))
    branch = attention_branch(normed[None], region_live[None, None, None, :], attn_params)[0]
    region_mid = low(low_back(regional + keep_scale * branch))
    joined = jnp.concatenate([region_mid[:, None, :], windows], axis=1)
    key_live = jnp.concatenate([jnp.ones((live_tokens.shape[0], 1), bool), live_tokens], axis=1)
    normed = low(layer_norm(joined, ln1_gain, ln1_bias))
    joined = joined + keep_scale * attention_branch(normed, key_live[:, None, None, :], attn_params)
    normed = low(layer_norm(joined, ln2_gain, ln2_bias))
    hidden = low(jax.nn.gelu(low_back(project(normed, w_fc1) + bias_fc1), approximate=False))
    return joined + keep_scale * low_back(project(hidden, w_fc2) + bias_fc2)

def to_windows(array):
    trailing = array.shape[3:]
    blocks = array.reshape((array.shape[0], array.shape[1] // WIN_SIDE, WIN_SIDE, REG_SIDE, WIN_SIDE) + trailing)
    blocks = jnp.swapaxes(blocks, 2, 3)
    return blocks.reshape((array.shape[0], NWIN_GRP, WIN) + trailing)

def reference(tokens, regional, pad_mask, keep_mask, window_slot, ln1_gain, ln1_bias, w_qkv, bias_q, bias_v, w_out, bias_out, ln2_gain, ln2_bias, w_fc1, bias_fc1, w_fc2, bias_fc2, cot_local, cot_regional):
    weights = tuple((argument.astype(jnp.float32) for argument in (ln1_gain, ln1_bias, w_qkv, bias_q, bias_v, w_out, bias_out, ln2_gain, ln2_bias, w_fc1, bias_fc1, w_fc2, bias_fc2)))
    live_tokens = to_windows(pad_mask != 0).reshape(GROUPS * IMGS_GRP, REGIONS, WIN)
    keep_scale = (keep_mask.astype(jnp.float32) / survive).reshape(GROUPS * IMGS_GRP)

    def forward(token_values, region_values, params):
        windows = to_windows(token_values).reshape(GROUPS * IMGS_GRP, REGIONS, WIN, D)
        region_rows = region_values.reshape(GROUPS * IMGS_GRP, REGIONS, D)
        per_image = jax.checkpoint(lambda packed: image_layer(params, *packed))
        result = lax.map(per_image, (windows, region_rows, live_tokens, keep_scale))
        result = result.reshape(GROUPS, NWIN_GRP, WIN + 1, D)
        return jax.vmap(lambda window_rows, slot_index: jnp.zeros_like(window_rows).at[slot_index].set(window_rows))(result, window_slot)
    placed, pullback = jax.vjp(forward, tokens.astype(jnp.float32), regional.astype(jnp.float32), weights)
    cotangent = jnp.concatenate([cot_regional.astype(jnp.float32)[:, :, None, :], cot_local.astype(jnp.float32)], axis=2)
    grad_tokens, grad_regional, grads = pullback(cotangent)
    return (placed[:, :, 1:].astype(jnp.bfloat16), placed[:, :, 0].astype(jnp.bfloat16), grad_tokens.astype(jnp.bfloat16), grad_regional.astype(jnp.bfloat16), grads[0], grads[1], grads[2], grads[3], grads[4], grads[5], grads[6], grads[7], grads[8], grads[9], grads[10], grads[11], grads[12])
```

```python
import jax
import jax.numpy as jnp
from jax import lax
from jax.sharding import PartitionSpec as P

HEADS = 16
HDIM = 32
WIN_SIDE = 7
REG_SIDE = 8
REGIONS = 64


norm_eps = 1e-05
survive = 0.9


def layer_norm(values, scale_gain, shift_bias):
    centered = values - jnp.mean(values, axis=-1, keepdims=True)
    spread = jnp.mean(centered * centered, axis=-1, keepdims=True)
    return centered * lax.rsqrt(spread + norm_eps) * scale_gain + shift_bias


def gelu_exact(values):
    return jax.nn.gelu(values, approximate=False)


def split_heads(values):
    return values.reshape(values.shape[:-1] + (HEADS, HDIM))


def merge_heads(values):
    return values.reshape(values.shape[:-2] + (HEADS * HDIM,))


def linear(values, matrix):
    return jnp.einsum("...i,ij->...j", values, matrix, preferred_element_type=jnp.float32)


def linear_back(grads, matrix):
    return jnp.einsum("...j,ij->...i", grads, matrix, preferred_element_type=jnp.float32)


def outer_sum(values, grads):
    flat_values = values.reshape(-1, values.shape[-1])
    flat_grads = grads.reshape(-1, grads.shape[-1])
    return jnp.einsum("ti,tj->ij", flat_values, flat_grads, preferred_element_type=jnp.float32)


def row_total(grads):
    return jnp.sum(grads.astype(jnp.float32).reshape(-1, grads.shape[-1]), axis=0)


def project_heads(normed, w_qkv, bias_q, bias_v):
    combined = linear(normed, w_qkv)
    model_width = bias_q.shape[0]
    queries = (combined[..., :model_width] + bias_q).astype(jnp.bfloat16)
    key_rows = combined[..., model_width : 2 * model_width].astype(jnp.bfloat16)
    values = (combined[..., 2 * model_width :] + bias_v).astype(jnp.bfloat16)
    return (queries, key_rows, values)


def masked_scores(queries, key_heads, allowed):
    raw_scores = jnp.einsum(
        "bqhe,bkhe->bhqk", queries, key_heads, preferred_element_type=jnp.float32
    )
    return jnp.where(allowed, raw_scores * HDIM ** (-0.5), -1e30)


def attend_forward(queries, key_heads, values, allowed):
    scores = masked_scores(queries, key_heads, allowed)
    highest_score = jnp.max(scores, axis=-1, keepdims=True)
    weighted = jnp.exp(scores - highest_score)
    normal_sum = jnp.sum(weighted, axis=-1, keepdims=True)
    attn_probs = (weighted / normal_sum).astype(jnp.bfloat16)
    mixed_heads = jnp.einsum(
        "bhqk,bkhe->bqhe", attn_probs, values, preferred_element_type=jnp.float32
    )
    return (mixed_heads, highest_score + jnp.log(normal_sum))


def attend_backward(queries, key_heads, values, allowed, log_total, grad_mixed):
    attn_probs = jnp.exp(masked_scores(queries, key_heads, allowed) - log_total)
    grad_values = jnp.einsum(
        "bhqk,bqhe->bkhe",
        attn_probs.astype(jnp.bfloat16),
        grad_mixed,
        preferred_element_type=jnp.float32,
    )
    grad_probs = jnp.einsum(
        "bqhe,bkhe->bhqk", grad_mixed, values, preferred_element_type=jnp.float32
    )
    row_inner = jnp.sum(attn_probs * grad_probs, axis=-1, keepdims=True)
    grad_scores = (attn_probs * (grad_probs - row_inner)).astype(jnp.bfloat16)
    factor = HDIM ** (-0.5)
    grad_queries = (
        jnp.einsum("bhqk,bkhe->bqhe", grad_scores, key_heads, preferred_element_type=jnp.float32)
        * factor
    )
    grad_keys = (
        jnp.einsum("bhqk,bqhe->bkhe", grad_scores, queries, preferred_element_type=jnp.float32)
        * factor
    )
    return (grad_queries, grad_keys, grad_values)


def band_to_windows(band_values, win_count):
    trailing = band_values.shape[2:]
    blocks = band_values.reshape(
        (band_values.shape[0] // WIN_SIDE, WIN_SIDE, REG_SIDE, WIN_SIDE) + trailing
    )
    return jnp.swapaxes(blocks, 1, 2).reshape((win_count, WIN_SIDE * WIN_SIDE) + trailing)


def windows_to_band(windows, band_rows):
    trailing = windows.shape[2:]
    blocks = windows.reshape((band_rows // WIN_SIDE, REG_SIDE, WIN_SIDE, WIN_SIDE) + trailing)
    return jnp.swapaxes(blocks, 1, 2).reshape((band_rows, REG_SIDE * WIN_SIDE) + trailing)


def keep_for(image_ids, keep_row):
    image_match = image_ids[:, None] == jnp.arange(keep_row.shape[0])[None, :]
    return (
        jnp.sum(jnp.where(image_match, keep_row[None, :], 0), axis=1).astype(jnp.float32) / survive
    )


def rank_of(keys):
    return jnp.sum(keys[None, :] < keys[:, None], axis=1)


def reduce_stages():
    img_bits = [("img", bit) for bit in range(lax.axis_size("img").bit_length() - 1)]
    dp_bits = [("dp", bit) for bit in range(lax.axis_size("dp").bit_length() - 1)]
    rest = img_bits[1:] + dp_bits
    return [img_bits[:1]] + [rest[at : at + 2] for at in range(0, len(rest), 2)]


def stage_peers(stage):
    dp_size, img_size = lax.axis_size("dp"), lax.axis_size("img")
    flat = lax.axis_index("dp") * img_size + lax.axis_index("img")
    masks = [(1 << bit) * (img_size if name == "dp" else 1) for name, bit in stage]
    own = sum(((flat // mask) % 2) << place for place, mask in enumerate(masks))
    moves = []
    for offset in range(1, 1 << len(masks)):
        flip = sum(mask for place, mask in enumerate(masks) if offset >> place & 1)
        moves.append((offset, [(at, at ^ flip) for at in range(dp_size * img_size)]))
    return own, moves


def reduce_shards(rows):
    for stage in reduce_stages():
        own, moves = stage_peers(stage)
        parts = rows.reshape((1 << len(stage), -1) + rows.shape[1:])
        got = [
            lax.ppermute(
                lax.dynamic_index_in_dim(parts, own ^ offset, 0, False), ("dp", "img"), pairs
            )
            for offset, pairs in moves
        ]
        total = lax.dynamic_index_in_dim(parts, own, 0, False).astype(jnp.float32)
        for piece in got:
            total = total + piece.astype(jnp.float32)
        rows = total.astype(jnp.bfloat16)
    return rows


def gather_shards(rows):
    for stage in reversed(reduce_stages()):
        own, moves = stage_peers(stage)
        got = [lax.ppermute(rows, ("dp", "img"), pairs) for offset, pairs in moves]
        pieces = [rows] + got
        ordered = []
        for place in range(len(pieces)):
            piece = pieces[0]
            for offset in range(1, len(pieces)):
                piece = jnp.where((own ^ place) == offset, pieces[offset], piece)
            ordered.append(piece)
        rows = jnp.concatenate(ordered, axis=0)
    return rows


def all_sum(rows):
    return gather_shards(reduce_shards(rows.astype(jnp.bfloat16)))


def small_rows(vectors, width):
    flat = jnp.concatenate([vector.reshape(-1, width) for vector in vectors], axis=0)
    return flat


def pack(matrices, vectors, parts):
    width = 512
    blocks = []
    for matrix in matrices:
        columns = matrix.shape[1] // width
        blocks.extend(matrix[:, at * width : (at + 1) * width] for at in range(columns))
    main = jnp.concatenate(blocks, axis=0).astype(jnp.bfloat16)
    small = jnp.concatenate([vector.reshape(-1, width) for vector in vectors], axis=0)
    extra = jnp.zeros((parts, 8, width), jnp.bfloat16)
    extra = extra.at[0, : small.shape[0]].set(small.astype(jnp.bfloat16))
    main = main.reshape(parts, -1, width)
    return jnp.concatenate([main, extra], axis=1).reshape(-1, width)


def unpack(rows, shapes, vector_sizes, parts):
    width = 512
    rows = rows.reshape(parts, -1, width)
    main = rows[:, :-8].reshape(-1, width)
    small = rows[0, -8:].astype(jnp.float32)
    outs, at = [], 0
    for height, columns in shapes:
        blocks = []
        for _ in range(columns // width):
            blocks.append(main[at : at + height])
            at += height
        outs.append(jnp.concatenate(blocks, axis=1).astype(jnp.float32))
    vectors, at = [], 0
    for size in vector_sizes:
        vectors.append(small[at : at + size // width].reshape(size))
        at += size // width
    return outs, vectors


def shards(
    tokens,
    regional,
    pad_mask,
    keep_mask,
    window_slot,
    ln1_gain,
    ln1_bias,
    w_qkv,
    bias_q,
    bias_v,
    w_out,
    bias_out,
    ln2_gain,
    ln2_bias,
    w_fc1,
    bias_fc1,
    w_fc2,
    bias_fc2,
    cot_local,
    cot_regional,
):
    devices = lax.axis_size("dp")
    parts = devices * lax.axis_size("img")
    own_rank = lax.axis_index("dp")
    win_count = regional.shape[1]
    all_windows = window_slot.shape[1]
    model_width = regional.shape[2]
    window_len = cot_local.shape[2]
    band_rows = tokens.shape[1]
    images_dev = win_count // REGIONS
    slot_of = window_slot[0]
    places = jnp.arange(win_count)
    own_target = lax.dynamic_slice_in_dim(slot_of, own_rank * win_count, win_count) // win_count
    own_place = rank_of(own_target * win_count + places)
    slot_hit = slot_of[None, :] == (own_rank * win_count + places)[:, None]
    window_here = jnp.sum(jnp.where(slot_hit, jnp.arange(all_windows)[None, :], 0), axis=1)
    here_place = rank_of(window_here)
    own_pick = (places[:, None] == own_place[None, :]).astype(jnp.bfloat16)
    here_pick = (places[:, None] == here_place[None, :]).astype(jnp.bfloat16)

    def deal(values, sender, receiver, name):
        packed = jnp.einsum("ps,tsf->ptf", sender, values, preferred_element_type=jnp.float32)
        packed = packed.astype(jnp.bfloat16)
        came = lax.all_to_all(packed, "dp", split_axis=0, concat_axis=0, tiled=True)
        return jnp.einsum(name, receiver, came, preferred_element_type=jnp.float32)

    cot_rows = jnp.concatenate([cot_regional, jnp.swapaxes(cot_local[0], 0, 1)], axis=0)
    grad_result = deal(cot_rows, here_pick, own_pick, "pw,ptf->wtf")
    keep_rows = keep_for((own_rank * win_count) // REGIONS + jnp.arange(images_dev), keep_mask[0])
    keep_rows = jnp.repeat(keep_rows, REGIONS)[:, None, None]
    keep_band = keep_rows[:, 0, 0]
    windows = band_to_windows(tokens[0], win_count)
    live_local = band_to_windows(pad_mask[0], win_count) != 0
    region_shape = (images_dev, REGIONS, HEADS, HDIM)
    region_band = regional[0].astype(jnp.float32)
    normed_region = layer_norm(region_band, ln1_gain, ln1_bias).astype(jnp.bfloat16)
    queries_r, keys_r, values_r = project_heads(normed_region, w_qkv, bias_q, bias_v)
    query_heads_r = queries_r.reshape(region_shape)
    key_heads_r = keys_r.reshape(region_shape)
    value_heads_r = values_r.reshape(region_shape)
    region_allowed = live_local[:, 0].reshape(images_dev, 1, 1, REGIONS)
    mixed_heads_r, total_r = attend_forward(
        query_heads_r, key_heads_r, value_heads_r, region_allowed
    )
    mixed_r = mixed_heads_r.reshape(win_count, model_width).astype(jnp.bfloat16)
    region_mid = (
        region_band + keep_band[:, None] * (linear(mixed_r, w_out) + bias_out)
    ).astype(jnp.bfloat16)
    joined = jnp.concatenate([region_mid[:, None, :], windows], axis=1).astype(jnp.float32)
    normed_local = layer_norm(joined, ln1_gain, ln1_bias).astype(jnp.bfloat16)
    queries_l, keys_l, values_l = project_heads(normed_local, w_qkv, bias_q, bias_v)
    local_allowed = jnp.concatenate([jnp.ones((win_count, 1), bool), live_local], axis=1)[
        :, None, None, :
    ]
    query_heads_l = split_heads(queries_l)
    key_heads_l = split_heads(keys_l)
    value_heads_l = split_heads(values_l)
    mixed_l, total_l = attend_forward(query_heads_l, key_heads_l, value_heads_l, local_allowed)
    mixed_l = merge_heads(mixed_l).astype(jnp.bfloat16)
    after_attention = joined + keep_rows * (linear(mixed_l, w_out) + bias_out)
    normed_mlp = layer_norm(after_attention, ln2_gain, ln2_bias).astype(jnp.bfloat16)
    pre_act = linear(normed_mlp, w_fc1) + bias_fc1
    hidden = gelu_exact(pre_act).astype(jnp.bfloat16)
    result = after_attention + keep_rows * (linear(hidden, w_fc2) + bias_fc2)
    result_rows = jnp.swapaxes(result.astype(jnp.bfloat16), 0, 1)
    out_rows = deal(result_rows, own_pick, here_pick, "ps,ptf->tsf").astype(jnp.bfloat16)
    out_regional = out_rows[0]
    out_local = jnp.swapaxes(out_rows[1:], 0, 1)
    grad_mlp = (keep_rows * grad_result).astype(jnp.bfloat16)
    grad_w_fc2 = outer_sum(hidden, grad_mlp)
    grad_bias_fc2 = row_total(grad_mlp)
    unused, gelu_pull = jax.vjp(gelu_exact, pre_act)
    grad_pre = gelu_pull(linear_back(grad_mlp, w_fc2))[0].astype(jnp.bfloat16)
    grad_w_fc1 = outer_sum(normed_mlp, grad_pre)
    grad_bias_fc1 = row_total(grad_pre)
    unused, norm_pull = jax.vjp(layer_norm, after_attention, ln2_gain, ln2_bias)
    grad_norm_in, grad_ln2_gain, grad_ln2_bias = norm_pull(linear_back(grad_pre, w_fc1))
    early = all_sum(
        pack(
            [grad_w_fc1, grad_w_fc2],
            [grad_bias_fc1, grad_bias_fc2, grad_ln2_gain, grad_ln2_bias],
            parts,
        )
    )
    (grad_w_fc1, grad_w_fc2), (grad_bias_fc1, grad_bias_fc2, grad_ln2_gain, grad_ln2_bias) = (
        unpack(
            early,
            [w_fc1.shape, w_fc2.shape],
            [bias_fc1.shape[0], model_width, model_width, model_width],
            parts,
        )
    )
    grad_after = grad_result + grad_norm_in
    grad_branch_l = (keep_rows * grad_after).astype(jnp.bfloat16)
    grad_w_out = outer_sum(mixed_l, grad_branch_l)
    grad_bias_out = row_total(grad_branch_l)
    grad_mixed_l = split_heads(linear_back(grad_branch_l, w_out).astype(jnp.bfloat16))
    grad_q_l, grad_k_l, grad_v_l = attend_backward(
        query_heads_l, key_heads_l, value_heads_l, local_allowed, total_l, grad_mixed_l
    )
    grad_qkv_l = jnp.concatenate(
        [merge_heads(grad_q_l), merge_heads(grad_k_l), merge_heads(grad_v_l)], axis=-1
    ).astype(jnp.bfloat16)
    grad_w_qkv = outer_sum(normed_local, grad_qkv_l)
    grad_bias_q = row_total(grad_qkv_l[..., :model_width])
    grad_bias_v = row_total(grad_qkv_l[..., 2 * model_width :])
    unused, local_pull = jax.vjp(layer_norm, joined, ln1_gain, ln1_bias)
    grad_joined_in, grad_ln1_gain, grad_ln1_bias = local_pull(linear_back(grad_qkv_l, w_qkv))
    grad_joined = (grad_after + grad_joined_in).astype(jnp.bfloat16)
    grad_band = windows_to_band(grad_joined[:, 1:], band_rows)
    raster_came = grad_joined[:, 0].astype(jnp.float32)
    grad_branch_r = (keep_band[:, None] * raster_came).astype(jnp.bfloat16)
    grad_w_out = grad_w_out + outer_sum(mixed_r, grad_branch_r)
    grad_bias_out = grad_bias_out + row_total(grad_branch_r)
    grad_mixed_r = linear_back(grad_branch_r, w_out).astype(jnp.bfloat16).reshape(region_shape)
    grad_q_r, grad_k_r, grad_v_r = attend_backward(
        query_heads_r, key_heads_r, value_heads_r, region_allowed, total_r, grad_mixed_r
    )
    grad_qkv_r = jnp.concatenate(
        [
            grad_q_r.reshape(win_count, model_width),
            grad_k_r.reshape(win_count, model_width),
            grad_v_r.reshape(win_count, model_width),
        ],
        axis=-1,
    ).astype(jnp.bfloat16)
    grad_w_qkv = grad_w_qkv + outer_sum(normed_region, grad_qkv_r)
    grad_bias_q = grad_bias_q + row_total(grad_qkv_r[..., :model_width])
    grad_bias_v = grad_bias_v + row_total(grad_qkv_r[..., 2 * model_width :])
    unused, region_pull = jax.vjp(layer_norm, region_band, ln1_gain, ln1_bias)
    grad_region_in, region_gain, region_bias = region_pull(linear_back(grad_qkv_r, w_qkv))
    grad_ln1_gain = grad_ln1_gain + region_gain
    grad_ln1_bias = grad_ln1_bias + region_bias
    raster_region = (raster_came + grad_region_in).astype(jnp.bfloat16)
    late = all_sum(
        pack(
            [grad_w_qkv, grad_w_out],
            [grad_ln1_gain, grad_ln1_bias, grad_bias_q, grad_bias_v, grad_bias_out],
            parts,
        )
    )
    (grad_w_qkv, grad_w_out), late_vectors = unpack(
        late, [w_qkv.shape, w_out.shape], [model_width] * 5, parts
    )
    grad_ln1_gain, grad_ln1_bias, grad_bias_q, grad_bias_v, grad_bias_out = late_vectors
    return (
        out_local[None],
        out_regional[None],
        grad_band[None],
        raster_region[None],
        grad_ln1_gain,
        grad_ln1_bias,
        grad_w_qkv,
        grad_bias_q,
        grad_bias_v,
        grad_w_out,
        grad_bias_out,
        grad_ln2_gain,
        grad_ln2_bias,
        grad_w_fc1,
        grad_bias_fc1,
        grad_w_fc2,
        grad_bias_fc2,
    )


def solution(mesh):
    in_specs = (
        P("img", "dp", None, None),
        P("img", "dp", None),
        P("img", "dp", None),
        P("img", None),
        P("img", None),
        P(),
        P(),
        P(),
        P(),
        P(),
        P(),
        P(),
        P(),
        P(),
        P(),
        P(),
        P(),
        P(),
        P("img", "dp", None, None),
        P("img", "dp", None),
    )
    out_specs = (
        P("img", "dp", None, None),
        P("img", "dp", None),
        P("img", "dp", None, None),
        P("img", "dp", None),
        P(),
        P(),
        P(),
        P(),
        P(),
        P(),
        P(),
        P(),
        P(),
        P(),
        P(),
        P(),
        P(),
    )
    return jax.shard_map(shards, mesh=mesh, in_specs=in_specs, out_specs=out_specs, check_vma=False)
```

```python
import math
import jax
import jax.numpy as jnp
import numpy as np
from jax import lax
from jax.experimental import pallas as pl
from jax.experimental.pallas import tpu as pltpu
from jax.sharding import PartitionSpec as P

HEADS = 16
HDIM = 32
WIN_SIDE = 7
REG_SIDE = 8
REGIONS = 64

norm_eps = 1e-05
survive = 0.9

WIDTH = 512
SLOT = 64
TALL = 56
TILE = 8
GROUP = 4
LANES = 128
VMEM_LIMIT = 60 * 1024 * 1024

f32 = jnp.float32
bf16 = jnp.bfloat16


def dot(left, right):
    return lax.dot_general(left, right, (((1,), (0,)), ((), ())), preferred_element_type=f32)


def dot_nt(left, right):
    return lax.dot_general(left, right, (((1,), (1,)), ((), ())), preferred_element_type=f32)


def head_masks():
    lane_head = np.arange(LANES) // HDIM
    plain = np.repeat(np.arange(GROUP), SLOT)
    mixed = np.repeat(np.array([0, 2, 1, 3]), SLOT)
    return (
        jnp.asarray(plain[:, None] == lane_head[None, :], bf16),
        jnp.asarray(mixed[:, None] == lane_head[None, :], bf16),
    )


def spread_heads(rows, mask):
    return jnp.concatenate([rows] * GROUP, axis=0) * mask


def turn(blocks):
    stacked = jnp.concatenate([blocks[:, :LANES], blocks[:, LANES:]], axis=0)
    turned = stacked.T
    return jnp.concatenate([turned[:SLOT], turned[SLOT:]], axis=1)


def attend_group(queries, key_rows, values, bias, plain, mixed):
    scores = dot_nt(key_rows, spread_heads(queries, plain)) + bias
    highest = jnp.max(scores, axis=0, keepdims=True)
    weighted = jnp.exp2((scores - highest) * (HDIM**-0.5 * math.log2(math.e)))
    total = jnp.sum(weighted, axis=0, keepdims=True)
    probs = (weighted * (1.0 / total)).astype(bf16)
    return probs, dot(turn(probs), spread_heads(values, mixed))


def attend_group_back(queries, key_rows, values, probs, grad_mixed, plain, mixed):
    grad_wide = spread_heads(grad_mixed, plain)
    grad_values = dot(probs, grad_wide)
    grad_probs = dot_nt(values, grad_wide)
    soft = probs.astype(f32)
    weighted = soft * grad_probs
    inner = jnp.sum(weighted, axis=0, keepdims=True)
    grad_scores = (weighted - soft * inner).astype(bf16)
    factor = HDIM**-0.5
    grad_keys = dot(grad_scores, spread_heads(queries, plain)) * factor
    grad_queries = dot(turn(grad_scores), spread_heads(key_rows, mixed)) * factor
    return grad_queries, grad_keys, grad_values


def normalize(rows):
    centered = rows - jnp.mean(rows, axis=-1, keepdims=True)
    spread = jnp.mean(centered * centered, axis=-1, keepdims=True)
    scale = lax.rsqrt(spread + norm_eps)
    return centered * scale, scale


def normalize_back(grad_unit, unit, scale):
    first = jnp.mean(grad_unit, axis=-1, keepdims=True)
    second = jnp.mean(grad_unit * unit, axis=-1, keepdims=True)
    return scale * (grad_unit - first - unit * second)


def gelu_pair(values):
    size = jnp.abs(values)
    spot = 1.0 / (1.0 + (0.3275911 * 0.7071067811865476) * size)
    bell = jnp.exp2(values * values * (-0.5 * math.log2(math.e)))
    tail = 0.5 * 1.061405429
    for factor in (-1.453152027, 1.421413741, -0.284496736, 0.254829592):
        tail = tail * spot + 0.5 * factor
    tail = tail * spot * bell
    below = jnp.where(values >= 0, 1.0 - tail, tail)
    return values * below, below + values * bell * 0.3989422804014327


def column_sum(rows):
    return jnp.sum(rows, axis=0, keepdims=True)


def attend_window(qkv, bias, plain, mixed, put_probs):
    outs = []
    wide_bias = jnp.concatenate([bias, bias], axis=1)
    for group in range(HEADS // GROUP):
        at = group * LANES
        probs, out = attend_group(
            qkv[:, at : at + LANES],
            qkv[:, WIDTH + at : WIDTH + at + LANES],
            qkv[:, 2 * WIDTH + at : 2 * WIDTH + at + LANES],
            wide_bias,
            plain,
            mixed,
        )
        put_probs(group, probs)
        outs.append(out)
    return jnp.concatenate(outs, axis=1)


def attend_window_back(qkv, probs_of, grad_mixed, plain, mixed):
    parts = []
    for group in range(HEADS // GROUP):
        at = group * LANES
        parts.append(
            attend_group_back(
                qkv[:, at : at + LANES],
                qkv[:, WIDTH + at : WIDTH + at + LANES],
                qkv[:, 2 * WIDTH + at : 2 * WIDTH + at + LANES],
                probs_of(group),
                grad_mixed[:, at : at + LANES],
                plain,
                mixed,
            )
        )
    return jnp.concatenate(
        [parts[g][which] for which in range(3) for g in range(len(parts))], axis=1
    ).astype(bf16)


def forward_kernel(
    order_ref, keep_ref,
    tokens_ref, regional_ref, window_bias_ref, region_bias_ref, spread_ref, squeeze_ref,
    plain_ref, mixed_mask_ref, gain1_ref, bias1_ref, w_qkv_ref, bias_qkv_ref, w_out_ref, bias_out_ref,
    gain2_ref, bias2_ref, w_fc1_ref, bias_fc1_ref, w_fc2_ref, bias_fc2_ref,
    out_ref, qkv_ref, probs_ref, joined_ref, mixed_ref, after_ref, hidden_ref, slope_ref,
    qkv_r_ref, probs_r_ref, mixed_r_ref,
    windows, normed, mixed_rows,
):
    step = pl.program_id(0)
    keep = keep_ref[0]
    plain = plain_ref[...]
    mixed = mixed_mask_ref[...]

    @pl.when(step == 0)
    def first():
        region = regional_ref[...].astype(f32)
        unit, _ = normalize(region)
        region_norm = (unit * gain1_ref[...] + bias1_ref[...]).astype(bf16)
        qkv_r_ref[...] = (dot(region_norm, w_qkv_ref[...]) + bias_qkv_ref[...]).astype(bf16)

        def put(group, probs):
            probs_r_ref[:, group * 2 * LANES : (group + 1) * 2 * LANES] = probs

        region_mixed = attend_window(
            qkv_r_ref[...], region_bias_ref[...], plain, mixed, put
        ).astype(bf16)
        mixed_r_ref[...] = region_mixed
        region_mid = region + keep * (dot(region_mixed, w_out_ref[...]) + bias_out_ref[...])
        region_mid = region_mid.astype(bf16)
        row = lax.broadcasted_iota(jnp.int32, (TILE * SLOT, REGIONS), 0)
        column = lax.broadcasted_iota(jnp.int32, (TILE * SLOT, REGIONS), 1)

        def relay(line, carry):
            pick = (row == (column - line * TILE) * SLOT).astype(bf16)
            rows = dot(spread_ref[...], tokens_ref[line]) + dot(pick, region_mid)
            windows[pl.ds(line * TILE, TILE)] = rows.reshape(TILE, SLOT, WIDTH)
            return carry

        lax.fori_loop(0, REG_SIDE, relay, 0)

    for at in range(TILE):
        rows = windows[order_ref[step * TILE + at]]
        joined_ref[at] = rows.astype(bf16)
        unit, _ = normalize(rows)
        normed[at * SLOT : (at + 1) * SLOT] = (unit * gain1_ref[...] + bias1_ref[...]).astype(bf16)
    for part in range(3):
        cols = slice(part * WIDTH, (part + 1) * WIDTH)
        qkv = dot(normed[...], w_qkv_ref[:, cols]) + bias_qkv_ref[:, cols]
        qkv_ref[:, :, cols] = qkv.astype(bf16).reshape(TILE, SLOT, WIDTH)

    def one(at, carry):
        def put(group, probs):
            probs_ref[at, :, group * 2 * LANES : (group + 1) * 2 * LANES] = probs

        mixed_rows[at] = attend_window(
            qkv_ref[at], window_bias_ref[order_ref[step * TILE + at]], plain, mixed, put
        )
        return carry

    lax.fori_loop(0, TILE, one, 0)
    rows_count = TILE * TALL
    mixed_low = mixed_rows[:, :TALL].reshape(rows_count, WIDTH).astype(bf16)
    mixed_ref[...] = mixed_low
    joined = joined_ref[...].astype(f32)[:, :TALL].reshape(rows_count, WIDTH)
    after = joined + keep * (dot(mixed_low, w_out_ref[...]) + bias_out_ref[...])
    after_ref[...] = after
    unit, _ = normalize(after)
    mlp_norm = (unit * gain2_ref[...] + bias2_ref[...]).astype(bf16)
    total = after + keep * bias_fc2_ref[...]
    chunk = 512
    for at in range(0, w_fc1_ref.shape[1], chunk):
        cols = slice(at, at + chunk)
        hidden, slope = gelu_pair(dot(mlp_norm, w_fc1_ref[:, cols]) + bias_fc1_ref[:, cols])
        hidden = hidden.astype(bf16)
        hidden_ref[:, cols] = hidden
        slope_ref[:, cols] = slope.astype(bf16)
        total = total + keep * dot(hidden, w_fc2_ref[cols, :])
    out_ref[0] = dot(squeeze_ref[...], total.astype(bf16)).astype(bf16)


def whole(shape):
    return pl.BlockSpec(shape, lambda step, *_: (0,) * len(shape))


def tiles(shape):
    return pl.BlockSpec(shape, lambda step, *_: (step,) + (0,) * (len(shape) - 1))


def run_forward(order, keep, tokens, regional, window_bias, region_bias, spread, squeeze, plain, mixed,
                gain1, bias1, w_qkv, bias_qkv, w_out, bias_out, gain2, bias2, w_fc1, bias_fc1, w_fc2, bias_fc2):
    windows = regional.shape[0]
    steps = windows // TILE
    rows = TILE * TALL
    hidden = w_fc1.shape[1]
    compact = squeeze.shape[0]
    args = (tokens, regional, window_bias, region_bias, spread, squeeze, plain, mixed,
            gain1, bias1, w_qkv, bias_qkv, w_out, bias_out, gain2, bias2, w_fc1, bias_fc1, w_fc2, bias_fc2)
    outs = [
        ((steps, compact, WIDTH), bf16, (1, compact, WIDTH)),
        ((windows, SLOT, 3 * WIDTH), bf16, (TILE, SLOT, 3 * WIDTH)),
        ((windows, SLOT, HEADS * SLOT), bf16, (TILE, SLOT, HEADS * SLOT)),
        ((windows, SLOT, WIDTH), bf16, (TILE, SLOT, WIDTH)),
        ((steps * rows, WIDTH), bf16, (rows, WIDTH)),
        ((steps * rows, WIDTH), f32, (rows, WIDTH)),
        ((steps * rows, hidden), bf16, (rows, hidden)),
        ((steps * rows, hidden), bf16, (rows, hidden)),
    ]
    fixed = [((REGIONS, 3 * WIDTH), bf16), ((REGIONS, HEADS * SLOT), bf16), ((REGIONS, WIDTH), bf16)]
    return pl.pallas_call(
        forward_kernel,
        grid_spec=pltpu.PrefetchScalarGridSpec(
            num_scalar_prefetch=2,
            grid=(steps,),
            in_specs=[whole(a.shape) for a in args],
            out_specs=[tiles(block) for _, _, block in outs] + [whole(s) for s, _ in fixed],
            scratch_shapes=[
                pltpu.VMEM((windows, SLOT, WIDTH), f32),
                pltpu.VMEM((TILE * SLOT, WIDTH), bf16),
                pltpu.VMEM((TILE, SLOT, WIDTH), f32),
            ],
        ),
        out_shape=[jax.ShapeDtypeStruct(s, d) for s, d, _ in outs]
        + [jax.ShapeDtypeStruct(s, d) for s, d in fixed],
        compiler_params=pltpu.CompilerParams(
            dimension_semantics=("arbitrary",), vmem_limit_bytes=VMEM_LIMIT
        ),
        cost_estimate=pl.CostEstimate(flops=30_000_000_000, bytes_accessed=60_000_000, transcendentals=20_000_000),
        name="forward",
    )(order, keep, *args)


def back_mlp_kernel(
    keep_ref, cot_ref, after_ref, mixed_ref, hidden_ref, slope_ref, stretch_ref,
    gain2_ref, bias2_ref, w_fc1_ref, w_fc2_ref, w_out_ref,
    grad_after_ref, grad_mixed_ref, early_ref, grad_out_ref, small_ref, bias_row_ref,
    sum_fc1, sum_fc2, sum_out, sums, sum_hidden,
):
    step = pl.program_id(0)
    last = pl.num_programs(0) - 1
    keep = keep_ref[0]

    @pl.when(step == 0)
    def clear():
        for ref in (sum_fc1, sum_fc2, sum_out, sums, sum_hidden):
            ref[...] = jnp.zeros_like(ref)

    unit, scale = normalize(after_ref[...])
    mlp_norm = (unit * gain2_ref[...] + bias2_ref[...]).astype(bf16)
    norm_turned = mlp_norm.T
    cot = dot(stretch_ref[...], cot_ref[0])
    grad_mlp = (keep * cot).astype(bf16)
    grad_turned = grad_mlp.T
    sums[0:1] += column_sum(grad_mlp.astype(f32))
    grad_norm = jnp.zeros(after_ref.shape, f32)
    chunk = 512
    for at in range(0, w_fc1_ref.shape[1], chunk):
        cols = slice(at, at + chunk)
        grad_hidden = dot_nt(grad_mlp, w_fc2_ref[cols, :])
        grad_pre = (slope_ref[:, cols].astype(f32) * grad_hidden).astype(bf16)
        sum_fc2[:, cols] += dot(grad_turned, hidden_ref[:, cols])
        sum_fc1[:, cols] += dot(norm_turned, grad_pre)
        sum_hidden[0:1, cols] += column_sum(grad_pre.astype(f32))
        grad_norm = grad_norm + dot_nt(grad_pre, w_fc1_ref[:, cols])
    sums[1:2] += column_sum(grad_norm * unit)
    sums[2:3] += column_sum(grad_norm)
    grad_after = cot + normalize_back(grad_norm * gain2_ref[...], unit, scale)
    grad_after_ref[...] = grad_after
    grad_branch = (keep * grad_after).astype(bf16)
    sums[3:4] += column_sum(grad_branch.astype(f32))
    sum_out[...] += dot(mixed_ref[...].T, grad_branch)
    grad_mixed = dot_nt(grad_branch, w_out_ref[...]).reshape(TILE, TALL, WIDTH)
    empty = jnp.zeros((TILE, SLOT - TALL, WIDTH), f32)
    grad_mixed_ref[...] = jnp.concatenate([grad_mixed, empty], axis=1).astype(bf16)

    @pl.when(step == last)
    def finish():
        for at in range(4):
            cols = slice(at * WIDTH, (at + 1) * WIDTH)
            early_ref[cols, :] = sum_fc1[:, cols].astype(bf16)
            early_ref[4 * WIDTH + at * WIDTH : 4 * WIDTH + (at + 1) * WIDTH, :] = (
                sum_fc2[:, cols].T.astype(bf16)
            )
        grad_out_ref[...] = sum_out[...]
        small_ref[...] = sums[...]
        bias_row_ref[...] = sum_hidden[...]


def run_back_mlp(keep, cot, after, mixed, hidden, slope, stretch, gain2, bias2, w_fc1, w_fc2, w_out):
    steps, compact, _ = cot.shape
    rows = TILE * TALL
    units = w_fc1.shape[1]
    tiled = [(1, compact, WIDTH), (rows, WIDTH), (rows, WIDTH), (rows, units), (rows, units)]
    fixed = (stretch, gain2, bias2, w_fc1, w_fc2, w_out)
    outs = [
        ((steps * rows, WIDTH), f32, (rows, WIDTH)),
        ((steps * TILE, SLOT, WIDTH), bf16, (TILE, SLOT, WIDTH)),
    ]
    whole_outs = [((2 * units, WIDTH), bf16), ((WIDTH, WIDTH), f32), ((8, WIDTH), f32), ((8, units), f32)]
    return pl.pallas_call(
        back_mlp_kernel,
        grid_spec=pltpu.PrefetchScalarGridSpec(
            num_scalar_prefetch=1,
            grid=(steps,),
            in_specs=[tiles(b) for b in tiled] + [whole(a.shape) for a in fixed],
            out_specs=[tiles(block) for _, _, block in outs] + [whole(s) for s, _ in whole_outs],
            scratch_shapes=[
                pltpu.VMEM((WIDTH, units), f32),
                pltpu.VMEM((WIDTH, units), f32),
                pltpu.VMEM((WIDTH, WIDTH), f32),
                pltpu.VMEM((8, WIDTH), f32),
                pltpu.VMEM((8, units), f32),
            ],
        ),
        out_shape=[jax.ShapeDtypeStruct(s, d) for s, d, _ in outs]
        + [jax.ShapeDtypeStruct(s, d) for s, d in whole_outs],
        compiler_params=pltpu.CompilerParams(
            dimension_semantics=("arbitrary",), vmem_limit_bytes=VMEM_LIMIT
        ),
        cost_estimate=pl.CostEstimate(flops=40_000_000_000, bytes_accessed=60_000_000, transcendentals=0),
        name="back_mlp",
    )(keep, cot, after, mixed, hidden, slope, *fixed)


def back_attention_kernel(
    order_ref, keep_ref,
    qkv_ref, probs_ref, joined_ref, grad_mixed_ref, grad_after_ref, grad_out_ref,
    gather_ref, plain_ref, mixed_mask_ref, regional_ref, qkv_r_ref, probs_r_ref, mixed_r_ref,
    gain1_ref, bias1_ref, w_qkv_ref, w_out_ref,
    tokens_out_ref, regional_out_ref, late_ref, small_ref,
    windows, grads, sum_qkv, sums, region_grad,
):
    step = pl.program_id(0)
    last = pl.num_programs(0) - 1
    keep = keep_ref[0]
    plain = plain_ref[...]
    mixed = mixed_mask_ref[...]
    gain1 = gain1_ref[...]

    @pl.when(step == 0)
    def clear():
        sum_qkv[...] = jnp.zeros_like(sum_qkv)
        sums[...] = jnp.zeros_like(sums)

    def one(at, carry):
        def probs_of(group):
            return probs_ref[at, :, group * 2 * LANES : (group + 1) * 2 * LANES]

        grads[pl.ds(pl.multiple_of(at * SLOT, SLOT), SLOT)] = attend_window_back(
            qkv_ref[at], probs_of, grad_mixed_ref[at], plain, mixed
        )
        return carry

    lax.fori_loop(0, TILE, one, 0)
    joined = joined_ref[...].astype(f32).reshape(TILE * SLOT, WIDTH)
    unit, scale = normalize(joined)
    normed = (unit * gain1 + bias1_ref[...]).astype(bf16)
    grad_qkv = grads[...]
    sum_qkv[...] += dot(normed.T, grad_qkv)
    sums[2:3] += column_sum(grad_qkv[:, :WIDTH].astype(f32))
    sums[3:4] += column_sum(grad_qkv[:, 2 * WIDTH :].astype(f32))
    grad_normed = dot_nt(grad_qkv, w_qkv_ref[...])
    sums[0:1] += column_sum(grad_normed * unit)
    sums[1:2] += column_sum(grad_normed)
    grad_in = normalize_back(grad_normed * gain1, unit, scale)
    for at in range(TILE):
        rows = grad_in[at * SLOT : at * SLOT + TALL] + grad_after_ref[at * TALL : (at + 1) * TALL]
        windows[order_ref[step * TILE + at], :TALL] = rows

    @pl.when(step == last)
    def finish():
        def relay(line, carry):
            block = windows[pl.ds(line * TILE, TILE)][:, :TALL].reshape(TILE * TALL, WIDTH)
            rows = dot(gather_ref[...], block.astype(bf16))
            tokens_out_ref[line] = rows[: rows.shape[0] - TILE].astype(bf16)
            region_grad[pl.ds(pl.multiple_of(line * TILE, TILE), TILE)] = rows[rows.shape[0] - TILE :]
            return carry

        lax.fori_loop(0, REG_SIDE, relay, 0)
        came = region_grad[...]
        grad_branch = (keep * came).astype(bf16)
        grad_mixed = dot_nt(grad_branch, w_out_ref[...]).astype(bf16)

        def probs_of(group):
            return probs_r_ref[:, group * 2 * LANES : (group + 1) * 2 * LANES]

        grad_qkv_r = attend_window_back(qkv_r_ref[...], probs_of, grad_mixed, plain, mixed)
        region = regional_ref[...].astype(f32)
        unit_r, scale_r = normalize(region)
        normed_r = (unit_r * gain1 + bias1_ref[...]).astype(bf16)
        total = sum_qkv[...] + dot(normed_r.T, grad_qkv_r)
        for part in range(3):
            cols = slice(part * WIDTH, (part + 1) * WIDTH)
            late_ref[cols, :] = total[:, cols].astype(bf16)
        late_ref[3 * WIDTH :, :] = (
            grad_out_ref[...] + dot(mixed_r_ref[...].T, grad_branch)
        ).astype(bf16)
        grad_normed_r = dot_nt(grad_qkv_r, w_qkv_ref[...])
        sums[0:1] += column_sum(grad_normed_r * unit_r)
        sums[1:2] += column_sum(grad_normed_r)
        sums[2:3] += column_sum(grad_qkv_r[:, :WIDTH].astype(f32))
        sums[3:4] += column_sum(grad_qkv_r[:, 2 * WIDTH :].astype(f32))
        sums[4:5] += column_sum(grad_branch.astype(f32))
        regional_out_ref[...] = (
            came + normalize_back(grad_normed_r * gain1, unit_r, scale_r)
        ).astype(bf16)
        small_ref[...] = sums[...]


def run_back_attention(order, keep, qkv, probs, joined, grad_mixed, grad_after, grad_out, gather, plain, mixed,
                       regional, qkv_r, probs_r, mixed_r, gain1, bias1, w_qkv, w_out):
    windows = regional.shape[0]
    steps = windows // TILE
    rows = TILE * TALL
    lines = gather.shape[0] - TILE
    tiled = [(TILE, SLOT, 3 * WIDTH), (TILE, SLOT, HEADS * SLOT), (TILE, SLOT, WIDTH), (TILE, SLOT, WIDTH), (rows, WIDTH)]
    fixed = (grad_out, gather, plain, mixed, regional, qkv_r, probs_r, mixed_r, gain1, bias1, w_qkv, w_out)
    whole_outs = [((REG_SIDE, lines, WIDTH), bf16), ((windows, WIDTH), bf16), ((4 * WIDTH, WIDTH), bf16), ((8, WIDTH), f32)]
    return pl.pallas_call(
        back_attention_kernel,
        grid_spec=pltpu.PrefetchScalarGridSpec(
            num_scalar_prefetch=2,
            grid=(steps,),
            in_specs=[tiles(b) for b in tiled] + [whole(a.shape) for a in fixed],
            out_specs=[whole(s) for s, _ in whole_outs],
            scratch_shapes=[
                pltpu.VMEM((windows, SLOT, WIDTH), f32),
                pltpu.VMEM((TILE * SLOT, 3 * WIDTH), bf16),
                pltpu.VMEM((WIDTH, 3 * WIDTH), f32),
                pltpu.VMEM((8, WIDTH), f32),
                pltpu.VMEM((windows, WIDTH), f32),
            ],
        ),
        out_shape=[jax.ShapeDtypeStruct(s, d) for s, d in whole_outs],
        compiler_params=pltpu.CompilerParams(
            dimension_semantics=("arbitrary",), vmem_limit_bytes=VMEM_LIMIT
        ),
        cost_estimate=pl.CostEstimate(flops=30_000_000_000, bytes_accessed=60_000_000, transcendentals=0),
        name="back_attention",
    )(order, keep, qkv, probs, joined, grad_mixed, grad_after, *fixed)


def band_to_windows(band_values, win_count):
    trailing = band_values.shape[2:]
    blocks = band_values.reshape(
        (band_values.shape[0] // WIN_SIDE, WIN_SIDE, REG_SIDE, WIN_SIDE) + trailing
    )
    return jnp.swapaxes(blocks, 1, 2).reshape((win_count, WIN_SIDE * WIN_SIDE) + trailing)


def rank_of(keys):
    return jnp.sum(keys[None, :] < keys[:, None], axis=1)


def reduce_stages():
    img_bits = [("img", bit) for bit in range(lax.axis_size("img").bit_length() - 1)]
    dp_bits = [("dp", bit) for bit in range(lax.axis_size("dp").bit_length() - 1)]
    rest = img_bits[1:] + dp_bits
    return [img_bits[:1]] + [rest[at : at + 2] for at in range(0, len(rest), 2)]


def stage_peers(stage):
    dp_size, img_size = lax.axis_size("dp"), lax.axis_size("img")
    flat = lax.axis_index("dp") * img_size + lax.axis_index("img")
    masks = [(1 << bit) * (img_size if name == "dp" else 1) for name, bit in stage]
    own = sum(((flat // mask) % 2) << place for place, mask in enumerate(masks))
    moves = []
    for offset in range(1, 1 << len(masks)):
        flip = sum(mask for place, mask in enumerate(masks) if offset >> place & 1)
        moves.append((offset, [(at, at ^ flip) for at in range(dp_size * img_size)]))
    return own, moves


def reduce_shards(rows):
    for stage in reduce_stages():
        own, moves = stage_peers(stage)
        parts = rows.reshape((1 << len(stage), -1) + rows.shape[1:])
        got = [
            lax.ppermute(
                lax.dynamic_index_in_dim(parts, own ^ offset, 0, False), ("dp", "img"), pairs
            )
            for offset, pairs in moves
        ]
        total = lax.dynamic_index_in_dim(parts, own, 0, False).astype(jnp.float32)
        for piece in got:
            total = total + piece.astype(jnp.float32)
        rows = total.astype(jnp.bfloat16)
    return rows


def gather_shards(rows):
    for stage in reversed(reduce_stages()):
        own, moves = stage_peers(stage)
        got = [lax.ppermute(rows, ("dp", "img"), pairs) for offset, pairs in moves]
        pieces = [rows] + got
        ordered = []
        for place in range(len(pieces)):
            piece = pieces[0]
            for offset in range(1, len(pieces)):
                piece = jnp.where((own ^ place) == offset, pieces[offset], piece)
            ordered.append(piece)
        rows = jnp.concatenate(ordered, axis=0)
    return rows


def all_sum(rows):
    return gather_shards(reduce_shards(rows.astype(jnp.bfloat16)))


def deal_kernel(pick_ref, region_ref, local_ref, out_ref):
    groups = out_ref.shape[0]
    for pair in range(out_ref.shape[1] // 16):
        head = region_ref[...] if pair == 0 else local_ref[2 * pair - 1]
        rows = jnp.concatenate([head, local_ref[2 * pair]], axis=0)
        out_ref[:, 16 * pair : 16 * pair + 16, :] = (
            dot(pick_ref[...], rows).astype(bf16).reshape(groups, 16, WIDTH)
        )


def collect_kernel(pick_ref, came_ref, region_ref, local_ref):
    slots = region_ref.shape[0]
    for pair in range(came_ref.shape[1] // 16):
        rows = came_ref[:, 16 * pair : 16 * pair + 16, :].reshape(2 * slots, WIDTH)
        rows = dot(pick_ref[...], rows).astype(bf16)
        if pair == 0:
            region_ref[...] = rows[:slots]
        else:
            local_ref[2 * pair - 1] = rows[:slots]
        local_ref[2 * pair] = rows[slots:]


def run_deal(pick, region, local):
    count = region.shape[0] // TILE
    return pl.pallas_call(
        deal_kernel,
        out_shape=jax.ShapeDtypeStruct((count, (local.shape[0] + 1) * TILE, WIDTH), bf16),
        compiler_params=pltpu.CompilerParams(vmem_limit_bytes=VMEM_LIMIT),
        cost_estimate=pl.CostEstimate(flops=1_000_000_000, bytes_accessed=7_000_000, transcendentals=0),
        name="deal",
    )(pick, region, local)


def run_collect(pick, came):
    slots = came.shape[0] * TILE
    return pl.pallas_call(
        collect_kernel,
        out_shape=[
            jax.ShapeDtypeStruct((slots, WIDTH), bf16),
            jax.ShapeDtypeStruct((came.shape[1] // TILE - 1, slots, WIDTH), bf16),
        ],
        compiler_params=pltpu.CompilerParams(vmem_limit_bytes=VMEM_LIMIT),
        cost_estimate=pl.CostEstimate(flops=1_000_000_000, bytes_accessed=7_000_000, transcendentals=0),
        name="collect",
    )(pick, came)


def swap_tiles(tiles_sent, devices):
    count, rows, width = tiles_sent.shape
    share = count * TILE // devices
    if share == TILE:
        return lax.all_to_all(tiles_sent, "dp", split_axis=0, concat_axis=0, tiled=True)
    places = rows // TILE
    sent = tiles_sent.reshape(count, places, TILE, width).transpose(1, 0, 2, 3)
    sent = sent.reshape(places, devices, share, width).transpose(1, 0, 2, 3)
    came = lax.all_to_all(sent, "dp", split_axis=0, concat_axis=0, tiled=True)
    came = came.transpose(1, 0, 2, 3).reshape(places, count, TILE, width)
    return came.transpose(1, 0, 2, 3).reshape(count, rows, width)


def row_maps():
    window = np.arange(TILE)[:, None]
    place = np.arange(WIN_SIDE * WIN_SIDE)[None, :]
    raster = place // WIN_SIDE * (TILE * WIN_SIDE) + window * WIN_SIDE + place % WIN_SIDE
    band = TILE * WIN_SIDE * WIN_SIDE
    spread = np.zeros((TILE * SLOT, band), np.float32)
    spread[window * SLOT + 1 + place, raster] = 1
    gather = np.zeros((band + TILE, TILE * TALL), np.float32)
    gather[raster, window * TALL + 1 + place] = 1
    gather[band + window, window * TALL] = 1
    place = np.arange(WIN_SIDE * WIN_SIDE + 1)[None, :]
    squeeze = np.zeros(((WIN_SIDE * WIN_SIDE + 1) * TILE, TILE * TALL), np.float32)
    squeeze[place * TILE + window, window * TALL + place] = 1
    return [jnp.asarray(table, bf16) for table in (spread, gather, squeeze, squeeze.T)]


def shards(
    tokens,
    regional,
    pad_mask,
    keep_mask,
    window_slot,
    ln1_gain,
    ln1_bias,
    w_qkv,
    bias_q,
    bias_v,
    w_out,
    bias_out,
    ln2_gain,
    ln2_bias,
    w_fc1,
    bias_fc1,
    w_fc2,
    bias_fc2,
    cot_local,
    cot_regional,
):
    devices = lax.axis_size("dp")
    parts = devices * lax.axis_size("img")
    own_rank = lax.axis_index("dp")
    win_count = regional.shape[1]
    all_windows = window_slot.shape[1]
    slot_of = window_slot[0]
    places = jnp.arange(win_count)
    own_target = lax.dynamic_slice_in_dim(slot_of, own_rank * win_count, win_count) // win_count
    own_place = rank_of(own_target * win_count + places)
    order = jnp.sum(jnp.where(own_place[None, :] == places[:, None], places[None, :], 0), axis=1)
    slot_hit = slot_of[None, :] == (own_rank * win_count + places)[:, None]
    window_here = jnp.sum(jnp.where(slot_hit, jnp.arange(all_windows)[None, :], 0), axis=1)
    here_place = rank_of(window_here)
    deal_row = jnp.arange(2 * win_count)
    row_place = deal_row // (2 * TILE) * TILE + deal_row % TILE
    row_half = deal_row // TILE % 2
    column_hit = row_place[:, None] == jnp.concatenate([here_place, here_place])[None, :]
    pick = (column_hit & (row_half[:, None] == (deal_row // win_count)[None, :])).astype(bf16)
    pick_back = (column_hit & (row_half[:, None] == (deal_row // win_count)[None, :])).T.astype(bf16)
    cot = swap_tiles(
        run_deal(pick, cot_regional[0], jnp.swapaxes(cot_local[0], 0, 1)), devices
    )
    image = own_rank * win_count // REGIONS
    keep = lax.dynamic_slice_in_dim(keep_mask[0], image, 1).astype(f32) / survive
    live = band_to_windows(pad_mask[0], win_count) != 0
    allowed = jnp.concatenate(
        [jnp.ones((win_count, 1), bool), live, jnp.zeros((win_count, SLOT - 1 - live.shape[1]), bool)],
        axis=1,
    )
    window_bias = jnp.broadcast_to(
        jnp.where(allowed, 0.0, -1e30).astype(f32)[:, :, None], (win_count, SLOT, LANES)
    )
    region_bias = jnp.broadcast_to(
        jnp.where(live[:, 0], 0.0, -1e30).astype(f32)[:, None], (win_count, LANES)
    )
    spread, gather, squeeze, stretch = row_maps()
    plain, mixed_mask = head_masks()
    bias_qkv = jnp.concatenate([bias_q, jnp.zeros_like(bias_q), bias_v])[None]
    gain1, bias1, gain2, bias2 = ln1_gain[None], ln1_bias[None], ln2_gain[None], ln2_bias[None]
    out, qkv, probs, joined, mixed, after, hidden, slope, qkv_r, probs_r, mixed_r = run_forward(
        order, keep, tokens.reshape(REG_SIDE, -1, WIDTH), regional[0], window_bias, region_bias,
        spread, squeeze, plain, mixed_mask, gain1, bias1, w_qkv, bias_qkv, w_out, bias_out[None],
        gain2, bias2, w_fc1, bias_fc1[None], w_fc2, bias_fc2[None],
    )
    came = swap_tiles(out, devices)
    grad_after, grad_mixed, early, grad_out, small, row_fc1 = run_back_mlp(
        keep, cot, after, mixed, hidden, slope, stretch, gain2, bias2, w_fc1, w_fc2, w_out
    )
    early = all_sum(early)
    tokens_out, regional_out, late, small_late = run_back_attention(
        order, keep, qkv, probs, joined, grad_mixed, grad_after, grad_out, gather, plain, mixed_mask,
        regional[0], qkv_r, probs_r, mixed_r, gain1, bias1, w_qkv, w_out,
    )
    out_regional, out_local = run_collect(pick_back, came)
    vectors = jnp.concatenate(
        [
            small_late[0:4],
            (small[3] + small_late[4])[None],
            small[1:3],
            small[0:1],
            row_fc1[0].reshape(-1, WIDTH),
        ],
        axis=0,
    )
    late_share = late.shape[0] // parts
    extra = jnp.zeros((2 * 8, WIDTH), bf16).at[: vectors.shape[0]].set(vectors.astype(bf16))
    extra = jnp.concatenate([extra.reshape(2, 8, WIDTH), jnp.zeros((parts - 2, 8, WIDTH), bf16)])
    late = jnp.concatenate([late.reshape(parts, late_share, WIDTH), extra], axis=1)
    late = all_sum(late.reshape(-1, WIDTH)).reshape(parts, late_share + 8, WIDTH)
    vectors = late[:2, late_share:].reshape(-1, WIDTH).astype(f32)
    late = late[:, :late_share].reshape(-1, WIDTH)
    grad_w_qkv = jnp.concatenate([late[at * WIDTH : (at + 1) * WIDTH] for at in range(3)], axis=1)
    units = w_fc1.shape[1]
    grad_w_fc1 = jnp.concatenate(
        [early[at : at + WIDTH] for at in range(0, units, WIDTH)], axis=1
    )
    return (
        jnp.swapaxes(out_local, 0, 1)[None],
        out_regional[None],
        tokens_out.reshape(tokens.shape),
        regional_out[None],
        vectors[0],
        vectors[1],
        grad_w_qkv.astype(f32),
        vectors[2],
        vectors[3],
        late[3 * WIDTH :].astype(f32),
        vectors[4],
        vectors[5],
        vectors[6],
        grad_w_fc1.astype(f32),
        vectors[8:12].reshape(-1),
        early[units:].astype(f32),
        vectors[7],
    )


def solution(mesh):
    in_specs = (
        P("img", "dp", None, None),
        P("img", "dp", None),
        P("img", "dp", None),
        P("img", None),
        P("img", None),
        P(),
        P(),
        P(),
        P(),
        P(),
        P(),
        P(),
        P(),
        P(),
        P(),
        P(),
        P(),
        P(),
        P("img", "dp", None, None),
        P("img", "dp", None),
    )
    out_specs = (
        P("img", "dp", None, None),
        P("img", "dp", None),
        P("img", "dp", None, None),
        P("img", "dp", None),
        P(),
        P(),
        P(),
        P(),
        P(),
        P(),
        P(),
        P(),
        P(),
        P(),
        P(),
        P(),
        P(),
    )
    return jax.shard_map(shards, mesh=mesh, in_specs=in_specs, out_specs=out_specs, check_vma=False)
```

```python
import functools
import math
import jax
import jax.numpy as jnp
import numpy as np
from jax import lax
from jax.experimental import pallas as pl
from jax.experimental.pallas import tpu as pltpu
from jax.sharding import PartitionSpec as P

HEADS = 16
HDIM = 32
WIN_SIDE = 7
REG_SIDE = 8
REGIONS = 64

norm_eps = 1e-05
survive = 0.9

WIDTH = 512
SLOT = 64
TALL = 56
TILE = 8
GROUP = 4
GROUPS = HEADS // GROUP
TOGETHER = 8
LANES = 128
FIRST_TILES = 2
CHUNK = 512
VMEM_LIMIT = 60 * 1024 * 1024

f32 = jnp.float32
bf16 = jnp.bfloat16


def dot(left, right):
    return lax.dot_general(left, right, (((1,), (0,)), ((), ())), preferred_element_type=f32)


def dot_nt(left, right):
    return lax.dot_general(left, right, (((1,), (1,)), ((), ())), preferred_element_type=f32)


def head_masks():
    lane_head = np.arange(LANES) // HDIM
    plain = np.repeat(np.arange(GROUP), SLOT)
    mixed = np.repeat(np.array([0, 2, 1, 3]), SLOT)
    return (
        jnp.asarray(plain[:, None] == lane_head[None, :], bf16),
        jnp.asarray(mixed[:, None] == lane_head[None, :], bf16),
    )


def spread_heads(rows, mask):
    return jnp.concatenate([rows] * GROUP, axis=0) * mask


def turn(blocks):
    stacked = jnp.concatenate([blocks[:, :LANES], blocks[:, LANES:]], axis=0)
    turned = stacked.T
    return jnp.concatenate([turned[:SLOT], turned[SLOT:]], axis=1)


def attend(items, plain, mixed):
    scores = [dot_nt(key_rows, spread_heads(queries, plain)) for queries, key_rows, _, _ in items]
    probs = []
    for rows, (_, _, _, bias) in zip(scores, items):
        rows = rows + bias
        highest = jnp.max(rows, axis=0, keepdims=True)
        weighted = jnp.exp2((rows - highest) * (HDIM**-0.5 * math.log2(math.e)))
        total = jnp.sum(weighted, axis=0, keepdims=True)
        probs.append((weighted * (1.0 / total)).astype(bf16))
    turned = [turn(rows) for rows in probs]
    outs = [dot(rows, spread_heads(item[2], mixed)) for rows, item in zip(turned, items)]
    return probs, outs


def attend_back(items, plain, mixed):
    wide = [spread_heads(item[4], plain) for item in items]
    grad_probs = [dot_nt(item[2], rows) for item, rows in zip(items, wide)]
    grad_values = [dot(item[3], rows) for item, rows in zip(items, wide)]
    scores = []
    for rows, item in zip(grad_probs, items):
        soft = item[3].astype(f32)
        weighted = soft * rows
        inner = jnp.sum(weighted, axis=0, keepdims=True)
        scores.append((weighted - soft * inner).astype(bf16))
    turned = [turn(rows) for rows in scores]
    factor = HDIM**-0.5
    grad_keys = [dot(rows, spread_heads(item[0], plain)) * factor for rows, item in zip(scores, items)]
    grad_queries = [dot(rows, spread_heads(item[1], mixed)) * factor for rows, item in zip(turned, items)]
    return list(zip(grad_queries, grad_keys, grad_values))


def normalize(rows):
    centered = rows - jnp.mean(rows, axis=-1, keepdims=True)
    spread = jnp.mean(centered * centered, axis=-1, keepdims=True)
    scale = lax.rsqrt(spread + norm_eps)
    return centered * scale, scale


def normalize_back(grad_unit, unit, scale):
    first = jnp.mean(grad_unit, axis=-1, keepdims=True)
    second = jnp.mean(grad_unit * unit, axis=-1, keepdims=True)
    return scale * (grad_unit - first - unit * second)


def gelu_pair(values):
    size = jnp.abs(values)
    spot = 1.0 / (1.0 + (0.3275911 * 0.7071067811865476) * size)
    bell = jnp.exp2(values * values * (-0.5 * math.log2(math.e)))
    tail = 0.5 * 1.061405429
    for factor in (-1.453152027, 1.421413741, -0.284496736, 0.254829592):
        tail = tail * spot + 0.5 * factor
    tail = tail * spot * bell
    below = jnp.where(values >= 0, 1.0 - tail, tail)
    return values * below, below + values * bell * 0.3989422804014327


def column_sum(rows):
    return jnp.sum(rows, axis=0, keepdims=True)


def attend_windows(windows, plain, mixed):
    items = []
    for qkv_of, bias, _, _ in windows:
        wide = jnp.concatenate([bias, bias], axis=1)
        for group in range(GROUPS):
            items.append((qkv_of(group), qkv_of(GROUPS + group), qkv_of(2 * GROUPS + group), wide))
    probs, outs = attend(items, plain, mixed)
    for at, (_, _, put_probs, put_mixed) in enumerate(windows):
        for group in range(GROUPS):
            rows = probs[at * GROUPS + group]
            put_probs(2 * group, rows[:, :LANES])
            put_probs(2 * group + 1, rows[:, LANES:])
            put_mixed(group, outs[at * GROUPS + group])


def attend_windows_back(windows, plain, mixed):
    items = []
    for qkv_of, probs_of, grad_of, _ in windows:
        for group in range(GROUPS):
            probs = jnp.concatenate([probs_of(2 * group), probs_of(2 * group + 1)], axis=1)
            items.append(
                (qkv_of(group), qkv_of(GROUPS + group), qkv_of(2 * GROUPS + group), probs, grad_of(group))
            )
    grads = attend_back(items, plain, mixed)
    for at, (_, _, _, put_grad) in enumerate(windows):
        for group in range(GROUPS):
            for part in range(3):
                put_grad(part * GROUPS + group, grads[at * GROUPS + group][part].astype(bf16))


def forward_kernel(
    order_ref, keep_ref,
    tokens_ref, regional_ref, window_bias_ref, region_bias_ref, spread_ref, squeeze_ref,
    plain_ref, mixed_mask_ref, gain1_ref, bias1_ref, w_qkv_ref, bias_qkv_ref, w_out_ref, bias_out_ref,
    gain2_ref, bias2_ref, w_fc1_ref, bias_fc1_ref, w_fc2_ref, bias_fc2_ref,
    out_ref, qkv_ref, probs_ref, joined_ref, mixed_ref, after_ref, hidden_ref, slope_ref,
    qkv_r_ref, probs_r_ref, mixed_r_ref,
    windows, normed, mixed_rows,
):
    step = pl.program_id(0)
    keep = keep_ref[0]
    plain = plain_ref[...]
    mixed = mixed_mask_ref[...]

    @pl.when(step == 0)
    def first():
        region = regional_ref[...].astype(f32)
        unit, _ = normalize(region)
        region_norm = (unit * gain1_ref[...] + bias1_ref[...]).astype(bf16)
        region_qkv = (dot(region_norm, w_qkv_ref[...]) + bias_qkv_ref[...]).astype(bf16)
        for at in range(3 * GROUPS):
            qkv_r_ref[at] = region_qkv[:, at * LANES : (at + 1) * LANES]

        def put_probs(at, probs):
            probs_r_ref[at] = probs

        def put_mixed(at, rows):
            mixed_r_ref[:, at * LANES : (at + 1) * LANES] = rows.astype(bf16)

        attend_windows(
            [(lambda at: qkv_r_ref[at], region_bias_ref[...], put_probs, put_mixed)], plain, mixed
        )
        region_mixed = mixed_r_ref[...]
        region_mid = region + keep * (dot(region_mixed, w_out_ref[...]) + bias_out_ref[...])
        region_mid = region_mid.astype(bf16)
        row = lax.broadcasted_iota(jnp.int32, (TILE * SLOT, REGIONS), 0)
        column = lax.broadcasted_iota(jnp.int32, (TILE * SLOT, REGIONS), 1)

        def relay(line, carry):
            pick = (row == (column - line * TILE) * SLOT).astype(bf16)
            rows = dot(spread_ref[...], tokens_ref[line]) + dot(pick, region_mid)
            windows[pl.ds(line * TILE, TILE)] = rows.reshape(TILE, SLOT, WIDTH)
            return carry

        lax.fori_loop(0, REG_SIDE, relay, 0)

    for at in range(TILE):
        rows = windows[order_ref[step * TILE + at]]
        joined_ref[at] = rows.astype(bf16)
        unit, _ = normalize(rows)
        normed[at * SLOT : (at + 1) * SLOT] = (unit * gain1_ref[...] + bias1_ref[...]).astype(bf16)
    for part in range(3):
        cols = slice(part * WIDTH, (part + 1) * WIDTH)
        qkv = dot(normed[...], w_qkv_ref[:, cols]) + bias_qkv_ref[:, cols]
        qkv = qkv.astype(bf16).reshape(TILE, SLOT, WIDTH)
        for group in range(GROUPS):
            qkv_ref[:, part * GROUPS + group] = qkv[:, :, group * LANES : (group + 1) * LANES]

    def some(batch, carry):
        def window(at):
            def put_probs(place, probs):
                probs_ref[at, place] = probs

            def put_mixed(group, rows):
                mixed_rows[at, :, group * LANES : (group + 1) * LANES] = rows

            bias = window_bias_ref[order_ref[step * TILE + at]]
            return lambda place: qkv_ref[at, place], bias, put_probs, put_mixed

        attend_windows([window(batch * TOGETHER + at) for at in range(TOGETHER)], plain, mixed)
        return carry

    lax.fori_loop(0, TILE // TOGETHER, some, 0)
    rows_count = TILE * TALL
    mixed_low = mixed_rows[:, :TALL].reshape(rows_count, WIDTH).astype(bf16)
    mixed_ref[...] = mixed_low
    joined = joined_ref[...].astype(f32)[:, :TALL].reshape(rows_count, WIDTH)
    after = joined + keep * (dot(mixed_low, w_out_ref[...]) + bias_out_ref[...])
    after_ref[...] = after
    unit, _ = normalize(after)
    mlp_norm = (unit * gain2_ref[...] + bias2_ref[...]).astype(bf16)
    total = after + keep * bias_fc2_ref[...]
    chunks = [slice(at, at + CHUNK) for at in range(0, w_fc1_ref.shape[1], CHUNK)]
    ahead = dot(mlp_norm, w_fc1_ref[:, chunks[0]])
    for at, cols in enumerate(chunks):
        pre_act = ahead + bias_fc1_ref[:, cols]
        if at + 1 < len(chunks):
            ahead = dot(mlp_norm, w_fc1_ref[:, chunks[at + 1]])
        hidden, slope = gelu_pair(pre_act)
        hidden = hidden.astype(bf16)
        hidden_ref[:, cols] = hidden
        slope_ref[:, cols] = slope.astype(bf16)
        total = total + keep * dot(hidden, w_fc2_ref[cols, :])
    out_ref[0] = dot(squeeze_ref[...], total.astype(bf16)).astype(bf16)


def whole(shape):
    return pl.BlockSpec(shape, lambda step, *_: (0,) * len(shape))


def tiles(shape):
    return pl.BlockSpec(shape, lambda step, *_: (step,) + (0,) * (len(shape) - 1))


def run_forward(order, keep, tokens, regional, window_bias, region_bias, spread, squeeze, plain, mixed,
                gain1, bias1, w_qkv, bias_qkv, w_out, bias_out, gain2, bias2, w_fc1, bias_fc1, w_fc2, bias_fc2):
    windows = regional.shape[0]
    steps = windows // TILE
    rows = TILE * TALL
    hidden = w_fc1.shape[1]
    compact = squeeze.shape[0]
    args = (tokens, regional, window_bias, region_bias, spread, squeeze, plain, mixed,
            gain1, bias1, w_qkv, bias_qkv, w_out, bias_out, gain2, bias2, w_fc1, bias_fc1, w_fc2, bias_fc2)
    outs = [
        ((steps, compact, WIDTH), bf16, (1, compact, WIDTH)),
        ((windows, 3 * GROUPS, SLOT, LANES), bf16, (TILE, 3 * GROUPS, SLOT, LANES)),
        ((windows, 2 * GROUPS, SLOT, LANES), bf16, (TILE, 2 * GROUPS, SLOT, LANES)),
        ((windows, SLOT, WIDTH), bf16, (TILE, SLOT, WIDTH)),
        ((steps * rows, WIDTH), bf16, (rows, WIDTH)),
        ((steps * rows, WIDTH), f32, (rows, WIDTH)),
        ((steps * rows, hidden), bf16, (rows, hidden)),
        ((steps * rows, hidden), bf16, (rows, hidden)),
    ]
    fixed = [
        ((3 * GROUPS, REGIONS, LANES), bf16),
        ((2 * GROUPS, REGIONS, LANES), bf16),
        ((REGIONS, WIDTH), bf16),
    ]
    return pl.pallas_call(
        forward_kernel,
        grid_spec=pltpu.PrefetchScalarGridSpec(
            num_scalar_prefetch=2,
            grid=(steps,),
            in_specs=[whole(a.shape) for a in args],
            out_specs=[tiles(block) for _, _, block in outs] + [whole(s) for s, _ in fixed],
            scratch_shapes=[
                pltpu.VMEM((windows, SLOT, WIDTH), f32),
                pltpu.VMEM((TILE * SLOT, WIDTH), bf16),
                pltpu.VMEM((TILE, SLOT, WIDTH), f32),
            ],
        ),
        out_shape=[jax.ShapeDtypeStruct(s, d) for s, d, _ in outs]
        + [jax.ShapeDtypeStruct(s, d) for s, d in fixed],
        compiler_params=pltpu.CompilerParams(
            dimension_semantics=("arbitrary",), vmem_limit_bytes=VMEM_LIMIT
        ),
        cost_estimate=pl.CostEstimate(flops=30_000_000_000, bytes_accessed=60_000_000, transcendentals=20_000_000),
        name="forward",
    )(order, keep, *args)


def back_mlp_kernel(
    keep_ref, cot_ref, after_ref, mixed_ref, hidden_ref, slope_ref, stretch_ref,
    gain2_ref, bias2_ref, w_fc1_ref, w_fc2_ref, w_out_ref,
    grad_after_ref, grad_mixed_ref, early_ref, grad_out_ref, small_ref, bias_row_ref,
    sum_fc1, sum_fc2, sum_out, sums, sum_hidden,
):
    step = pl.program_id(0)
    last = pl.num_programs(0) - 1
    keep = keep_ref[0]

    @pl.when(step == 0)
    def clear():
        for ref in (sum_fc1, sum_fc2, sum_out, sums, sum_hidden):
            ref[...] = jnp.zeros_like(ref)

    unit, scale = normalize(after_ref[...])
    mlp_norm = (unit * gain2_ref[...] + bias2_ref[...]).astype(bf16)
    norm_turned = mlp_norm.T
    cot = dot(stretch_ref[...], cot_ref[0])
    grad_mlp = (keep * cot).astype(bf16)
    grad_turned = grad_mlp.T
    sums[0:1] += column_sum(grad_mlp.astype(f32))
    grad_norm = jnp.zeros(after_ref.shape, f32)
    chunks = [slice(at, at + CHUNK) for at in range(0, w_fc1_ref.shape[1], CHUNK)]
    ahead = dot_nt(grad_mlp, w_fc2_ref[chunks[0], :])
    for at, cols in enumerate(chunks):
        grad_hidden = ahead
        if at + 1 < len(chunks):
            ahead = dot_nt(grad_mlp, w_fc2_ref[chunks[at + 1], :])
        sum_fc2[:, cols] += dot(grad_turned, hidden_ref[:, cols])
        grad_pre = (slope_ref[:, cols].astype(f32) * grad_hidden).astype(bf16)
        sum_fc1[:, cols] += dot(norm_turned, grad_pre)
        sum_hidden[0:1, cols] += column_sum(grad_pre.astype(f32))
        grad_norm = grad_norm + dot_nt(grad_pre, w_fc1_ref[:, cols])
    sums[1:2] += column_sum(grad_norm * unit)
    sums[2:3] += column_sum(grad_norm)
    grad_after = cot + normalize_back(grad_norm * gain2_ref[...], unit, scale)
    grad_after_ref[...] = grad_after
    grad_branch = (keep * grad_after).astype(bf16)
    sums[3:4] += column_sum(grad_branch.astype(f32))
    sum_out[...] += dot(mixed_ref[...].T, grad_branch)
    grad_mixed = dot_nt(grad_branch, w_out_ref[...]).reshape(TILE, TALL, WIDTH)
    empty = jnp.zeros((TILE, SLOT - TALL, WIDTH), f32)
    grad_mixed = jnp.concatenate([grad_mixed, empty], axis=1).astype(bf16)
    for group in range(GROUPS):
        grad_mixed_ref[:, group] = grad_mixed[:, :, group * LANES : (group + 1) * LANES]

    @pl.when(step == last)
    def finish():
        for at in range(4):
            cols = slice(at * WIDTH, (at + 1) * WIDTH)
            early_ref[cols, :] = sum_fc1[:, cols].astype(bf16)
            early_ref[4 * WIDTH + at * WIDTH : 4 * WIDTH + (at + 1) * WIDTH, :] = (
                sum_fc2[:, cols].T.astype(bf16)
            )
        grad_out_ref[...] = sum_out[...]
        small_ref[...] = sums[...]
        bias_row_ref[...] = sum_hidden[...]


def run_back_mlp(keep, cot, after, mixed, hidden, slope, stretch, gain2, bias2, w_fc1, w_fc2, w_out):
    steps, compact, _ = cot.shape
    rows = TILE * TALL
    units = w_fc1.shape[1]
    tiled = [(1, compact, WIDTH), (rows, WIDTH), (rows, WIDTH), (rows, units), (rows, units)]
    fixed = (stretch, gain2, bias2, w_fc1, w_fc2, w_out)
    outs = [
        ((steps * rows, WIDTH), f32, (rows, WIDTH)),
        ((steps * TILE, GROUPS, SLOT, LANES), bf16, (TILE, GROUPS, SLOT, LANES)),
    ]
    whole_outs = [((2 * units, WIDTH), bf16), ((WIDTH, WIDTH), f32), ((8, WIDTH), f32), ((8, units), f32)]
    return pl.pallas_call(
        back_mlp_kernel,
        grid_spec=pltpu.PrefetchScalarGridSpec(
            num_scalar_prefetch=1,
            grid=(steps,),
            in_specs=[tiles(b) for b in tiled] + [whole(a.shape) for a in fixed],
            out_specs=[tiles(block) for _, _, block in outs] + [whole(s) for s, _ in whole_outs],
            scratch_shapes=[
                pltpu.VMEM((WIDTH, units), f32),
                pltpu.VMEM((WIDTH, units), f32),
                pltpu.VMEM((WIDTH, WIDTH), f32),
                pltpu.VMEM((8, WIDTH), f32),
                pltpu.VMEM((8, units), f32),
            ],
        ),
        out_shape=[jax.ShapeDtypeStruct(s, d) for s, d, _ in outs]
        + [jax.ShapeDtypeStruct(s, d) for s, d in whole_outs],
        compiler_params=pltpu.CompilerParams(
            dimension_semantics=("arbitrary",), vmem_limit_bytes=VMEM_LIMIT
        ),
        cost_estimate=pl.CostEstimate(flops=40_000_000_000, bytes_accessed=60_000_000, transcendentals=0),
        name="back_mlp",
    )(keep, cot, after, mixed, hidden, slope, *fixed)


def back_attention_kernel(
    first, last, order_ref, keep_ref,
    qkv_ref, probs_ref, joined_ref, grad_mixed_ref, grad_after_ref,
    plain_ref, mixed_mask_ref, head_ref, gain1_ref, bias1_ref, *refs,
):
    if first:
        held_in = ()
    else:
        held_in, refs = refs[:4], refs[5:]
    if last:
        (grad_out_ref, order_row_ref, regional_ref, qkv_r_ref, probs_r_ref, mixed_r_ref, w_qkv_ref, w_out_ref), refs = (
            refs[:8],
            refs[8:],
        )
        grad_qkv_ref, late_ref, regional_out_ref, small_ref, sum_qkv, sums, heads, after_heads = refs
    else:
        grad_qkv_ref, sum_qkv, sums, heads, after_heads = refs
    step = pl.program_id(0)
    plain = plain_ref[...]
    mixed = mixed_mask_ref[...]

    @pl.when(step == 0)
    def begin():
        for at, ref in enumerate((sum_qkv, sums, heads, after_heads)):
            ref[...] = jnp.zeros_like(ref) if first else held_in[at][...]

    def some(batch, carry):
        def window(at):
            rows = pl.ds(pl.multiple_of(at * SLOT, SLOT), SLOT)

            def put_grad(place, values):
                grad_qkv_ref[rows, place * LANES : (place + 1) * LANES] = values

            return (
                lambda place: qkv_ref[at, place],
                lambda place: probs_ref[at, place],
                lambda place: grad_mixed_ref[at, place],
                put_grad,
            )

        attend_windows_back([window(batch * TOGETHER + at) for at in range(TOGETHER)], plain, mixed)
        return carry

    lax.fori_loop(0, TILE // TOGETHER, some, 0)
    joined = joined_ref[...].reshape(TILE * SLOT, WIDTH)
    unit, _ = normalize(joined.astype(f32))
    normed = (unit * gain1_ref[...] + bias1_ref[...]).astype(bf16)
    grad_qkv = grad_qkv_ref[...]
    sum_qkv[...] += dot(normed.T, grad_qkv)
    sums[2:3] += column_sum(grad_qkv[:, :WIDTH].astype(f32))
    sums[3:4] += column_sum(grad_qkv[:, 2 * WIDTH :].astype(f32))
    rows = pl.ds(pl.multiple_of((step + (0 if first else FIRST_TILES)) * TILE, TILE), TILE)
    heads[rows, : 3 * WIDTH] = dot(head_ref[...], grad_qkv)
    heads[rows, 3 * WIDTH :] = dot(head_ref[...], joined)
    after_heads[rows] = jnp.concatenate(
        [grad_after_ref[at * TALL : at * TALL + 1] for at in range(TILE)], axis=0
    )
    if not last:
        return

    @pl.when(step == pl.num_programs(0) - 1)
    def finish():
        keep = keep_ref[0]
        gain1 = gain1_ref[...]
        grad_normed = dot_nt(heads[:, : 3 * WIDTH].astype(bf16), w_qkv_ref[...])
        unit, scale = normalize(heads[:, 3 * WIDTH :])
        grad_mid = after_heads[...] + normalize_back(grad_normed * gain1, unit, scale)
        windows = grad_mid.shape[0]
        raster = lax.broadcasted_iota(jnp.int32, (windows, windows), 0)
        came = dot((raster == order_row_ref[...]).astype(bf16), grad_mid.astype(bf16))
        grad_branch = (keep * came).astype(bf16)
        grad_mixed = dot_nt(grad_branch, w_out_ref[...]).astype(bf16)
        parts = {}
        attend_windows_back(
            [
                (
                    lambda place: qkv_r_ref[place],
                    lambda place: probs_r_ref[place],
                    lambda place: grad_mixed[:, place * LANES : (place + 1) * LANES],
                    parts.__setitem__,
                )
            ],
            plain,
            mixed,
        )
        grad_qkv_r = jnp.concatenate([parts[place] for place in range(3 * GROUPS)], axis=1)
        unit_r, scale_r = normalize(regional_ref[...].astype(f32))
        normed_r = (unit_r * gain1 + bias1_ref[...]).astype(bf16)
        total = sum_qkv[...] + dot(normed_r.T, grad_qkv_r)
        for part in range(3):
            cols = slice(part * WIDTH, (part + 1) * WIDTH)
            late_ref[cols, :] = total[:, cols].astype(bf16)
        late_ref[3 * WIDTH :, :] = (
            grad_out_ref[...] + dot(mixed_r_ref[...].T, grad_branch)
        ).astype(bf16)
        grad_normed_r = dot_nt(grad_qkv_r, w_qkv_ref[...])
        small_ref[...] = sums[...]
        small_ref[0:1] = column_sum(grad_normed_r * unit_r)
        small_ref[1:2] = column_sum(grad_normed_r)
        small_ref[2:3] += column_sum(grad_qkv_r[:, :WIDTH].astype(f32))
        small_ref[3:4] += column_sum(grad_qkv_r[:, 2 * WIDTH :].astype(f32))
        small_ref[4:5] = column_sum(grad_branch.astype(f32))
        regional_out_ref[...] = (
            came + normalize_back(grad_normed_r * gain1, unit_r, scale_r)
        ).astype(bf16)


def run_back_attention(order, keep, qkv, probs, joined, grad_mixed, grad_after, plain, mixed, head, gain1, bias1,
                       held=None, ending=None):
    windows = qkv.shape[0]
    steps = windows // TILE
    rows = TILE * TALL
    begin = 0 if held is None else FIRST_TILES
    count = FIRST_TILES if held is None else steps - FIRST_TILES

    def tile(shape):
        return pl.BlockSpec(shape, lambda step, *_: (step + begin,) + (0,) * (len(shape) - 1))

    tiled = [
        (TILE, 3 * GROUPS, SLOT, LANES),
        (TILE, 2 * GROUPS, SLOT, LANES),
        (TILE, SLOT, WIDTH),
        (TILE, GROUPS, SLOT, LANES),
        (rows, WIDTH),
    ]
    fixed = [plain, mixed, head, gain1, bias1]
    in_specs = [tile(b) for b in tiled] + [whole(a.shape) for a in fixed]
    args = [qkv, probs, joined, grad_mixed, grad_after] + fixed
    aliases = {}
    if held is not None:
        in_specs += [whole(a.shape) for a in held[:4]] + [pl.BlockSpec(memory_space=pl.ANY)]
        args += list(held)
        aliases = {2 + len(args) - 1: 0}
    if ending is not None:
        in_specs += [whole(a.shape) for a in ending]
        args += list(ending)
    held_shapes = [(WIDTH, 3 * WIDTH), (8, WIDTH), (windows, 4 * WIDTH), (windows, WIDTH)]
    outs = [((steps * TILE * SLOT, 3 * WIDTH), bf16, tile((TILE * SLOT, 3 * WIDTH)))]
    scratch = []
    if ending is None:
        outs += [(s, f32, whole(s)) for s in held_shapes]
    else:
        outs += [
            ((4 * WIDTH, WIDTH), bf16, whole((4 * WIDTH, WIDTH))),
            ((windows, WIDTH), bf16, whole((windows, WIDTH))),
            ((8, WIDTH), f32, whole((8, WIDTH))),
        ]
        scratch = [pltpu.VMEM(s, f32) for s in held_shapes]
    return pl.pallas_call(
        functools.partial(back_attention_kernel, held is None, ending is not None),
        grid_spec=pltpu.PrefetchScalarGridSpec(
            num_scalar_prefetch=2,
            grid=(count,),
            in_specs=in_specs,
            out_specs=[spec for _, _, spec in outs],
            scratch_shapes=scratch,
        ),
        out_shape=[jax.ShapeDtypeStruct(s, d) for s, d, _ in outs],
        input_output_aliases=aliases,
        compiler_params=pltpu.CompilerParams(
            dimension_semantics=("arbitrary",), vmem_limit_bytes=VMEM_LIMIT
        ),
        cost_estimate=pl.CostEstimate(
            flops=4_500_000_000 * count, bytes_accessed=5_000_000 * count, transcendentals=0
        ),
        name="back_attention",
    )(order, keep, *args)


def back_rows_kernel(
    order_ref, grad_qkv_ref, joined_ref, grad_after_ref, gather_ref, gain1_ref, w_qkv_ref,
    tokens_out_ref, small_ref, windows,
):
    step = pl.program_id(0)
    gain1 = gain1_ref[...]

    @pl.when(step == 0)
    def clear():
        small_ref[...] = jnp.zeros_like(small_ref)

    unit, scale = normalize(joined_ref[...].astype(f32).reshape(TILE * SLOT, WIDTH))
    grad_normed = dot_nt(grad_qkv_ref[...], w_qkv_ref[...])
    small_ref[0:1] += column_sum(grad_normed * unit)
    small_ref[1:2] += column_sum(grad_normed)
    grad_in = normalize_back(grad_normed * gain1, unit, scale)
    for at in range(TILE):
        rows = grad_in[at * SLOT : at * SLOT + TALL] + grad_after_ref[at * TALL : (at + 1) * TALL]
        windows[order_ref[step * TILE + at], :TALL] = rows

    @pl.when(step == pl.num_programs(0) - 1)
    def finish():
        def relay(line, carry):
            block = windows[pl.ds(line * TILE, TILE)][:, :TALL].reshape(TILE * TALL, WIDTH)
            tokens_out_ref[line] = dot(gather_ref[...], block.astype(bf16)).astype(bf16)
            return carry

        lax.fori_loop(0, REG_SIDE, relay, 0)


def run_back_rows(order, grad_qkv, joined, grad_after, gather, gain1, w_qkv):
    windows = joined.shape[0]
    tiled = [(TILE * SLOT, 3 * WIDTH), (TILE, SLOT, WIDTH), (TILE * TALL, WIDTH)]
    fixed = (gather, gain1, w_qkv)
    outs = [((REG_SIDE, gather.shape[0], WIDTH), bf16), ((8, WIDTH), f32)]
    return pl.pallas_call(
        back_rows_kernel,
        grid_spec=pltpu.PrefetchScalarGridSpec(
            num_scalar_prefetch=1,
            grid=(windows // TILE,),
            in_specs=[tiles(b) for b in tiled] + [whole(a.shape) for a in fixed],
            out_specs=[whole(s) for s, _ in outs],
            scratch_shapes=[pltpu.VMEM((windows, SLOT, WIDTH), f32)],
        ),
        out_shape=[jax.ShapeDtypeStruct(s, d) for s, d in outs],
        compiler_params=pltpu.CompilerParams(
            dimension_semantics=("arbitrary",), vmem_limit_bytes=VMEM_LIMIT
        ),
        cost_estimate=pl.CostEstimate(flops=15_000_000_000, bytes_accessed=30_000_000, transcendentals=0),
        name="back_rows",
    )(order, grad_qkv, joined, grad_after, *fixed)


def band_to_windows(band_values, win_count):
    trailing = band_values.shape[2:]
    blocks = band_values.reshape(
        (band_values.shape[0] // WIN_SIDE, WIN_SIDE, REG_SIDE, WIN_SIDE) + trailing
    )
    return jnp.swapaxes(blocks, 1, 2).reshape((win_count, WIN_SIDE * WIN_SIDE) + trailing)


def rank_of(keys):
    return jnp.sum(keys[None, :] < keys[:, None], axis=1)


def reduce_stages():
    img_bits = [("img", bit) for bit in range(lax.axis_size("img").bit_length() - 1)]
    dp_bits = [("dp", bit) for bit in range(lax.axis_size("dp").bit_length() - 1)]
    rest = img_bits[1:] + dp_bits
    return [img_bits[:1]] + [rest[at : at + 2] for at in range(0, len(rest), 2)]


def stage_peers(stage):
    dp_size, img_size = lax.axis_size("dp"), lax.axis_size("img")
    flat = lax.axis_index("dp") * img_size + lax.axis_index("img")
    masks = [(1 << bit) * (img_size if name == "dp" else 1) for name, bit in stage]
    own = sum(((flat // mask) % 2) << place for place, mask in enumerate(masks))
    moves = []
    for offset in range(1, 1 << len(masks)):
        flip = sum(mask for place, mask in enumerate(masks) if offset >> place & 1)
        moves.append((offset, [(at, at ^ flip) for at in range(dp_size * img_size)]))
    return own, moves


def sum_stage(rows, stage):
    own, moves = stage_peers(stage)
    parts = rows.reshape((1 << len(stage), -1) + rows.shape[1:])
    got = [
        lax.ppermute(lax.dynamic_index_in_dim(parts, own ^ offset, 0, False), ("dp", "img"), pairs)
        for offset, pairs in moves
    ]
    total = lax.dynamic_index_in_dim(parts, own, 0, False).astype(f32)
    for piece in got:
        total = total + piece.astype(f32)
    return total.astype(bf16)


def gather_stage(rows, stage):
    own, moves = stage_peers(stage)
    pieces = [rows] + [lax.ppermute(rows, ("dp", "img"), pairs) for _, pairs in moves]
    ordered = []
    for place in range(len(pieces)):
        piece = pieces[0]
        for offset in range(1, len(pieces)):
            piece = jnp.where((own ^ place) == offset, pieces[offset], piece)
        ordered.append(piece)
    return jnp.concatenate(ordered, axis=0)


def sum_small(rows, stages):
    for stage in stages:
        _, moves = stage_peers(stage)
        got = [lax.ppermute(rows, ("dp", "img"), pairs) for _, pairs in moves]
        for piece in got:
            rows = rows + piece
    return rows


def deal_kernel(pick_ref, region_ref, local_ref, out_ref):
    groups = out_ref.shape[0]
    for pair in range(out_ref.shape[1] // 16):
        head = region_ref[...] if pair == 0 else local_ref[2 * pair - 1]
        rows = jnp.concatenate([head, local_ref[2 * pair]], axis=0)
        out_ref[:, 16 * pair : 16 * pair + 16, :] = (
            dot(pick_ref[...], rows).astype(bf16).reshape(groups, 16, WIDTH)
        )


def collect_kernel(pick_ref, came_ref, region_ref, local_ref):
    slots = region_ref.shape[0]
    for pair in range(came_ref.shape[1] // 16):
        rows = came_ref[:, 16 * pair : 16 * pair + 16, :].reshape(2 * slots, WIDTH)
        rows = dot(pick_ref[...], rows).astype(bf16)
        if pair == 0:
            region_ref[...] = rows[:slots]
        else:
            local_ref[2 * pair - 1] = rows[:slots]
        local_ref[2 * pair] = rows[slots:]


def run_deal(pick, region, local):
    count = region.shape[0] // TILE
    return pl.pallas_call(
        deal_kernel,
        out_shape=jax.ShapeDtypeStruct((count, (local.shape[0] + 1) * TILE, WIDTH), bf16),
        compiler_params=pltpu.CompilerParams(vmem_limit_bytes=VMEM_LIMIT),
        cost_estimate=pl.CostEstimate(flops=1_000_000_000, bytes_accessed=7_000_000, transcendentals=0),
        name="deal",
    )(pick, region, local)


def run_collect(pick, came):
    slots = came.shape[0] * TILE
    return pl.pallas_call(
        collect_kernel,
        out_shape=[
            jax.ShapeDtypeStruct((slots, WIDTH), bf16),
            jax.ShapeDtypeStruct((came.shape[1] // TILE - 1, slots, WIDTH), bf16),
        ],
        compiler_params=pltpu.CompilerParams(vmem_limit_bytes=VMEM_LIMIT),
        cost_estimate=pl.CostEstimate(flops=1_000_000_000, bytes_accessed=7_000_000, transcendentals=0),
        name="collect",
    )(pick, came)


def swap_tiles(tiles_sent, devices):
    count, rows, width = tiles_sent.shape
    share = count * TILE // devices
    if share == TILE:
        return lax.all_to_all(tiles_sent, "dp", split_axis=0, concat_axis=0, tiled=True)
    places = rows // TILE
    sent = tiles_sent.reshape(count, places, TILE, width).transpose(1, 0, 2, 3)
    sent = sent.reshape(places, devices, share, width).transpose(1, 0, 2, 3)
    came = lax.all_to_all(sent, "dp", split_axis=0, concat_axis=0, tiled=True)
    came = came.transpose(1, 0, 2, 3).reshape(places, count, TILE, width)
    return came.transpose(1, 0, 2, 3).reshape(count, rows, width)


def row_maps():
    window = np.arange(TILE)[:, None]
    place = np.arange(WIN_SIDE * WIN_SIDE)[None, :]
    raster = place // WIN_SIDE * (TILE * WIN_SIDE) + window * WIN_SIDE + place % WIN_SIDE
    band = TILE * WIN_SIDE * WIN_SIDE
    spread = np.zeros((TILE * SLOT, band), np.float32)
    spread[window * SLOT + 1 + place, raster] = 1
    gather = np.zeros((band, TILE * TALL), np.float32)
    gather[raster, window * TALL + 1 + place] = 1
    head = np.zeros((TILE, TILE * SLOT), np.float32)
    head[np.arange(TILE), np.arange(TILE) * SLOT] = 1
    place = np.arange(WIN_SIDE * WIN_SIDE + 1)[None, :]
    squeeze = np.zeros(((WIN_SIDE * WIN_SIDE + 1) * TILE, TILE * TALL), np.float32)
    squeeze[place * TILE + window, window * TALL + place] = 1
    return [jnp.asarray(table, bf16) for table in (spread, gather, head, squeeze, squeeze.T)]


def shards(
    tokens,
    regional,
    pad_mask,
    keep_mask,
    window_slot,
    ln1_gain,
    ln1_bias,
    w_qkv,
    bias_q,
    bias_v,
    w_out,
    bias_out,
    ln2_gain,
    ln2_bias,
    w_fc1,
    bias_fc1,
    w_fc2,
    bias_fc2,
    cot_local,
    cot_regional,
):
    devices = lax.axis_size("dp")
    stages = reduce_stages()
    own_rank = lax.axis_index("dp")
    win_count = regional.shape[1]
    all_windows = window_slot.shape[1]
    slot_of = window_slot[0]
    places = jnp.arange(win_count)
    own_target = lax.dynamic_slice_in_dim(slot_of, own_rank * win_count, win_count) // win_count
    own_place = rank_of(own_target * win_count + places)
    order = jnp.sum(jnp.where(own_place[None, :] == places[:, None], places[None, :], 0), axis=1)
    slot_hit = slot_of[None, :] == (own_rank * win_count + places)[:, None]
    window_here = jnp.sum(jnp.where(slot_hit, jnp.arange(all_windows)[None, :], 0), axis=1)
    here_place = rank_of(window_here)
    deal_row = jnp.arange(2 * win_count)
    row_place = deal_row // (2 * TILE) * TILE + deal_row % TILE
    row_half = deal_row // TILE % 2
    column_hit = row_place[:, None] == jnp.concatenate([here_place, here_place])[None, :]
    pick = (column_hit & (row_half[:, None] == (deal_row // win_count)[None, :])).astype(bf16)
    pick_back = (column_hit & (row_half[:, None] == (deal_row // win_count)[None, :])).T.astype(bf16)
    cot = swap_tiles(
        run_deal(pick, cot_regional[0], jnp.swapaxes(cot_local[0], 0, 1)), devices
    )
    image = own_rank * win_count // REGIONS
    keep = lax.dynamic_slice_in_dim(keep_mask[0], image, 1).astype(f32) / survive
    live = band_to_windows(pad_mask[0], win_count) != 0
    allowed = jnp.concatenate(
        [jnp.ones((win_count, 1), bool), live, jnp.zeros((win_count, SLOT - 1 - live.shape[1]), bool)],
        axis=1,
    )
    window_bias = jnp.broadcast_to(
        jnp.where(allowed, 0.0, -1e30).astype(f32)[:, :, None], (win_count, SLOT, LANES)
    )
    region_bias = jnp.broadcast_to(
        jnp.where(live[:, 0], 0.0, -1e30).astype(f32)[:, None], (win_count, LANES)
    )
    spread, gather, head, squeeze, stretch = row_maps()
    plain, mixed_mask = head_masks()
    bias_qkv = jnp.concatenate([bias_q, jnp.zeros_like(bias_q), bias_v])[None]
    gain1, bias1, gain2, bias2 = ln1_gain[None], ln1_bias[None], ln2_gain[None], ln2_bias[None]
    out, qkv, probs, joined, mixed, after, hidden, slope, qkv_r, probs_r, mixed_r = run_forward(
        order, keep, tokens.reshape(REG_SIDE, -1, WIDTH), regional[0], window_bias, region_bias,
        spread, squeeze, plain, mixed_mask, gain1, bias1, w_qkv, bias_qkv, w_out, bias_out[None],
        gain2, bias2, w_fc1, bias_fc1[None], w_fc2, bias_fc2[None],
    )
    came = swap_tiles(out, devices)
    grad_after, grad_mixed, early, grad_out, small, row_fc1 = run_back_mlp(
        keep, cot, after, mixed, hidden, slope, stretch, gain2, bias2, w_fc1, w_fc2, w_out
    )
    early = sum_stage(early, stages[0])
    attention = (order, keep, qkv, probs, joined, grad_mixed, grad_after, plain, mixed_mask, head, gain1, bias1)
    grad_qkv, *held = run_back_attention(*attention)
    held, early = lax.optimization_barrier((held, early))
    early = sum_stage(early, stages[1])
    grad_qkv, late, regional_out, small_late = run_back_attention(
        *attention,
        held=(*held, grad_qkv),
        ending=(grad_out, order[None], regional[0], qkv_r, probs_r, mixed_r, w_qkv, w_out),
    )
    late = sum_stage(late, stages[0])
    grad_qkv, early, came = lax.optimization_barrier((grad_qkv, early, came))
    for stage in stages[2:]:
        early = sum_stage(early, stage)
    tokens_out, small_rows = run_back_rows(order, grad_qkv, joined, grad_after, gather, gain1, w_qkv)
    out_regional, out_local = run_collect(pick_back, came)
    vectors = jnp.concatenate(
        [
            small_late[0:2] + small_rows[0:2],
            small_late[2:4],
            small[3:4] + small_late[4:5],
            small[1:3],
            small[0:1],
            row_fc1[0].reshape(-1, WIDTH),
            jnp.zeros((4, WIDTH), f32),
        ],
        axis=0,
    )
    for stage in stages[1:]:
        late = sum_stage(late, stage)
    for stage in reversed(stages):
        early = gather_stage(early, stage)
    for stage in reversed(stages):
        late = gather_stage(late, stage)
    vectors = sum_small(vectors, stages)
    grad_w_qkv = jnp.concatenate([late[at * WIDTH : (at + 1) * WIDTH] for at in range(3)], axis=1)
    units = w_fc1.shape[1]
    grad_w_fc1 = jnp.concatenate(
        [early[at : at + WIDTH] for at in range(0, units, WIDTH)], axis=1
    )
    return (
        jnp.swapaxes(out_local, 0, 1)[None],
        out_regional[None],
        tokens_out.reshape(tokens.shape),
        regional_out[None],
        vectors[0],
        vectors[1],
        grad_w_qkv.astype(f32),
        vectors[2],
        vectors[3],
        late[3 * WIDTH :].astype(f32),
        vectors[4],
        vectors[5],
        vectors[6],
        grad_w_fc1.astype(f32),
        vectors[8:12].reshape(-1),
        early[units:].astype(f32),
        vectors[7],
    )


def solution(mesh):
    in_specs = (
        P("img", "dp", None, None),
        P("img", "dp", None),
        P("img", "dp", None),
        P("img", None),
        P("img", None),
        P(),
        P(),
        P(),
        P(),
        P(),
        P(),
        P(),
        P(),
        P(),
        P(),
        P(),
        P(),
        P(),
        P("img", "dp", None, None),
        P("img", "dp", None),
    )
    out_specs = (
        P("img", "dp", None, None),
        P("img", "dp", None),
        P("img", "dp", None, None),
        P("img", "dp", None),
        P(),
        P(),
        P(),
        P(),
        P(),
        P(),
        P(),
        P(),
        P(),
        P(),
        P(),
        P(),
        P(),
    )
    return jax.shard_map(shards, mesh=mesh, in_specs=in_specs, out_specs=out_specs, check_vma=False)
```

```python
import functools
import math
import jax
import jax.numpy as jnp
import numpy as np
from jax import lax
from jax.experimental import pallas as pl
from jax.experimental.pallas import tpu as pltpu
from jax.sharding import PartitionSpec as P

HEADS = 16
HDIM = 32
WIN_SIDE = 7
REG_SIDE = 8
REGIONS = 64

norm_eps = 1e-05
survive = 0.9

WIDTH = 512
SLOT = 64
TALL = 56
TILE = 8
GROUP = 4
GROUPS = HEADS // GROUP
TOGETHER = 8
LANES = 128
ROWS_FIRST = 2
FIRST_TILES = 3
CHUNK = 512
VMEM_LIMIT = 60 * 1024 * 1024

f32 = jnp.float32


def took(micros):
    return pl.CostEstimate(flops=int(micros * 1.15e9), bytes_accessed=1_000_000, transcendentals=0)

bf16 = jnp.bfloat16


def dot(left, right):
    return lax.dot_general(left, right, (((1,), (0,)), ((), ())), preferred_element_type=f32)


def dot_nt(left, right):
    return lax.dot_general(left, right, (((1,), (1,)), ((), ())), preferred_element_type=f32)


def head_masks():
    lane_head = np.arange(LANES) // HDIM
    plain = np.repeat(np.arange(GROUP), SLOT)
    mixed = np.repeat(np.array([0, 2, 1, 3]), SLOT)
    return (
        jnp.asarray(plain[:, None] == lane_head[None, :], bf16),
        jnp.asarray(mixed[:, None] == lane_head[None, :], bf16),
    )


def spread_heads(rows, mask):
    return jnp.concatenate([rows] * GROUP, axis=0) * mask


def turn(blocks):
    stacked = jnp.concatenate([blocks[:, :LANES], blocks[:, LANES:]], axis=0)
    turned = stacked.T
    return jnp.concatenate([turned[:SLOT], turned[SLOT:]], axis=1)


def attend_scores(items, plain):
    return [dot_nt(key_rows, spread_heads(queries, plain)) for queries, key_rows, _, _ in items]


def attend_probs(items, scores):
    probs = []
    for rows, (_, _, _, bias) in zip(scores, items):
        rows = rows + bias
        highest = jnp.max(rows, axis=0, keepdims=True)
        weighted = jnp.exp2((rows - highest) * (HDIM**-0.5 * math.log2(math.e)))
        total = jnp.sum(weighted, axis=0, keepdims=True)
        probs.append((weighted * (1.0 / total)).astype(bf16))
    return probs


def attend_mix(items, turned, mixed):
    return [dot(rows, spread_heads(item[2], mixed)) for rows, item in zip(turned, items)]


def attend_back(items, plain, mixed):
    wide = [spread_heads(item[4], plain) for item in items]
    grad_probs = [dot_nt(item[2], rows) for item, rows in zip(items, wide)]
    grad_values = [dot(item[3], rows) for item, rows in zip(items, wide)]
    scores = []
    for rows, item in zip(grad_probs, items):
        soft = item[3].astype(f32)
        weighted = soft * rows
        inner = jnp.sum(weighted, axis=0, keepdims=True)
        scores.append((weighted - soft * inner).astype(bf16))
    turned = [turn(rows) for rows in scores]
    factor = HDIM**-0.5
    grad_keys = [dot(rows, spread_heads(item[0], plain)) * factor for rows, item in zip(scores, items)]
    grad_queries = [dot(rows, spread_heads(item[1], mixed)) * factor for rows, item in zip(turned, items)]
    return list(zip(grad_queries, grad_keys, grad_values))


def normalize(rows):
    centered = rows - jnp.mean(rows, axis=-1, keepdims=True)
    spread = jnp.mean(centered * centered, axis=-1, keepdims=True)
    scale = lax.rsqrt(spread + norm_eps)
    return centered * scale, scale


def normalize_back(grad_unit, unit, scale):
    first = jnp.mean(grad_unit, axis=-1, keepdims=True)
    second = jnp.mean(grad_unit * unit, axis=-1, keepdims=True)
    return scale * (grad_unit - first - unit * second)


def gelu_pair(values):
    below = 0.5 + 0.5 * lax.erf(values * 0.7071067811865476)
    bell = jnp.exp2(values * values * (-0.5 * math.log2(math.e)))
    return values * below, below + values * bell * 0.3989422804014327


def fold_lanes(rows):
    return sum(rows[:, at : at + LANES] for at in range(0, rows.shape[1], LANES))


def column_sum(rows):
    return jnp.sum(rows, axis=0, keepdims=True)


def window_items(qkv_of, bias):
    wide = jnp.concatenate([bias, bias], axis=1)
    return [
        (qkv_of(group), qkv_of(GROUPS + group), qkv_of(2 * GROUPS + group), wide) for group in range(GROUPS)
    ]


def attend_windows_back(windows, plain, mixed):
    items = []
    for qkv_of, probs_of, grad_of, _ in windows:
        for group in range(GROUPS):
            probs = jnp.concatenate([probs_of(2 * group), probs_of(2 * group + 1)], axis=1)
            items.append(
                (qkv_of(group), qkv_of(GROUPS + group), qkv_of(2 * GROUPS + group), probs, grad_of(group))
            )
    grads = attend_back(items, plain, mixed)
    for at, (_, _, _, put_grad) in enumerate(windows):
        for group in range(GROUPS):
            for part in range(3):
                put_grad(part * GROUPS + group, grads[at * GROUPS + group][part].astype(bf16))


def forward_kernel(
    order_ref, keep_ref,
    tokens_ref, regional_ref, window_bias_ref, region_bias_ref, spread_ref, squeeze_ref,
    plain_ref, mixed_mask_ref, gain1_ref, bias1_ref, w_qkv_ref, bias_qkv_ref, w_out_ref, bias_out_ref,
    gain2_ref, bias2_ref, w_fc1_ref, bias_fc1_ref, w_fc2_ref, bias_fc2_ref,
    out_ref, qkv_ref, probs_ref, joined_ref, mixed_ref, after_ref, hidden_ref, slope_ref,
    qkv_r_ref, probs_r_ref, mixed_r_ref,
    windows, normed, mixed_rows, joined_rows,
):
    step = pl.program_id(0)
    last = pl.num_programs(0) - 1
    keep = keep_ref[0]
    plain = plain_ref[...]
    mixed = mixed_mask_ref[...]
    count = TILE * TALL
    chunks = [slice(at, at + CHUNK) for at in range(0, w_fc1_ref.shape[1], CHUNK)]
    tile = {}

    @pl.when(step == 0)
    def first():
        region = regional_ref[...].astype(f32)
        unit, _ = normalize(region)
        region_norm = (unit * gain1_ref[...] + bias1_ref[...]).astype(bf16)
        region_qkv = (dot(region_norm, w_qkv_ref[...]) + bias_qkv_ref[...]).astype(bf16)
        for at in range(3 * GROUPS):
            qkv_r_ref[at] = region_qkv[:, at * LANES : (at + 1) * LANES]
        items = window_items(lambda at: region_qkv[:, at * LANES : (at + 1) * LANES], region_bias_ref[...])
        probs = attend_probs(items, attend_scores(items, plain))
        for group in range(GROUPS):
            probs_r_ref[2 * group] = probs[group][:, :LANES]
            probs_r_ref[2 * group + 1] = probs[group][:, LANES:]
        outs = attend_mix(items, [turn(rows) for rows in probs], mixed)
        region_mixed = jnp.concatenate(outs, axis=1).astype(bf16)
        mixed_r_ref[...] = region_mixed
        region_mid = region + keep * (dot(region_mixed, w_out_ref[...]) + bias_out_ref[...])
        region_mid = region_mid.astype(bf16)
        row = lax.broadcasted_iota(jnp.int32, (TILE * SLOT, REGIONS), 0)
        column = lax.broadcasted_iota(jnp.int32, (TILE * SLOT, REGIONS), 1)

        def relay(line, carry):
            pick = (row == (column - line * TILE) * SLOT).astype(bf16)
            rows = dot(spread_ref[...], tokens_ref[line]) + dot(pick, region_mid)
            windows[pl.ds(line * TILE, TILE)] = rows.reshape(TILE, SLOT, WIDTH)
            return carry

        lax.fori_loop(0, REG_SIDE, relay, 0)


    def norm_rows():
        for at in range(TILE):
            rows = windows[order_ref[step * TILE + at]]
            joined_ref[at] = rows.astype(bf16)
            unit, _ = normalize(rows)
            normed[at * SLOT : (at + 1) * SLOT] = (unit * gain1_ref[...] + bias1_ref[...]).astype(bf16)

    def project(part):
        cols = slice(part * WIDTH, (part + 1) * WIDTH)
        qkv = dot(normed[...], w_qkv_ref[:, cols]) + bias_qkv_ref[:, cols]
        qkv = qkv.astype(bf16).reshape(TILE, SLOT, WIDTH)
        for group in range(GROUPS):
            qkv_ref[:, part * GROUPS + group] = qkv[:, :, group * LANES : (group + 1) * LANES]

    def score(half):
        items = []
        for at in half:
            bias = window_bias_ref[order_ref[step * TILE + at]]
            items += window_items(lambda place, at=at: qkv_ref[at, place], bias)
        return items, attend_scores(items, plain)

    def soften(half, items, scores):
        probs = attend_probs(items, scores)
        for at, rows in enumerate(probs):
            window, group = half[at // GROUPS], at % GROUPS
            probs_ref[window, 2 * group] = rows[:, :LANES]
            probs_ref[window, 2 * group + 1] = rows[:, LANES:]
        return [turn(rows) for rows in probs]

    def mix(half, items, turned):
        outs = attend_mix(items, turned, mixed)
        for at, rows in enumerate(outs):
            window, group = half[at // GROUPS], at % GROUPS
            mixed_rows[window, :, group * LANES : (group + 1) * LANES] = rows

    def keep_joined():
        for at in range(TILE):
            joined_rows[at] = joined_ref[at].astype(f32)


    def branch():
        mixed_low = mixed_rows[:, :TALL].reshape(count, WIDTH).astype(bf16)
        mixed_ref[...] = mixed_low
        after = joined_rows[:, :TALL].reshape(count, WIDTH) + keep * (
            dot(mixed_low, w_out_ref[...]) + bias_out_ref[...]
        )
        after_ref[...] = after

    def norm_after():
        unit, _ = normalize(after_ref[...])
        tile["norm"] = (unit * gain2_ref[...] + bias2_ref[...]).astype(bf16)
        tile["total"] = jnp.zeros((count, WIDTH), f32)

    def widen(at):
        tile[at] = dot(tile["norm"], w_fc1_ref[:, chunks[at]])

    def bend(at):
        cols = chunks[at]
        hidden, slope = gelu_pair(tile[at] + bias_fc1_ref[:, cols])
        tile[at] = hidden.astype(bf16)
        hidden_ref[:, cols] = tile[at]
        slope_ref[:, cols] = slope.astype(bf16)

    def narrow(at):
        tile["total"] = tile["total"] + dot(tile[at], w_fc2_ref[chunks[at], :])

    def send():
        result = after_ref[...] + keep * (tile["total"] + bias_fc2_ref[...])
        out_ref[0] = dot(squeeze_ref[...], result.astype(bf16)).astype(bf16)

    halves = [list(range(TILE // 2)), list(range(TILE // 2, TILE))]

    @pl.when(step == 0)
    def attention_only():
        norm_rows()
        for part in range(3):
            project(part)
        scored = [score(half) for half in halves]
        turned = [soften(half, *pair) for half, pair in zip(halves, scored)]
        for half, pair, rows in zip(halves, scored, turned):
            mix(half, pair[0], rows)
        keep_joined()

    @pl.when((step > 0) & (step < last))
    def both():
        branch()
        norm_rows()
        project(0)
        norm_after()
        project(1)
        widen(0)
        project(2)
        widen(1)
        bend(0)
        scored = [score(halves[0]), None]
        narrow(0)
        bend(1)
        widen(2)
        scored[1] = score(halves[1])
        turned = [soften(halves[0], *scored[0]), None]
        narrow(1)
        widen(3)
        bend(2)
        mix(halves[0], scored[0][0], turned[0])
        turned[1] = soften(halves[1], *scored[1])
        narrow(2)
        bend(3)
        mix(halves[1], scored[1][0], turned[1])
        narrow(3)
        send()
        keep_joined()

    @pl.when(step == last)
    def feed_only():
        branch()
        norm_after()
        widen(0)
        for at in range(len(chunks)):
            if at + 1 < len(chunks):
                widen(at + 1)
            bend(at)
            narrow(at)
        send()


def whole(shape):
    return pl.BlockSpec(shape, lambda step, *_: (0,) * len(shape))


def tiles(shape):
    return pl.BlockSpec(shape, lambda step, *_: (step,) + (0,) * (len(shape) - 1))


def run_forward(order, keep, tokens, regional, window_bias, region_bias, spread, squeeze, plain, mixed,
                gain1, bias1, w_qkv, bias_qkv, w_out, bias_out, gain2, bias2, w_fc1, bias_fc1, w_fc2, bias_fc2):
    windows = regional.shape[0]
    steps = windows // TILE
    rows = TILE * TALL
    hidden = w_fc1.shape[1]
    compact = squeeze.shape[0]
    args = (tokens, regional, window_bias, region_bias, spread, squeeze, plain, mixed,
            gain1, bias1, w_qkv, bias_qkv, w_out, bias_out, gain2, bias2, w_fc1, bias_fc1, w_fc2, bias_fc2)
    def ahead(shape):
        return pl.BlockSpec(
            shape, lambda step, *_: (jnp.minimum(step, steps - 1),) + (0,) * (len(shape) - 1)
        )

    def behind(shape):
        return pl.BlockSpec(shape, lambda step, *_: (jnp.maximum(step - 1, 0),) + (0,) * (len(shape) - 1))

    outs = [
        ((steps, compact, WIDTH), bf16, behind((1, compact, WIDTH))),
        ((windows, 3 * GROUPS, SLOT, LANES), bf16, ahead((TILE, 3 * GROUPS, SLOT, LANES))),
        ((windows, 2 * GROUPS, SLOT, LANES), bf16, ahead((TILE, 2 * GROUPS, SLOT, LANES))),
        ((windows, SLOT, WIDTH), bf16, ahead((TILE, SLOT, WIDTH))),
        ((steps * rows, WIDTH), bf16, behind((rows, WIDTH))),
        ((steps * rows, WIDTH), f32, behind((rows, WIDTH))),
        ((steps * rows, hidden), bf16, behind((rows, hidden))),
        ((steps * rows, hidden), bf16, behind((rows, hidden))),
    ]
    fixed = [
        ((3 * GROUPS, REGIONS, LANES), bf16),
        ((2 * GROUPS, REGIONS, LANES), bf16),
        ((REGIONS, WIDTH), bf16),
    ]
    return pl.pallas_call(
        forward_kernel,
        grid_spec=pltpu.PrefetchScalarGridSpec(
            num_scalar_prefetch=2,
            grid=(steps + 1,),
            in_specs=[whole(a.shape) for a in args],
            out_specs=[spec for _, _, spec in outs] + [whole(s) for s, _ in fixed],
            scratch_shapes=[
                pltpu.VMEM((windows, SLOT, WIDTH), f32),
                pltpu.VMEM((TILE * SLOT, WIDTH), bf16),
                pltpu.VMEM((TILE, SLOT, WIDTH), f32),
                pltpu.VMEM((TILE, SLOT, WIDTH), f32),
            ],
        ),
        out_shape=[jax.ShapeDtypeStruct(s, d) for s, d, _ in outs]
        + [jax.ShapeDtypeStruct(s, d) for s, d in fixed],
        compiler_params=pltpu.CompilerParams(
            dimension_semantics=("arbitrary",), vmem_limit_bytes=VMEM_LIMIT
        ),
        cost_estimate=took(61),
        name="forward",
    )(order, keep, *args)


def put_shares(own, keep_ref, send_ref, chunk_of):
    half = keep_ref.shape[0]

    def fill(refs):
        for which, ref in enumerate(refs):
            for at in range(half):
                ref[at ^ (own % half)] = chunk_of(which * half + at)

    @pl.when(own < half)
    def low():
        fill((keep_ref, send_ref))

    @pl.when(own >= half)
    def high():
        fill((send_ref, keep_ref))


def back_mlp_kernel(
    keep_ref, own_ref, cot_ref, after_ref, mixed_ref, hidden_ref, slope_ref, stretch_ref,
    gain2_ref, bias2_ref, w_fc1_ref, w_fc2_ref, w_out_ref,
    grad_after_ref, grad_mixed_ref, stay_ref, send_ref, grad_out_ref, small_ref, bias_row_ref,
    sum_fc1, sum_fc2, sum_out, sums, sum_hidden, early_rows,
):
    step = pl.program_id(0)
    last = pl.num_programs(0) - 1
    keep = keep_ref[0]

    @pl.when(step == 0)
    def clear():
        for ref in (sum_fc1, sum_fc2, sum_out, sums, sum_hidden):
            ref[...] = jnp.zeros_like(ref)

    unit, scale = normalize(after_ref[...])
    mlp_norm = (unit * gain2_ref[...] + bias2_ref[...]).astype(bf16)
    norm_turned = mlp_norm.T
    cot = dot(stretch_ref[...], cot_ref[0])
    grad_mlp = (keep * cot).astype(bf16)
    grad_turned = grad_mlp.T
    sums[0:1] += column_sum(grad_mlp.astype(f32))
    grad_norm = jnp.zeros(after_ref.shape, f32)
    chunks = [slice(at, at + CHUNK) for at in range(0, w_fc1_ref.shape[1], CHUNK)]
    ahead = dot_nt(grad_mlp, w_fc2_ref[chunks[0], :])
    for at, cols in enumerate(chunks):
        grad_hidden = ahead
        if at + 1 < len(chunks):
            ahead = dot_nt(grad_mlp, w_fc2_ref[chunks[at + 1], :])
        sum_fc2[:, cols] += dot(grad_turned, hidden_ref[:, cols])
        grad_pre = (slope_ref[:, cols].astype(f32) * grad_hidden).astype(bf16)
        sum_fc1[:, cols] += dot(norm_turned, grad_pre)
        sum_hidden[0:1, cols] += column_sum(grad_pre.astype(f32))
        grad_norm = grad_norm + dot_nt(grad_pre, w_fc1_ref[:, cols])
    sums[1:2] += column_sum(grad_norm * unit)
    sums[2:3] += column_sum(grad_norm)
    grad_after = cot + normalize_back(grad_norm * gain2_ref[...], unit, scale)
    grad_after_ref[...] = grad_after
    grad_branch = (keep * grad_after).astype(bf16)
    sums[3:4] += column_sum(grad_branch.astype(f32))
    sum_out[...] += dot(mixed_ref[...].T, grad_branch)
    grad_mixed = dot_nt(grad_branch, w_out_ref[...]).reshape(TILE, TALL, WIDTH)
    empty = jnp.zeros((TILE, SLOT - TALL, WIDTH), f32)
    grad_mixed = jnp.concatenate([grad_mixed, empty], axis=1).astype(bf16)
    for group in range(GROUPS):
        grad_mixed_ref[:, group] = grad_mixed[:, :, group * LANES : (group + 1) * LANES]

    @pl.when(step == last)
    def finish():
        for at in range(4):
            cols = slice(at * WIDTH, (at + 1) * WIDTH)
            early_rows[cols, :] = sum_fc1[:, cols].astype(bf16)
            early_rows[4 * WIDTH + at * WIDTH : 4 * WIDTH + (at + 1) * WIDTH, :] = (
                sum_fc2[:, cols].T.astype(bf16)
            )
        rows = stay_ref.shape[1]
        put_shares(
            own_ref[0], stay_ref, send_ref, lambda at: early_rows[at * rows : (at + 1) * rows, :]
        )
        grad_out_ref[...] = sum_out[...]
        small_ref[...] = sums[...]
        bias_row_ref[...] = sum_hidden[...]


def run_back_mlp(parts, keep, own, cot, after, mixed, hidden, slope, stretch, gain2, bias2, w_fc1, w_fc2, w_out):
    steps, compact, _ = cot.shape
    rows = TILE * TALL
    units = w_fc1.shape[1]
    tiled = [(1, compact, WIDTH), (rows, WIDTH), (rows, WIDTH), (rows, units), (rows, units)]
    fixed = (stretch, gain2, bias2, w_fc1, w_fc2, w_out)
    outs = [
        ((steps * rows, WIDTH), f32, (rows, WIDTH)),
        ((steps * TILE, GROUPS, SLOT, LANES), bf16, (TILE, GROUPS, SLOT, LANES)),
    ]
    share = (parts // 2, 2 * units // parts, WIDTH)
    whole_outs = [(share, bf16), (share, bf16), ((WIDTH, WIDTH), f32), ((8, WIDTH), f32), ((8, units), f32)]
    return pl.pallas_call(
        back_mlp_kernel,
        grid_spec=pltpu.PrefetchScalarGridSpec(
            num_scalar_prefetch=2,
            grid=(steps,),
            in_specs=[tiles(b) for b in tiled] + [whole(a.shape) for a in fixed],
            out_specs=[tiles(block) for _, _, block in outs] + [whole(s) for s, _ in whole_outs],
            scratch_shapes=[
                pltpu.VMEM((WIDTH, units), f32),
                pltpu.VMEM((WIDTH, units), f32),
                pltpu.VMEM((WIDTH, WIDTH), f32),
                pltpu.VMEM((8, WIDTH), f32),
                pltpu.VMEM((8, units), f32),
                pltpu.VMEM((2 * units, WIDTH), bf16),
            ],
        ),
        out_shape=[jax.ShapeDtypeStruct(s, d) for s, d, _ in outs]
        + [jax.ShapeDtypeStruct(s, d) for s, d in whole_outs],
        compiler_params=pltpu.CompilerParams(
            dimension_semantics=("arbitrary",), vmem_limit_bytes=VMEM_LIMIT
        ),
        cost_estimate=took(55),
        name="back_mlp",
    )(keep, own, cot, after, mixed, hidden, slope, *fixed)


def back_attention_kernel(
    first, last, order_ref, keep_ref, own_ref,
    qkv_ref, probs_ref, joined_ref, grad_mixed_ref, grad_after_ref,
    plain_ref, mixed_mask_ref, head_ref, gain1_ref, bias1_ref, *refs,
):
    if first:
        held_in = ()
    else:
        held_in, refs = refs[:4], refs[5:]
    if last:
        ending, refs = refs[:10], refs[10:]
        grad_out_ref, order_row_ref, regional_ref, qkv_r_ref, probs_r_ref, mixed_r_ref = ending[:6]
        w_qkv_ref, w_out_ref, sums_mlp_ref, row_fc1_ref = ending[6:]
        grad_qkv_ref, stay_ref, send_ref, regional_out_ref, sum_qkv, sums, heads, after_heads, late_rows = refs
    else:
        grad_qkv_ref, sum_qkv, sums, heads, after_heads = refs
    step = pl.program_id(0)
    plain = plain_ref[...]
    mixed = mixed_mask_ref[...]

    @pl.when(step == 0)
    def begin():
        for at, ref in enumerate((sum_qkv, sums, heads, after_heads)):
            ref[...] = jnp.zeros_like(ref) if first else held_in[at][...]

    def some(batch, carry):
        def window(at):
            rows = pl.ds(pl.multiple_of(at * SLOT, SLOT), SLOT)

            def put_grad(place, values):
                grad_qkv_ref[rows, place * LANES : (place + 1) * LANES] = values

            return (
                lambda place: qkv_ref[at, place],
                lambda place: probs_ref[at, place],
                lambda place: grad_mixed_ref[at, place],
                put_grad,
            )

        attend_windows_back([window(batch * TOGETHER + at) for at in range(TOGETHER)], plain, mixed)
        return carry

    lax.fori_loop(0, TILE // TOGETHER, some, 0)
    joined = joined_ref[...].reshape(TILE * SLOT, WIDTH)
    unit, _ = normalize(joined.astype(f32))
    normed = (unit * gain1_ref[...] + bias1_ref[...]).astype(bf16)
    grad_qkv = grad_qkv_ref[...]
    sum_qkv[...] += dot(normed.T, grad_qkv)
    sums[0:1] += column_sum(grad_qkv.astype(f32))
    rows = pl.ds(pl.multiple_of((step + (0 if first else FIRST_TILES)) * TILE, TILE), TILE)
    heads[rows, : 3 * WIDTH] = dot(head_ref[...], grad_qkv)
    heads[rows, 3 * WIDTH :] = dot(head_ref[...], joined)
    after_heads[rows] = jnp.concatenate(
        [grad_after_ref[at * TALL : at * TALL + 1] for at in range(TILE)], axis=0
    )
    if not last:
        return

    @pl.when(step == pl.num_programs(0) - 1)
    def finish():
        keep = keep_ref[0]
        gain1 = gain1_ref[...]
        grad_normed = dot_nt(heads[:, : 3 * WIDTH].astype(bf16), w_qkv_ref[...])
        unit, scale = normalize(heads[:, 3 * WIDTH :])
        grad_mid = after_heads[...] + normalize_back(grad_normed * gain1, unit, scale)
        windows = grad_mid.shape[0]
        raster = lax.broadcasted_iota(jnp.int32, (windows, windows), 0)
        came = dot((raster == order_row_ref[...]).astype(bf16), grad_mid.astype(bf16))
        grad_branch = (keep * came).astype(bf16)
        grad_mixed = dot_nt(grad_branch, w_out_ref[...]).astype(bf16)
        parts = {}
        attend_windows_back(
            [
                (
                    lambda place: qkv_r_ref[place],
                    lambda place: probs_r_ref[place],
                    lambda place: grad_mixed[:, place * LANES : (place + 1) * LANES],
                    parts.__setitem__,
                )
            ],
            plain,
            mixed,
        )
        grad_qkv_r = jnp.concatenate([parts[place] for place in range(3 * GROUPS)], axis=1)
        unit_r, scale_r = normalize(regional_ref[...].astype(f32))
        normed_r = (unit_r * gain1 + bias1_ref[...]).astype(bf16)
        total = sum_qkv[...] + dot(normed_r.T, grad_qkv_r)
        columns = sums[0:1] + column_sum(grad_qkv_r.astype(f32))
        for part in range(3):
            cols = slice(part * WIDTH, (part + 1) * WIDTH)
            late_rows[cols, :] = total[:, cols].astype(bf16)
        late_rows[3 * WIDTH :, :] = (
            grad_out_ref[...] + dot(mixed_r_ref[...].T, grad_branch)
        ).astype(bf16)
        weights = w_qkv_ref[...].astype(f32)
        by_bias = weights * columns
        by_gain = weights * total
        turned_bias = fold_lanes(by_bias).T
        turned_gain = fold_lanes(by_gain).T
        grad_bias1 = column_sum(turned_bias)
        grad_gain1 = (column_sum(turned_gain) - bias1_ref[...] * grad_bias1) / gain1
        small = [
            grad_gain1,
            grad_bias1,
            columns[:, :WIDTH],
            columns[:, 2 * WIDTH :],
            sums_mlp_ref[3:4] + column_sum(grad_branch.astype(f32)),
            sums_mlp_ref[1:2],
            sums_mlp_ref[2:3],
            sums_mlp_ref[0:1],
        ]
        units = row_fc1_ref.shape[1] // WIDTH
        more = [row_fc1_ref[0:1, at * WIDTH : (at + 1) * WIDTH] for at in range(units)]
        more.append(jnp.zeros((8 - units, WIDTH), f32))
        share = stay_ref.shape[1] - 8

        def chunk_of(part):
            extra = jnp.zeros((8, WIDTH), f32)
            if part < 2:
                extra = jnp.concatenate(more if part else small, axis=0)
            rows = late_rows[part * share : (part + 1) * share]
            return jnp.concatenate([rows, extra.astype(bf16)], axis=0)

        put_shares(own_ref[0], stay_ref, send_ref, chunk_of)
        grad_normed_r = dot_nt(grad_qkv_r, w_qkv_ref[...])
        regional_out_ref[...] = (
            came + normalize_back(grad_normed_r * gain1, unit_r, scale_r)
        ).astype(bf16)


def run_back_attention(order, keep, own, qkv, probs, joined, grad_mixed, grad_after, plain, mixed, head, gain1, bias1,
                       held=None, ending=None, parts=1):
    windows = qkv.shape[0]
    steps = windows // TILE
    rows = TILE * TALL
    begin = 0 if held is None else FIRST_TILES
    count = FIRST_TILES if held is None else steps - FIRST_TILES

    def tile(shape):
        return pl.BlockSpec(shape, lambda step, *_: (step + begin,) + (0,) * (len(shape) - 1))

    tiled = [
        (TILE, 3 * GROUPS, SLOT, LANES),
        (TILE, 2 * GROUPS, SLOT, LANES),
        (TILE, SLOT, WIDTH),
        (TILE, GROUPS, SLOT, LANES),
        (rows, WIDTH),
    ]
    fixed = [plain, mixed, head, gain1, bias1]
    in_specs = [tile(b) for b in tiled] + [whole(a.shape) for a in fixed]
    args = [qkv, probs, joined, grad_mixed, grad_after] + fixed
    aliases = {}
    if held is not None:
        in_specs += [whole(a.shape) for a in held[:4]] + [pl.BlockSpec(memory_space=pl.ANY)]
        args += list(held)
        aliases = {3 + len(args) - 1: 0}
    if ending is not None:
        in_specs += [whole(a.shape) for a in ending]
        args += list(ending)
    held_shapes = [(WIDTH, 3 * WIDTH), (8, 3 * WIDTH), (windows, 4 * WIDTH), (windows, WIDTH)]
    outs = [((steps * TILE * SLOT, 3 * WIDTH), bf16, tile((TILE * SLOT, 3 * WIDTH)))]
    scratch = []
    late_shape = (parts // 2, 4 * WIDTH // parts + 8, WIDTH)
    if ending is None:
        outs += [(s, f32, whole(s)) for s in held_shapes]
    else:
        outs += [
            (late_shape, bf16, whole(late_shape)),
            (late_shape, bf16, whole(late_shape)),
            ((windows, WIDTH), bf16, whole((windows, WIDTH))),
        ]
        scratch = [pltpu.VMEM(s, f32) for s in held_shapes] + [pltpu.VMEM((4 * WIDTH, WIDTH), bf16)]
    return pl.pallas_call(
        functools.partial(back_attention_kernel, held is None, ending is not None),
        grid_spec=pltpu.PrefetchScalarGridSpec(
            num_scalar_prefetch=3,
            grid=(count,),
            in_specs=in_specs,
            out_specs=[spec for _, _, spec in outs],
            scratch_shapes=scratch,
        ),
        out_shape=[jax.ShapeDtypeStruct(s, d) for s, d, _ in outs],
        input_output_aliases=aliases,
        compiler_params=pltpu.CompilerParams(
            dimension_semantics=("arbitrary",), vmem_limit_bytes=VMEM_LIMIT
        ),
        cost_estimate=took(5 * count),
        name="back_attention",
    )(order, keep, own, *args)


def back_rows_kernel(begin, order_ref, grad_qkv_ref, joined_ref, grad_after_ref, gain1_ref, w_qkv_ref, *refs):
    windows_ref, rows_low, done = refs[-3:]
    step = pl.program_id(0)

    def copies(at_step):
        places = [order_ref[(begin + at_step) * TILE + at] for at in range(TILE)]
        return [
            pltpu.make_async_copy(rows_low.at[at], windows_ref.at[place], done.at[at])
            for at, place in enumerate(places)
        ]

    unit, scale = normalize(joined_ref[...].astype(f32).reshape(TILE * SLOT, WIDTH))
    grad_normed = dot_nt(grad_qkv_ref[...], w_qkv_ref[...])
    grad_in = normalize_back(grad_normed * gain1_ref[...], unit, scale)

    @pl.when(step > 0)
    def drain():
        for copy in copies(step - 1):
            copy.wait()

    empty = jnp.zeros((SLOT - TALL, WIDTH), f32)
    for at in range(TILE):
        rows = grad_in[at * SLOT : at * SLOT + TALL] + grad_after_ref[at * TALL : (at + 1) * TALL]
        rows_low[at] = jnp.concatenate([rows, empty], axis=0).astype(bf16)
    for copy in copies(step):
        copy.start()

    @pl.when(step == pl.num_programs(0) - 1)
    def finish():
        for copy in copies(step):
            copy.wait()


def run_back_rows(order, grad_qkv, joined, grad_after, gain1, w_qkv, begin, count, held=None):
    windows = joined.shape[0]

    def tile(shape):
        return pl.BlockSpec(shape, lambda step, *_: (step + begin,) + (0,) * (len(shape) - 1))

    tiled = [(TILE * SLOT, 3 * WIDTH), (TILE, SLOT, WIDTH), (TILE * TALL, WIDTH)]
    fixed = [gain1, w_qkv]
    in_specs = [tile(b) for b in tiled] + [whole(a.shape) for a in fixed]
    args = [grad_qkv, joined, grad_after] + fixed
    aliases = {}
    if held is not None:
        in_specs.append(pl.BlockSpec(memory_space=pl.ANY))
        args.append(held)
        aliases = {len(args): 0}
    return pl.pallas_call(
        functools.partial(back_rows_kernel, begin),
        grid_spec=pltpu.PrefetchScalarGridSpec(
            num_scalar_prefetch=1,
            grid=(count,),
            in_specs=in_specs,
            out_specs=pl.BlockSpec(memory_space=pl.ANY),
            scratch_shapes=[pltpu.VMEM((TILE, SLOT, WIDTH), bf16), pltpu.SemaphoreType.DMA((TILE,))],
        ),
        out_shape=jax.ShapeDtypeStruct((windows, SLOT, WIDTH), bf16),
        input_output_aliases=aliases,
        compiler_params=pltpu.CompilerParams(
            dimension_semantics=("arbitrary",), vmem_limit_bytes=VMEM_LIMIT
        ),
        cost_estimate=took(2.5 * count),
        name="back_rows",
    )(order, *args)


def relay_kernel(gather_ref, windows_ref, tokens_out_ref):
    for line in range(tokens_out_ref.shape[0]):
        rows = windows_ref[line * TILE : (line + 1) * TILE].reshape(TILE * SLOT, WIDTH)
        tokens_out_ref[line] = dot(gather_ref[...], rows).astype(bf16)


def run_relay(gather, windows):
    lines = windows.shape[0] // TILE
    return pl.pallas_call(
        relay_kernel,
        grid=(lines // 2,),
        in_specs=[whole(gather.shape), tiles((2 * TILE, SLOT, WIDTH))],
        out_specs=tiles((2, gather.shape[0], WIDTH)),
        out_shape=jax.ShapeDtypeStruct((lines, gather.shape[0], WIDTH), bf16),
        compiler_params=pltpu.CompilerParams(
            dimension_semantics=("arbitrary",), vmem_limit_bytes=VMEM_LIMIT
        ),
        cost_estimate=took(5),
        name="relay",
    )(gather, windows)


def early_out_kernel(own_ref, near_ref, far_ref, fc1_ref, fc2_ref):
    block = pl.program_id(0)
    per, share, _ = near_ref.shape
    inner = own_ref[0] % per
    place = block ^ (own_ref[0] // per)

    def fill(rows_ref):
        @pl.when(block < 2)
        def first():
            for at in range(per):
                start = at * share
                column = start // WIDTH * WIDTH
                fc1_ref[start - column : start - column + share, column : column + WIDTH] = rows_ref[
                    at ^ inner
                ].astype(f32)

        @pl.when(block >= 2)
        def second():
            for at in range(per):
                fc2_ref[at * share : (at + 1) * share] = rows_ref[at ^ inner].astype(f32)

    @pl.when(place < 2)
    def near():
        fill(near_ref)

    @pl.when(place >= 2)
    def far():
        fill(far_ref)


def run_early_out(own, near, far, units):
    half, share, _ = near.shape
    per = half // 2
    return pl.pallas_call(
        early_out_kernel,
        grid_spec=pltpu.PrefetchScalarGridSpec(
            num_scalar_prefetch=1,
            grid=(4,),
            in_specs=[
                pl.BlockSpec((per, share, WIDTH), lambda at, own: (jnp.minimum(at ^ (own[0] // per), 1), 0, 0)),
                pl.BlockSpec(
                    (per, share, WIDTH), lambda at, own: (jnp.maximum((at ^ (own[0] // per)) - 2, 0), 0, 0)
                ),
            ],
            out_specs=[
                pl.BlockSpec((WIDTH, units // 2), lambda at, own: (0, jnp.minimum(at, 1))),
                pl.BlockSpec((units // 2, WIDTH), lambda at, own: (jnp.maximum(at - 2, 0), 0)),
            ],
        ),
        out_shape=[
            jax.ShapeDtypeStruct((WIDTH, units), f32),
            jax.ShapeDtypeStruct((units, WIDTH), f32),
        ],
        compiler_params=pltpu.CompilerParams(
            dimension_semantics=("arbitrary",), vmem_limit_bytes=VMEM_LIMIT
        ),
        cost_estimate=took(7),
        name="early_out",
    )(own, near, far)


def late_out_kernel(own_ref, near_ref, far_ref, qkv_ref, out_ref, small_ref):
    half, share, _ = near_ref.shape
    share -= 8
    own = own_ref[0]

    def fill(halves):
        for at in range(2 * half):
            rows = halves[at // half][(at % half) ^ (own % half)].astype(f32)
            row, part = at * share % WIDTH, at * share // WIDTH
            if part < 3:
                qkv_ref[row : row + share, part * WIDTH : (part + 1) * WIDTH] = rows[:share]
            else:
                out_ref[row : row + share] = rows[:share]
            if at < 2:
                small_ref[8 * at : 8 * at + 8] = rows[share:]

    @pl.when(own < half)
    def low():
        fill((near_ref, far_ref))

    @pl.when(own >= half)
    def high():
        fill((far_ref, near_ref))


def run_late_out(own, near, far):
    return pl.pallas_call(
        late_out_kernel,
        in_specs=[
            pl.BlockSpec(memory_space=pltpu.SMEM),
            pl.BlockSpec(memory_space=pltpu.VMEM),
            pl.BlockSpec(memory_space=pltpu.VMEM),
        ],
        out_shape=[
            jax.ShapeDtypeStruct((WIDTH, 3 * WIDTH), f32),
            jax.ShapeDtypeStruct((WIDTH, WIDTH), f32),
            jax.ShapeDtypeStruct((16, WIDTH), f32),
        ],
        compiler_params=pltpu.CompilerParams(vmem_limit_bytes=VMEM_LIMIT),
        cost_estimate=took(4),
        name="late_out",
    )(own, near, far)


def band_to_windows(band_values, win_count):
    trailing = band_values.shape[2:]
    blocks = band_values.reshape(
        (band_values.shape[0] // WIN_SIDE, WIN_SIDE, REG_SIDE, WIN_SIDE) + trailing
    )
    return jnp.swapaxes(blocks, 1, 2).reshape((win_count, WIN_SIDE * WIN_SIDE) + trailing)


def rank_of(keys):
    return jnp.sum(keys[None, :] < keys[:, None], axis=1)


def reduce_stages():
    img_bits = [("img", bit) for bit in range(lax.axis_size("img").bit_length() - 1)]
    dp_bits = [("dp", bit) for bit in range(lax.axis_size("dp").bit_length() - 1)]
    rest = img_bits[1:] + dp_bits
    return [img_bits[:1]] + [rest[at : at + 2] for at in range(0, len(rest), 2)]


def stage_masks(stage):
    img_size = lax.axis_size("img")
    return [(1 << bit) * (img_size if name == "dp" else 1) for name, bit in stage]


def stage_moves(stage):
    devices = lax.axis_size("dp") * lax.axis_size("img")
    moves = []
    for offset in range(1, 1 << len(stage)):
        flip = sum(mask for place, mask in enumerate(stage_masks(stage)) if offset >> place & 1)
        moves.append((offset, [(at, at ^ flip) for at in range(devices)]))
    return moves


def own_share(stages):
    flat = lax.axis_index("dp") * lax.axis_size("img") + lax.axis_index("img")
    share = 0
    for stage in stages:
        own = sum(((flat // mask) % 2) << place for place, mask in enumerate(stage_masks(stage)))
        share = (share << len(stage)) + own
    return share


def swap(rows, pairs):
    return lax.ppermute(rows, ("dp", "img"), pairs)


def add_up(pieces):
    return sum(piece.astype(f32) for piece in pieces).astype(bf16)


def sum_stage(rows, stage):
    parts = rows.reshape((1 << len(stage), -1) + rows.shape[1:])
    return add_up([parts[0]] + [swap(parts[offset], pairs) for offset, pairs in stage_moves(stage)])


def gather_stage(rows, stage):
    return jnp.concatenate([rows] + [swap(rows, pairs) for _, pairs in stage_moves(stage)], axis=0)


def sum_stages(rows, stages):
    for stage in stages:
        rows = sum_stage(rows, stage)
    return rows


def deal_kernel(pick_ref, region_ref, local_ref, out_ref):
    groups = out_ref.shape[0]
    for pair in range(out_ref.shape[1] // 16):
        head = region_ref[...] if pair == 0 else local_ref[2 * pair - 1]
        rows = jnp.concatenate([head, local_ref[2 * pair]], axis=0)
        out_ref[:, 16 * pair : 16 * pair + 16, :] = (
            dot(pick_ref[...], rows).astype(bf16).reshape(groups, 16, WIDTH)
        )


def collect_kernel(pick_ref, came_ref, region_ref, local_ref):
    slots = region_ref.shape[0]
    for pair in range(came_ref.shape[1] // 16):
        rows = came_ref[:, 16 * pair : 16 * pair + 16, :].reshape(2 * slots, WIDTH)
        rows = dot(pick_ref[...], rows).astype(bf16)
        if pair == 0:
            region_ref[...] = rows[:slots]
        else:
            local_ref[2 * pair - 1] = rows[:slots]
        local_ref[2 * pair] = rows[slots:]


def run_deal(pick, region, local):
    count = region.shape[0] // TILE
    return pl.pallas_call(
        deal_kernel,
        out_shape=jax.ShapeDtypeStruct((count, (local.shape[0] + 1) * TILE, WIDTH), bf16),
        compiler_params=pltpu.CompilerParams(vmem_limit_bytes=VMEM_LIMIT),
        cost_estimate=took(5),
        name="deal",
    )(pick, region, local)


def run_collect(pick, came):
    slots = came.shape[0] * TILE
    return pl.pallas_call(
        collect_kernel,
        out_shape=[
            jax.ShapeDtypeStruct((slots, WIDTH), bf16),
            jax.ShapeDtypeStruct((came.shape[1] // TILE - 1, slots, WIDTH), bf16),
        ],
        compiler_params=pltpu.CompilerParams(vmem_limit_bytes=VMEM_LIMIT),
        cost_estimate=took(5),
        name="collect",
    )(pick, came)


def swap_tiles(tiles_sent, devices):
    count, rows, width = tiles_sent.shape
    share = count * TILE // devices
    if share == TILE:
        return lax.all_to_all(tiles_sent, "dp", split_axis=0, concat_axis=0, tiled=True)
    places = rows // TILE
    sent = tiles_sent.reshape(count, places, TILE, width).transpose(1, 0, 2, 3)
    sent = sent.reshape(places, devices, share, width).transpose(1, 0, 2, 3)
    came = lax.all_to_all(sent, "dp", split_axis=0, concat_axis=0, tiled=True)
    came = came.transpose(1, 0, 2, 3).reshape(places, count, TILE, width)
    return came.transpose(1, 0, 2, 3).reshape(count, rows, width)


def row_maps():
    window = np.arange(TILE)[:, None]
    place = np.arange(WIN_SIDE * WIN_SIDE)[None, :]
    raster = place // WIN_SIDE * (TILE * WIN_SIDE) + window * WIN_SIDE + place % WIN_SIDE
    band = TILE * WIN_SIDE * WIN_SIDE
    spread = np.zeros((TILE * SLOT, band), np.float32)
    spread[window * SLOT + 1 + place, raster] = 1
    gather = np.zeros((band, TILE * SLOT), np.float32)
    gather[raster, window * SLOT + 1 + place] = 1
    head = np.zeros((TILE, TILE * SLOT), np.float32)
    head[np.arange(TILE), np.arange(TILE) * SLOT] = 1
    place = np.arange(WIN_SIDE * WIN_SIDE + 1)[None, :]
    squeeze = np.zeros(((WIN_SIDE * WIN_SIDE + 1) * TILE, TILE * TALL), np.float32)
    squeeze[place * TILE + window, window * TALL + place] = 1
    return [jnp.asarray(table, bf16) for table in (spread, gather, head, squeeze, squeeze.T)]


def shards(
    tokens,
    regional,
    pad_mask,
    keep_mask,
    window_slot,
    ln1_gain,
    ln1_bias,
    w_qkv,
    bias_q,
    bias_v,
    w_out,
    bias_out,
    ln2_gain,
    ln2_bias,
    w_fc1,
    bias_fc1,
    w_fc2,
    bias_fc2,
    cot_local,
    cot_regional,
):
    devices = lax.axis_size("dp")
    stages = reduce_stages()
    parts = devices * lax.axis_size("img")
    own_rank = lax.axis_index("dp")
    win_count = regional.shape[1]
    all_windows = window_slot.shape[1]
    slot_of = window_slot[0]
    places = jnp.arange(win_count)
    own_target = lax.dynamic_slice_in_dim(slot_of, own_rank * win_count, win_count) // win_count
    own_place = rank_of(own_target * win_count + places)
    order = jnp.sum(jnp.where(own_place[None, :] == places[:, None], places[None, :], 0), axis=1)
    slot_hit = slot_of[None, :] == (own_rank * win_count + places)[:, None]
    window_here = jnp.sum(jnp.where(slot_hit, jnp.arange(all_windows)[None, :], 0), axis=1)
    here_place = rank_of(window_here)
    deal_row = jnp.arange(2 * win_count)
    row_place = deal_row // (2 * TILE) * TILE + deal_row % TILE
    row_half = deal_row // TILE % 2
    column_hit = row_place[:, None] == jnp.concatenate([here_place, here_place])[None, :]
    pick = (column_hit & (row_half[:, None] == (deal_row // win_count)[None, :])).astype(bf16)
    pick_back = (column_hit & (row_half[:, None] == (deal_row // win_count)[None, :])).T.astype(bf16)
    cot = swap_tiles(
        run_deal(pick, cot_regional[0], jnp.swapaxes(cot_local[0], 0, 1)), devices
    )
    image = own_rank * win_count // REGIONS
    keep = lax.dynamic_slice_in_dim(keep_mask[0], image, 1).astype(f32) / survive
    live = band_to_windows(pad_mask[0], win_count) != 0
    allowed = jnp.concatenate(
        [jnp.ones((win_count, 1), bool), live, jnp.zeros((win_count, SLOT - 1 - live.shape[1]), bool)],
        axis=1,
    )
    window_bias = jnp.broadcast_to(
        jnp.where(allowed, 0.0, -1e30).astype(f32)[:, :, None], (win_count, SLOT, LANES)
    )
    region_bias = jnp.broadcast_to(
        jnp.where(live[:, 0], 0.0, -1e30).astype(f32)[:, None], (win_count, LANES)
    )
    spread, gather, head, squeeze, stretch = row_maps()
    plain, mixed_mask = head_masks()
    bias_qkv = jnp.concatenate([bias_q, jnp.zeros_like(bias_q), bias_v])[None]
    gain1, bias1, gain2, bias2 = ln1_gain[None], ln1_bias[None], ln2_gain[None], ln2_bias[None]
    out, qkv, probs, joined, mixed, after, hidden, slope, qkv_r, probs_r, mixed_r = run_forward(
        order, keep, tokens.reshape(REG_SIDE, -1, WIDTH), regional[0], window_bias, region_bias,
        spread, squeeze, plain, mixed_mask, gain1, bias1, w_qkv, bias_qkv, w_out, bias_out[None],
        gain2, bias2, w_fc1, bias_fc1[None], w_fc2, bias_fc2[None],
    )
    came = swap_tiles(out, devices)
    own = own_share(stages)[None]
    grad_after, grad_mixed, early, early_sent, grad_out, small, row_fc1 = run_back_mlp(
        parts, keep, own, cot, after, mixed, hidden, slope, stretch, gain2, bias2, w_fc1, w_fc2, w_out
    )
    (_, pairs), = stage_moves(stages[0])
    early_came = swap(early_sent, pairs)
    attention = (
        order, keep, own, qkv, probs, joined, grad_mixed, grad_after, plain, mixed_mask, head, gain1, bias1
    )
    grad_qkv, *held = run_back_attention(*attention)
    early = add_up([early, early_came])
    held, early, came = lax.optimization_barrier((held, early, came))
    early = sum_stage(early, stages[1])
    grad_qkv, late, late_sent, regional_out = run_back_attention(
        *attention,
        held=(*held, grad_qkv),
        ending=(grad_out, order[None], regional[0], qkv_r, probs_r, mixed_r, w_qkv, w_out, small, row_fc1),
        parts=parts,
    )
    late_came = swap(late_sent, pairs)
    grad_qkv, early = lax.optimization_barrier((grad_qkv, early))
    early = sum_stages(early, stages[2:])
    rows = (order, grad_qkv, joined, grad_after, gain1, w_qkv)
    windows = run_back_rows(*rows, 0, ROWS_FIRST)
    windows, early, late_came = lax.optimization_barrier((windows, early, late_came))
    late = sum_stage(add_up([late, late_came]), stages[1])
    for stage in reversed(stages[2:]):
        early = gather_stage(early, stage)
    windows = run_back_rows(*rows, ROWS_FIRST, win_count // TILE - ROWS_FIRST, held=windows)
    windows, early, late = lax.optimization_barrier((windows, early, late))
    late = sum_stages(late, stages[2:])
    moves = stage_moves(stages[1])
    direct = [swap(early, moves[at][1]) for at in (0, 1)]
    tokens_out = run_relay(gather, windows)
    tokens_out, came, late, early, direct = lax.optimization_barrier((tokens_out, came, late, early, direct))
    for stage in reversed(stages[2:]):
        late = gather_stage(late, stage)
    out_regional, out_local = run_collect(pick_back, came)
    early = jnp.concatenate([early] + direct + [swap(early, pairs) for _, pairs in moves[2:]], axis=0)
    out_local, early, late = lax.optimization_barrier((out_local, early, late))
    late = gather_stage(late, stages[1])
    early_far = swap(early, pairs)
    grad_w_fc1, grad_w_fc2 = run_early_out(own, early, early_far, w_fc1.shape[1])
    grad_w_fc1, grad_w_fc2, late = lax.optimization_barrier((grad_w_fc1, grad_w_fc2, late))
    late_far = swap(late, pairs)
    grad_w_qkv, grad_w_out, vectors = run_late_out(own, late, late_far)
    return (
        jnp.swapaxes(out_local, 0, 1)[None],
        out_regional[None],
        tokens_out.reshape(tokens.shape),
        regional_out[None],
        vectors[0],
        vectors[1],
        grad_w_qkv,
        vectors[2],
        vectors[3],
        grad_w_out,
        vectors[4],
        vectors[5],
        vectors[6],
        grad_w_fc1,
        vectors[8:12].reshape(-1),
        grad_w_fc2,
        vectors[7],
    )


def solution(mesh):
    in_specs = (
        P("img", "dp", None, None),
        P("img", "dp", None),
        P("img", "dp", None),
        P("img", None),
        P("img", None),
        P(),
        P(),
        P(),
        P(),
        P(),
        P(),
        P(),
        P(),
        P(),
        P(),
        P(),
        P(),
        P(),
        P("img", "dp", None, None),
        P("img", "dp", None),
    )
    out_specs = (
        P("img", "dp", None, None),
        P("img", "dp", None),
        P("img", "dp", None, None),
        P("img", "dp", None),
        P(),
        P(),
        P(),
        P(),
        P(),
        P(),
        P(),
        P(),
        P(),
        P(),
        P(),
        P(),
        P(),
    )
    return jax.shard_map(shards, mesh=mesh, in_specs=in_specs, out_specs=out_specs, check_vma=False)
```

```python
import functools
import math
import jax
import jax.numpy as jnp
import numpy as np
from jax import lax
from jax.experimental import pallas as pl
from jax.experimental.pallas import tpu as pltpu
from jax.sharding import PartitionSpec as P

HEADS = 16
HDIM = 32
WIN_SIDE = 7
REG_SIDE = 8
REGIONS = 64

norm_eps = 1e-05
survive = 0.9

WIDTH = 512
SLOT = 64
TALL = 56
TILE = 8
GROUP = 4
GROUPS = HEADS // GROUP
TOGETHER = 8
LANES = 128
ROWS_FIRST = 2
FIRST_TILES = 3
ONES = 16
CHUNK = 512
VMEM_LIMIT = 60 * 1024 * 1024

f32 = jnp.float32


def took(micros):
    return pl.CostEstimate(flops=int(micros * 1.15e9), bytes_accessed=1_000_000, transcendentals=0)

bf16 = jnp.bfloat16


def dot(left, right):
    return lax.dot_general(left, right, (((1,), (0,)), ((), ())), preferred_element_type=f32)


def dot_nt(left, right):
    return lax.dot_general(left, right, (((1,), (1,)), ((), ())), preferred_element_type=f32)


def head_masks():
    lane_head = np.arange(LANES) // HDIM
    plain = np.repeat(np.arange(GROUP), SLOT)
    mixed = np.repeat(np.array([0, 2, 1, 3]), SLOT)
    return (
        jnp.asarray(plain[:, None] == lane_head[None, :], bf16),
        jnp.asarray(mixed[:, None] == lane_head[None, :], bf16),
    )


def spread_heads(rows, mask):
    return jnp.concatenate([rows] * GROUP, axis=0) * mask


def turn(blocks):
    stacked = jnp.concatenate([blocks[:, :LANES], blocks[:, LANES:]], axis=0)
    turned = stacked.T
    return jnp.concatenate([turned[:SLOT], turned[SLOT:]], axis=1)


def attend_scores(items, plain):
    return [dot_nt(key_rows, spread_heads(queries, plain)) for queries, key_rows, _, _ in items]


def attend_probs(items, scores):
    probs = []
    for rows, (_, _, _, bias) in zip(scores, items):
        rows = rows + bias
        highest = jnp.max(rows, axis=0, keepdims=True)
        weighted = jnp.exp2((rows - highest) * (HDIM**-0.5 * math.log2(math.e)))
        total = jnp.sum(weighted, axis=0, keepdims=True)
        probs.append((weighted * (1.0 / total)).astype(bf16))
    return probs


def attend_mix(items, turned, mixed):
    return [dot(rows, spread_heads(item[2], mixed)) for rows, item in zip(turned, items)]


def attend_back(items, plain, mixed):
    wide = [spread_heads(item[4], plain) for item in items]
    grad_probs = [dot_nt(item[2], rows) for item, rows in zip(items, wide)]
    grad_values = [dot(item[3], rows) for item, rows in zip(items, wide)]
    scores = []
    for rows, item in zip(grad_probs, items):
        soft = item[3].astype(f32)
        weighted = soft * rows
        inner = jnp.sum(weighted, axis=0, keepdims=True)
        scores.append((weighted - soft * inner).astype(bf16))
    turned = [turn(rows) for rows in scores]
    factor = HDIM**-0.5
    grad_keys = [dot(rows, spread_heads(item[0], plain)) * factor for rows, item in zip(scores, items)]
    grad_queries = [dot(rows, spread_heads(item[1], mixed)) * factor for rows, item in zip(turned, items)]
    return list(zip(grad_queries, grad_keys, grad_values))


def normalize(rows):
    centered = rows - jnp.mean(rows, axis=-1, keepdims=True)
    spread = jnp.mean(centered * centered, axis=-1, keepdims=True)
    scale = lax.rsqrt(spread + norm_eps)
    return centered * scale, scale


def normalize_back(grad_unit, unit, scale):
    first = jnp.mean(grad_unit, axis=-1, keepdims=True)
    second = jnp.mean(grad_unit * unit, axis=-1, keepdims=True)
    return scale * (grad_unit - first - unit * second)


def gelu_pair(values):
    below = 0.5 + 0.5 * lax.erf(values * 0.7071067811865476)
    bell = jnp.exp2(values * values * (-0.5 * math.log2(math.e)))
    return values * below, below + values * bell * 0.3989422804014327


def fold_lanes(rows):
    return sum(rows[:, at : at + LANES] for at in range(0, rows.shape[1], LANES))


def column_sum(rows):
    return jnp.sum(rows, axis=0, keepdims=True)


def window_items(qkv_of, bias):
    wide = jnp.concatenate([bias, bias], axis=1).astype(f32)
    return [
        (qkv_of(group), qkv_of(GROUPS + group), qkv_of(2 * GROUPS + group), wide) for group in range(GROUPS)
    ]


def attend_windows_back(windows, plain, mixed):
    items = []
    for qkv_of, probs_of, grad_of, _ in windows:
        for group in range(GROUPS):
            probs = jnp.concatenate([probs_of(2 * group), probs_of(2 * group + 1)], axis=1)
            items.append(
                (qkv_of(group), qkv_of(GROUPS + group), qkv_of(2 * GROUPS + group), probs, grad_of(group))
            )
    grads = attend_back(items, plain, mixed)
    for at, (_, _, _, put_grad) in enumerate(windows):
        for group in range(GROUPS):
            for part in range(3):
                put_grad(part * GROUPS + group, grads[at * GROUPS + group][part].astype(bf16))


def forward_kernel(
    order_ref, keep_ref,
    tokens_ref, regional_ref, window_bias_ref, region_bias_ref, spread_ref, squeeze_ref,
    plain_ref, mixed_mask_ref, gain1_ref, bias1_ref, w_qkv_ref, bias_q_ref, bias_v_ref, w_out_ref, bias_out_ref,
    gain2_ref, bias2_ref, w_fc1_ref, bias_fc1_ref, w_fc2_ref, bias_fc2_ref,
    out_ref, qkv_ref, probs_ref, joined_ref, mixed_ref, after_ref, hidden_ref, slope_ref,
    qkv_r_ref, probs_r_ref, mixed_r_ref,
    windows, normed, mixed_rows, joined_rows,
):
    step = pl.program_id(0)
    last = pl.num_programs(0) - 1
    keep = keep_ref[0]
    plain = plain_ref[...]
    mixed = mixed_mask_ref[...]
    count = TILE * TALL
    chunks = [slice(at, at + CHUNK) for at in range(0, w_fc1_ref.shape[1], CHUNK)]
    tile = {}

    @pl.when(step == 0)
    def first():
        region = regional_ref[...].astype(f32)
        unit, _ = normalize(region)
        region_norm = (unit * gain1_ref[...] + bias1_ref[...]).astype(bf16)
        region_qkv = dot(region_norm, w_qkv_ref[...])
        region_qkv = jnp.concatenate(
            [
                region_qkv[:, :WIDTH] + bias_q_ref[...],
                region_qkv[:, WIDTH : 2 * WIDTH],
                region_qkv[:, 2 * WIDTH :] + bias_v_ref[...],
            ],
            axis=1,
        ).astype(bf16)
        for at in range(3 * GROUPS):
            qkv_r_ref[at] = region_qkv[:, at * LANES : (at + 1) * LANES]
        items = window_items(lambda at: region_qkv[:, at * LANES : (at + 1) * LANES], region_bias_ref[...])
        probs = attend_probs(items, attend_scores(items, plain))
        for group in range(GROUPS):
            probs_r_ref[2 * group] = probs[group][:, :LANES]
            probs_r_ref[2 * group + 1] = probs[group][:, LANES:]
        outs = attend_mix(items, [turn(rows) for rows in probs], mixed)
        region_mixed = jnp.concatenate(outs, axis=1).astype(bf16)
        mixed_r_ref[...] = region_mixed
        region_mid = region + keep * (dot(region_mixed, w_out_ref[...]) + bias_out_ref[...])
        region_mid = region_mid.astype(bf16)
        row = lax.broadcasted_iota(jnp.int32, (TILE * SLOT, REGIONS), 0)
        column = lax.broadcasted_iota(jnp.int32, (TILE * SLOT, REGIONS), 1)

        def relay(line, carry):
            pick = (row == (column - line * TILE) * SLOT).astype(bf16)
            rows = dot(spread_ref[...], tokens_ref[line]) + dot(pick, region_mid)
            windows[pl.ds(line * TILE, TILE)] = rows.reshape(TILE, SLOT, WIDTH)
            return carry

        lax.fori_loop(0, REG_SIDE, relay, 0)


    def norm_rows():
        for at in range(TILE):
            rows = windows[order_ref[step * TILE + at]]
            joined_ref[at] = rows.astype(bf16)
            unit, _ = normalize(rows)
            normed[at * SLOT : (at + 1) * SLOT] = (unit * gain1_ref[...] + bias1_ref[...]).astype(bf16)

    def project(part):
        cols = slice(part * WIDTH, (part + 1) * WIDTH)
        qkv = dot(normed[...], w_qkv_ref[:, cols])
        if part != 1:
            qkv = qkv + (bias_q_ref if part == 0 else bias_v_ref)[...]
        qkv = qkv.astype(bf16).reshape(TILE, SLOT, WIDTH)
        for group in range(GROUPS):
            qkv_ref[:, part * GROUPS + group] = qkv[:, :, group * LANES : (group + 1) * LANES]

    def score(half):
        items = []
        for at in half:
            bias = window_bias_ref[order_ref[step * TILE + at]]
            items += window_items(lambda place, at=at: qkv_ref[at, place], bias)
        return items, attend_scores(items, plain)

    def soften(half, items, scores):
        probs = attend_probs(items, scores)
        for at, rows in enumerate(probs):
            window, group = half[at // GROUPS], at % GROUPS
            probs_ref[window, 2 * group] = rows[:, :LANES]
            probs_ref[window, 2 * group + 1] = rows[:, LANES:]
        return [turn(rows) for rows in probs]

    def mix(half, items, turned):
        outs = attend_mix(items, turned, mixed)
        for at, rows in enumerate(outs):
            window, group = half[at // GROUPS], at % GROUPS
            mixed_rows[window, :, group * LANES : (group + 1) * LANES] = rows

    def keep_joined():
        for at in range(TILE):
            joined_rows[at] = joined_ref[at].astype(f32)


    def branch():
        mixed_low = mixed_rows[:, :TALL].reshape(count, WIDTH).astype(bf16)
        mixed_ref[...] = mixed_low
        after = joined_rows[:, :TALL].reshape(count, WIDTH) + keep * (
            dot(mixed_low, w_out_ref[...]) + bias_out_ref[...]
        )
        after_ref[...] = after

    def norm_after():
        unit, _ = normalize(after_ref[...])
        tile["norm"] = (unit * gain2_ref[...] + bias2_ref[...]).astype(bf16)
        tile["total"] = jnp.zeros((count, WIDTH), f32)

    def widen(at):
        tile[at] = dot(tile["norm"], w_fc1_ref[:, chunks[at]])

    def bend(at):
        cols = chunks[at]
        hidden, slope = gelu_pair(tile[at] + bias_fc1_ref[:, cols])
        tile[at] = hidden.astype(bf16)
        hidden_ref[:, cols] = tile[at]
        slope_ref[:, cols] = slope.astype(bf16)

    def narrow(at):
        tile["total"] = tile["total"] + dot(tile[at], w_fc2_ref[chunks[at], :])

    def send():
        result = after_ref[...] + keep * (tile["total"] + bias_fc2_ref[...])
        out_ref[0] = dot(squeeze_ref[...], result.astype(bf16)).astype(bf16)

    halves = [list(range(TILE // 2)), list(range(TILE // 2, TILE))]

    @pl.when(step == 0)
    def attention_only():
        norm_rows()
        for part in range(3):
            project(part)
        scored = [score(half) for half in halves]
        turned = [soften(half, *pair) for half, pair in zip(halves, scored)]
        for half, pair, rows in zip(halves, scored, turned):
            mix(half, pair[0], rows)
        keep_joined()

    @pl.when((step > 0) & (step < last))
    def both():
        branch()
        norm_rows()
        project(0)
        norm_after()
        project(1)
        widen(0)
        project(2)
        widen(1)
        bend(0)
        scored = [score(halves[0]), None]
        narrow(0)
        bend(1)
        widen(2)
        scored[1] = score(halves[1])
        turned = [soften(halves[0], *scored[0]), None]
        narrow(1)
        widen(3)
        bend(2)
        mix(halves[0], scored[0][0], turned[0])
        turned[1] = soften(halves[1], *scored[1])
        narrow(2)
        bend(3)
        mix(halves[1], scored[1][0], turned[1])
        narrow(3)
        send()
        keep_joined()

    @pl.when(step == last)
    def feed_only():
        branch()
        norm_after()
        widen(0)
        for at in range(len(chunks)):
            if at + 1 < len(chunks):
                widen(at + 1)
            bend(at)
            narrow(at)
        send()


def whole(shape):
    return pl.BlockSpec(shape, lambda step, *_: (0,) * len(shape))


def tiles(shape):
    return pl.BlockSpec(shape, lambda step, *_: (step,) + (0,) * (len(shape) - 1))


def run_forward(order, keep, tokens, regional, window_bias, region_bias, spread, squeeze, plain, mixed,
                gain1, bias1, w_qkv, bias_q, bias_v, w_out, bias_out, gain2, bias2, w_fc1, bias_fc1, w_fc2, bias_fc2):
    windows = regional.shape[0]
    steps = windows // TILE
    rows = TILE * TALL
    hidden = w_fc1.shape[1]
    compact = squeeze.shape[0]
    args = (tokens, regional, window_bias, region_bias, spread, squeeze, plain, mixed,
            gain1, bias1, w_qkv, bias_q, bias_v, w_out, bias_out, gain2, bias2, w_fc1, bias_fc1, w_fc2, bias_fc2)
    def ahead(shape):
        return pl.BlockSpec(
            shape, lambda step, *_: (jnp.minimum(step, steps - 1),) + (0,) * (len(shape) - 1)
        )

    def behind(shape):
        return pl.BlockSpec(shape, lambda step, *_: (jnp.maximum(step - 1, 0),) + (0,) * (len(shape) - 1))

    outs = [
        ((steps, compact, WIDTH), bf16, behind((1, compact, WIDTH))),
        ((windows, 3 * GROUPS, SLOT, LANES), bf16, ahead((TILE, 3 * GROUPS, SLOT, LANES))),
        ((windows, 2 * GROUPS, SLOT, LANES), bf16, ahead((TILE, 2 * GROUPS, SLOT, LANES))),
        ((windows, SLOT, WIDTH), bf16, ahead((TILE, SLOT, WIDTH))),
        ((steps * rows, WIDTH), bf16, behind((rows, WIDTH))),
        ((steps * rows, WIDTH), f32, behind((rows, WIDTH))),
        ((steps * rows, hidden), bf16, behind((rows, hidden))),
        ((steps * rows, hidden), bf16, behind((rows, hidden))),
    ]
    fixed = [
        ((3 * GROUPS, REGIONS, LANES), bf16),
        ((2 * GROUPS, REGIONS, LANES), bf16),
        ((REGIONS, WIDTH), bf16),
    ]
    return pl.pallas_call(
        forward_kernel,
        grid_spec=pltpu.PrefetchScalarGridSpec(
            num_scalar_prefetch=2,
            grid=(steps + 1,),
            in_specs=[whole(a.shape) for a in args],
            out_specs=[spec for _, _, spec in outs] + [whole(s) for s, _ in fixed],
            scratch_shapes=[
                pltpu.VMEM((windows, SLOT, WIDTH), f32),
                pltpu.VMEM((TILE * SLOT, WIDTH), bf16),
                pltpu.VMEM((TILE, SLOT, WIDTH), f32),
                pltpu.VMEM((TILE, SLOT, WIDTH), f32),
            ],
        ),
        out_shape=[jax.ShapeDtypeStruct(s, d) for s, d, _ in outs]
        + [jax.ShapeDtypeStruct(s, d) for s, d in fixed],
        compiler_params=pltpu.CompilerParams(
            dimension_semantics=("arbitrary",), vmem_limit_bytes=VMEM_LIMIT
        ),
        cost_estimate=took(61),
        name="forward",
    )(order, keep, *args)


def put_shares(own, keep_ref, send_ref, chunk_of):
    half = keep_ref.shape[0]

    def fill(refs):
        for which, ref in enumerate(refs):
            for at in range(half):
                ref[at ^ (own % half)] = chunk_of(which * half + at)

    @pl.when(own < half)
    def low():
        fill((keep_ref, send_ref))

    @pl.when(own >= half)
    def high():
        fill((send_ref, keep_ref))


def back_mlp_kernel(
    keep_ref, own_ref, cot_ref, after_ref, mixed_ref, hidden_ref, slope_ref, stretch_ref,
    gain2_ref, bias2_ref, w_fc1_ref, w_fc2_ref, w_out_ref,
    grad_after_ref, grad_mixed_ref, stay_ref, send_ref, grad_out_ref, small_ref, bias_row_ref,
    sum_fc1, sum_fc2, sum_out, sums, sum_hidden, early_rows,
):
    step = pl.program_id(0)
    last = pl.num_programs(0) - 1
    keep = keep_ref[0]

    @pl.when(step == 0)
    def clear():
        for ref in (sum_fc1, sum_fc2, sum_out, sums, sum_hidden):
            ref[...] = jnp.zeros_like(ref)

    unit, scale = normalize(after_ref[...])
    mlp_norm = (unit * gain2_ref[...] + bias2_ref[...]).astype(bf16)
    norm_turned = mlp_norm.T
    cot = dot(stretch_ref[...], cot_ref[0])
    grad_mlp = (keep * cot).astype(bf16)
    grad_turned = grad_mlp.T
    sums[0:1] += column_sum(grad_mlp.astype(f32))
    grad_norm = jnp.zeros(after_ref.shape, f32)
    chunks = [slice(at, at + CHUNK) for at in range(0, w_fc1_ref.shape[1], CHUNK)]
    ahead = dot_nt(grad_mlp, w_fc2_ref[chunks[0], :])
    for at, cols in enumerate(chunks):
        grad_hidden = ahead
        if at + 1 < len(chunks):
            ahead = dot_nt(grad_mlp, w_fc2_ref[chunks[at + 1], :])
        sum_fc2[:, cols] += dot(grad_turned, hidden_ref[:, cols])
        grad_pre = (slope_ref[:, cols].astype(f32) * grad_hidden).astype(bf16)
        sum_fc1[:, cols] += dot(norm_turned, grad_pre)
        sum_hidden[0:1, cols] += column_sum(grad_pre.astype(f32))
        grad_norm = grad_norm + dot_nt(grad_pre, w_fc1_ref[:, cols])
    sums[1:2] += column_sum(grad_norm * unit)
    sums[2:3] += column_sum(grad_norm)
    grad_after = cot + normalize_back(grad_norm * gain2_ref[...], unit, scale)
    grad_after_ref[...] = grad_after
    grad_branch = (keep * grad_after).astype(bf16)
    sums[3:4] += column_sum(grad_branch.astype(f32))
    sum_out[...] += dot(mixed_ref[...].T, grad_branch)
    grad_mixed = dot_nt(grad_branch, w_out_ref[...]).reshape(TILE, TALL, WIDTH)
    empty = jnp.zeros((TILE, SLOT - TALL, WIDTH), f32)
    grad_mixed = jnp.concatenate([grad_mixed, empty], axis=1).astype(bf16)
    for group in range(GROUPS):
        grad_mixed_ref[:, group] = grad_mixed[:, :, group * LANES : (group + 1) * LANES]

    @pl.when(step == last)
    def finish():
        for at in range(4):
            cols = slice(at * WIDTH, (at + 1) * WIDTH)
            early_rows[cols, :] = sum_fc1[:, cols].astype(bf16)
            early_rows[4 * WIDTH + at * WIDTH : 4 * WIDTH + (at + 1) * WIDTH, :] = (
                sum_fc2[:, cols].T.astype(bf16)
            )
        rows = stay_ref.shape[1]
        put_shares(
            own_ref[0], stay_ref, send_ref, lambda at: early_rows[at * rows : (at + 1) * rows, :]
        )
        grad_out_ref[...] = sum_out[...]
        small_ref[...] = sums[...]
        bias_row_ref[...] = sum_hidden[...]


def run_back_mlp(parts, keep, own, cot, after, mixed, hidden, slope, stretch, gain2, bias2, w_fc1, w_fc2, w_out):
    steps, compact, _ = cot.shape
    rows = TILE * TALL
    units = w_fc1.shape[1]
    tiled = [(1, compact, WIDTH), (rows, WIDTH), (rows, WIDTH), (rows, units), (rows, units)]
    fixed = (stretch, gain2, bias2, w_fc1, w_fc2, w_out)
    outs = [
        ((steps * rows, WIDTH), f32, (rows, WIDTH)),
        ((steps * TILE, GROUPS, SLOT, LANES), bf16, (TILE, GROUPS, SLOT, LANES)),
    ]
    share = (parts // 2, 2 * units // parts, WIDTH)
    whole_outs = [(share, bf16), (share, bf16), ((WIDTH, WIDTH), f32), ((8, WIDTH), f32), ((8, units), f32)]
    return pl.pallas_call(
        back_mlp_kernel,
        grid_spec=pltpu.PrefetchScalarGridSpec(
            num_scalar_prefetch=2,
            grid=(steps,),
            in_specs=[tiles(b) for b in tiled] + [whole(a.shape) for a in fixed],
            out_specs=[tiles(block) for _, _, block in outs] + [whole(s) for s, _ in whole_outs],
            scratch_shapes=[
                pltpu.VMEM((WIDTH, units), f32),
                pltpu.VMEM((WIDTH, units), f32),
                pltpu.VMEM((WIDTH, WIDTH), f32),
                pltpu.VMEM((8, WIDTH), f32),
                pltpu.VMEM((8, units), f32),
                pltpu.VMEM((2 * units, WIDTH), bf16),
            ],
        ),
        out_shape=[jax.ShapeDtypeStruct(s, d) for s, d, _ in outs]
        + [jax.ShapeDtypeStruct(s, d) for s, d in whole_outs],
        compiler_params=pltpu.CompilerParams(
            dimension_semantics=("arbitrary",), vmem_limit_bytes=VMEM_LIMIT
        ),
        cost_estimate=took(55),
        name="back_mlp",
    )(keep, own, cot, after, mixed, hidden, slope, *fixed)


def back_attention_kernel(
    first, last, order_ref, keep_ref, own_ref,
    qkv_ref, probs_ref, joined_ref, grad_mixed_ref, grad_after_ref,
    plain_ref, mixed_mask_ref, gain1_ref, bias1_ref, *refs,
):
    if first:
        held_in = ()
    else:
        held_in, refs = refs[:3], refs[4:]
    if last:
        ending, refs = refs[:10], refs[10:]
        grad_out_ref, order_row_ref, regional_ref, qkv_r_ref, probs_r_ref, mixed_r_ref = ending[:6]
        w_qkv_ref, w_out_ref, sums_mlp_ref, row_fc1_ref = ending[6:]
        grad_qkv_ref, stay_ref, send_ref, regional_out_ref, sum_qkv, heads, after_heads, late_rows = refs
    else:
        grad_qkv_ref, sum_qkv, heads, after_heads = refs
    step = pl.program_id(0)
    plain = plain_ref[...]
    mixed = mixed_mask_ref[...]

    @pl.when(step == 0)
    def begin():
        for at, ref in enumerate((sum_qkv, heads, after_heads)):
            ref[...] = jnp.zeros_like(ref) if first else held_in[at][...]

    def some(batch, carry):
        def window(at):
            rows = pl.ds(pl.multiple_of(at * SLOT, SLOT), SLOT)

            def put_grad(place, values):
                grad_qkv_ref[rows, place * LANES : (place + 1) * LANES] = values

            return (
                lambda place: qkv_ref[at, place],
                lambda place: probs_ref[at, place],
                lambda place: grad_mixed_ref[at, place],
                put_grad,
            )

        attend_windows_back([window(batch * TOGETHER + at) for at in range(TOGETHER)], plain, mixed)
        return carry

    lax.fori_loop(0, TILE // TOGETHER, some, 0)
    joined = joined_ref[...].reshape(TILE * SLOT, WIDTH).astype(f32)
    unit, _ = normalize(joined)
    normed = (unit * gain1_ref[...] + bias1_ref[...]).astype(bf16)
    turned = jnp.concatenate([normed.T, jnp.ones((ONES, TILE * SLOT), bf16)], axis=0)
    sum_qkv[...] += dot(turned, grad_qkv_ref[...])
    rows = pl.ds(pl.multiple_of((step + (0 if first else FIRST_TILES)) * TILE, TILE), TILE)
    heads[rows, : 3 * WIDTH] = jnp.concatenate(
        [grad_qkv_ref[at * SLOT : at * SLOT + 16].astype(f32)[:1] for at in range(TILE)], axis=0
    )
    heads[rows, 3 * WIDTH :] = jnp.concatenate([joined_ref[at, :16].astype(f32)[:1] for at in range(TILE)], axis=0)
    after_heads[rows] = jnp.concatenate(
        [grad_after_ref[at * TALL : at * TALL + 1] for at in range(TILE)], axis=0
    )
    if not last:
        return

    @pl.when(step == pl.num_programs(0) - 1)
    def finish():
        keep = keep_ref[0]
        gain1 = gain1_ref[...]
        grad_normed = dot_nt(heads[:, : 3 * WIDTH].astype(bf16), w_qkv_ref[...])
        unit, scale = normalize(heads[:, 3 * WIDTH :])
        grad_mid = after_heads[...] + normalize_back(grad_normed * gain1, unit, scale)
        windows = grad_mid.shape[0]
        raster = lax.broadcasted_iota(jnp.int32, (windows, windows), 0)
        came = dot((raster == order_row_ref[...]).astype(bf16), grad_mid.astype(bf16))
        grad_branch = (keep * came).astype(bf16)
        grad_mixed = dot_nt(grad_branch, w_out_ref[...]).astype(bf16)
        parts = {}
        attend_windows_back(
            [
                (
                    lambda place: qkv_r_ref[place],
                    lambda place: probs_r_ref[place],
                    lambda place: grad_mixed[:, place * LANES : (place + 1) * LANES],
                    parts.__setitem__,
                )
            ],
            plain,
            mixed,
        )
        grad_qkv_r = jnp.concatenate([parts[place] for place in range(3 * GROUPS)], axis=1)
        unit_r, scale_r = normalize(regional_ref[...].astype(f32))
        normed_r = (unit_r * gain1 + bias1_ref[...]).astype(bf16)
        total = sum_qkv[:WIDTH] + dot(normed_r.T, grad_qkv_r)
        columns = sum_qkv[WIDTH : WIDTH + 1] + column_sum(grad_qkv_r.astype(f32))
        for part in range(3):
            cols = slice(part * WIDTH, (part + 1) * WIDTH)
            late_rows[cols, :] = total[:, cols].astype(bf16)
        late_rows[3 * WIDTH :, :] = (
            grad_out_ref[...] + dot(mixed_r_ref[...].T, grad_branch)
        ).astype(bf16)
        weights = w_qkv_ref[...].astype(f32)
        by_bias = weights * columns
        by_gain = weights * total
        turned_bias = fold_lanes(by_bias).T
        turned_gain = fold_lanes(by_gain).T
        grad_bias1 = column_sum(turned_bias)
        grad_gain1 = (column_sum(turned_gain) - bias1_ref[...] * grad_bias1) / gain1
        small = [
            grad_gain1,
            grad_bias1,
            columns[:, :WIDTH],
            columns[:, 2 * WIDTH :],
            sums_mlp_ref[3:4] + column_sum(grad_branch.astype(f32)),
            sums_mlp_ref[1:2],
            sums_mlp_ref[2:3],
            sums_mlp_ref[0:1],
        ]
        units = row_fc1_ref.shape[1] // WIDTH
        more = [row_fc1_ref[0:1, at * WIDTH : (at + 1) * WIDTH] for at in range(units)]
        more.append(jnp.zeros((8 - units, WIDTH), f32))
        share = stay_ref.shape[1] - 8

        def chunk_of(part):
            extra = jnp.zeros((8, WIDTH), f32)
            if part < 2:
                extra = jnp.concatenate(more if part else small, axis=0)
            rows = late_rows[part * share : (part + 1) * share]
            return jnp.concatenate([rows, extra.astype(bf16)], axis=0)

        put_shares(own_ref[0], stay_ref, send_ref, chunk_of)
        grad_normed_r = dot_nt(grad_qkv_r, w_qkv_ref[...])
        regional_out_ref[...] = (
            came + normalize_back(grad_normed_r * gain1, unit_r, scale_r)
        ).astype(bf16)


def run_back_attention(order, keep, own, qkv, probs, joined, grad_mixed, grad_after, plain, mixed, gain1, bias1,
                       held=None, ending=None, parts=1):
    windows = qkv.shape[0]
    steps = windows // TILE
    rows = TILE * TALL
    begin = 0 if held is None else FIRST_TILES
    count = FIRST_TILES if held is None else steps - FIRST_TILES

    def tile(shape):
        return pl.BlockSpec(shape, lambda step, *_: (step + begin,) + (0,) * (len(shape) - 1))

    tiled = [
        (TILE, 3 * GROUPS, SLOT, LANES),
        (TILE, 2 * GROUPS, SLOT, LANES),
        (TILE, SLOT, WIDTH),
        (TILE, GROUPS, SLOT, LANES),
        (rows, WIDTH),
    ]
    fixed = [plain, mixed, gain1, bias1]
    in_specs = [tile(b) for b in tiled] + [whole(a.shape) for a in fixed]
    args = [qkv, probs, joined, grad_mixed, grad_after] + fixed
    aliases = {}
    if held is not None:
        in_specs += [whole(a.shape) for a in held[:3]] + [pl.BlockSpec(memory_space=pl.ANY)]
        args += list(held)
        aliases = {3 + len(args) - 1: 0}
    if ending is not None:
        in_specs += [whole(a.shape) for a in ending]
        args += list(ending)
    held_shapes = [(WIDTH + ONES, 3 * WIDTH), (windows, 4 * WIDTH), (windows, WIDTH)]
    outs = [((steps * TILE * SLOT, 3 * WIDTH), bf16, tile((TILE * SLOT, 3 * WIDTH)))]
    scratch = []
    late_shape = (parts // 2, 4 * WIDTH // parts + 8, WIDTH)
    if ending is None:
        outs += [(s, f32, whole(s)) for s in held_shapes]
    else:
        outs += [
            (late_shape, bf16, whole(late_shape)),
            (late_shape, bf16, whole(late_shape)),
            ((windows, WIDTH), bf16, whole((windows, WIDTH))),
        ]
        scratch = [pltpu.VMEM(s, f32) for s in held_shapes] + [pltpu.VMEM((4 * WIDTH, WIDTH), bf16)]
    return pl.pallas_call(
        functools.partial(back_attention_kernel, held is None, ending is not None),
        grid_spec=pltpu.PrefetchScalarGridSpec(
            num_scalar_prefetch=3,
            grid=(count,),
            in_specs=in_specs,
            out_specs=[spec for _, _, spec in outs],
            scratch_shapes=scratch,
        ),
        out_shape=[jax.ShapeDtypeStruct(s, d) for s, d, _ in outs],
        input_output_aliases=aliases,
        compiler_params=pltpu.CompilerParams(
            dimension_semantics=("arbitrary",), vmem_limit_bytes=VMEM_LIMIT
        ),
        cost_estimate=took(5 * count),
        name="back_attention",
    )(order, keep, own, *args)


def back_rows_kernel(begin, order_ref, grad_qkv_ref, joined_ref, grad_after_ref, gain1_ref, w_qkv_ref, *refs):
    windows_ref, rows_low, done = refs[-3:]
    step = pl.program_id(0)

    def copies(at_step):
        places = [order_ref[(begin + at_step) * TILE + at] for at in range(TILE)]
        return [
            pltpu.make_async_copy(rows_low.at[at], windows_ref.at[place], done.at[at])
            for at, place in enumerate(places)
        ]

    unit, scale = normalize(joined_ref[...].astype(f32).reshape(TILE * SLOT, WIDTH))
    grad_normed = dot_nt(grad_qkv_ref[...], w_qkv_ref[...])
    grad_in = normalize_back(grad_normed * gain1_ref[...], unit, scale)

    @pl.when(step > 0)
    def drain():
        for copy in copies(step - 1):
            copy.wait()

    empty = jnp.zeros((SLOT - TALL, WIDTH), f32)
    for at in range(TILE):
        rows = grad_in[at * SLOT : at * SLOT + TALL] + grad_after_ref[at * TALL : (at + 1) * TALL]
        rows_low[at] = jnp.concatenate([rows, empty], axis=0).astype(bf16)
    for copy in copies(step):
        copy.start()

    @pl.when(step == pl.num_programs(0) - 1)
    def finish():
        for copy in copies(step):
            copy.wait()


def run_back_rows(order, grad_qkv, joined, grad_after, gain1, w_qkv, begin, count, held=None):
    windows = joined.shape[0]

    def tile(shape):
        return pl.BlockSpec(shape, lambda step, *_: (step + begin,) + (0,) * (len(shape) - 1))

    tiled = [(TILE * SLOT, 3 * WIDTH), (TILE, SLOT, WIDTH), (TILE * TALL, WIDTH)]
    fixed = [gain1, w_qkv]
    in_specs = [tile(b) for b in tiled] + [whole(a.shape) for a in fixed]
    args = [grad_qkv, joined, grad_after] + fixed
    aliases = {}
    if held is not None:
        in_specs.append(pl.BlockSpec(memory_space=pl.ANY))
        args.append(held)
        aliases = {len(args): 0}
    return pl.pallas_call(
        functools.partial(back_rows_kernel, begin),
        grid_spec=pltpu.PrefetchScalarGridSpec(
            num_scalar_prefetch=1,
            grid=(count,),
            in_specs=in_specs,
            out_specs=pl.BlockSpec(memory_space=pl.ANY),
            scratch_shapes=[pltpu.VMEM((TILE, SLOT, WIDTH), bf16), pltpu.SemaphoreType.DMA((TILE,))],
        ),
        out_shape=jax.ShapeDtypeStruct((windows, SLOT, WIDTH), bf16),
        input_output_aliases=aliases,
        compiler_params=pltpu.CompilerParams(
            dimension_semantics=("arbitrary",), vmem_limit_bytes=VMEM_LIMIT
        ),
        cost_estimate=took(2.5 * count),
        name="back_rows",
    )(order, *args)


def relay_kernel(gather_ref, windows_ref, tokens_out_ref):
    for line in range(tokens_out_ref.shape[0]):
        rows = windows_ref[line * TILE : (line + 1) * TILE].reshape(TILE * SLOT, WIDTH)
        tokens_out_ref[line] = dot(gather_ref[...], rows).astype(bf16)


def run_relay(gather, windows):
    lines = windows.shape[0] // TILE
    return pl.pallas_call(
        relay_kernel,
        grid=(lines // 2,),
        in_specs=[whole(gather.shape), tiles((2 * TILE, SLOT, WIDTH))],
        out_specs=tiles((2, gather.shape[0], WIDTH)),
        out_shape=jax.ShapeDtypeStruct((lines, gather.shape[0], WIDTH), bf16),
        compiler_params=pltpu.CompilerParams(
            dimension_semantics=("arbitrary",), vmem_limit_bytes=VMEM_LIMIT
        ),
        cost_estimate=took(5),
        name="relay",
    )(gather, windows)


def early_out_kernel(own_ref, *refs):
    pieces, (fc1_ref, fc2_ref, wide, done) = refs[:-4], refs[-4:]
    per, share, _ = pieces[0].shape
    own = own_ref[0]
    half = len(pieces) // 2

    def copy_first(block):
        columns = pl.ds(pl.multiple_of(block * WIDTH, WIDTH), WIDTH)
        return pltpu.make_async_copy(wide.at[block], fc1_ref.at[:, columns], done.at[block])

    def copy_second(block):
        rows = pl.ds(pl.multiple_of((block - half) * WIDTH, WIDTH), WIDTH)
        return pltpu.make_async_copy(wide.at[block], fc2_ref.at[rows, :], done.at[block])

    for at, piece in enumerate(pieces):
        block = at ^ (own // per)
        for chunk in range(per):
            row = pl.multiple_of((chunk ^ (own % per)) * share, share)
            wide[block, pl.ds(row, share)] = piece[chunk].astype(f32)

        @pl.when(block < half)
        def first(block=block):
            copy_first(block).start()

        @pl.when(block >= half)
        def second(block=block):
            copy_second(block).start()

    for block in range(len(pieces)):
        (copy_first if block < half else copy_second)(block).wait()


def run_early_out(own, pieces, units):
    count = len(pieces)
    return pl.pallas_call(
        early_out_kernel,
        in_specs=[pl.BlockSpec(memory_space=pltpu.SMEM)] + [pl.BlockSpec(memory_space=pltpu.VMEM)] * count,
        out_specs=[pl.BlockSpec(memory_space=pl.ANY)] * 2,
        out_shape=[
            jax.ShapeDtypeStruct((WIDTH, units), f32),
            jax.ShapeDtypeStruct((units, WIDTH), f32),
        ],
        scratch_shapes=[pltpu.VMEM((count, WIDTH, WIDTH), f32), pltpu.SemaphoreType.DMA((count,))],
        compiler_params=pltpu.CompilerParams(vmem_limit_bytes=VMEM_LIMIT),
        cost_estimate=took(5),
        name="early_out",
    )(own, *pieces)


def late_out_kernel(own_ref, *refs):
    pieces, (qkv_ref, out_ref), small_refs, (wide, done) = refs[:-13], refs[-13:-11], refs[-11:-2], refs[-2:]
    per, share, _ = pieces[0].shape
    share -= 8
    own = own_ref[0]
    count = len(pieces)
    height = per * share
    split = WIDTH // height

    def copy_first(block):
        rows = pl.ds(pl.multiple_of(block % split * height, height), height)
        columns = pl.ds(pl.multiple_of(block // split * WIDTH, WIDTH), WIDTH)
        return pltpu.make_async_copy(wide.at[block], qkv_ref.at[rows, columns], done.at[block])

    def copy_second(block):
        rows = pl.ds(pl.multiple_of((block - 3 * split) * height, height), height)
        return pltpu.make_async_copy(wide.at[block], out_ref.at[rows, :], done.at[block])

    for at, piece in enumerate(pieces):
        block = at ^ (own // per)
        for chunk in range(per):
            row = pl.multiple_of((chunk ^ (own % per)) * share, share)
            wide[block, pl.ds(row, share)] = piece[chunk][:share].astype(f32)

        @pl.when(block < 3 * split)
        def first(block=block):
            copy_first(block).start()

        @pl.when(block >= 3 * split)
        def second(block=block):
            copy_second(block).start()

        @pl.when(block == 0)
        def vectors(piece=piece):
            lines = piece[own % per][share:].astype(f32)
            for line in range(8):
                small_refs[line][...] = lines[line : line + 1]
            lines = piece[1 ^ (own % per)][share:].astype(f32)
            for line in range(small_refs[8].shape[1] // WIDTH):
                small_refs[8][:, line * WIDTH : (line + 1) * WIDTH] = lines[line : line + 1]

    for block in range(count):
        (copy_first if block < 3 * split else copy_second)(block).wait()


def run_late_out(own, pieces, units):
    count = len(pieces)
    per, share, _ = pieces[0].shape
    return pl.pallas_call(
        late_out_kernel,
        in_specs=[pl.BlockSpec(memory_space=pltpu.SMEM)] + [pl.BlockSpec(memory_space=pltpu.VMEM)] * count,
        out_specs=[pl.BlockSpec(memory_space=pl.ANY)] * 2 + [pl.BlockSpec(memory_space=pltpu.VMEM)] * 9,
        out_shape=[
            jax.ShapeDtypeStruct((WIDTH, 3 * WIDTH), f32),
            jax.ShapeDtypeStruct((WIDTH, WIDTH), f32),
            *[jax.ShapeDtypeStruct((1, WIDTH), f32)] * 8,
            jax.ShapeDtypeStruct((1, units), f32),
        ],
        scratch_shapes=[
            pltpu.VMEM((count, per * (share - 8), WIDTH), f32),
            pltpu.SemaphoreType.DMA((count,)),
        ],
        compiler_params=pltpu.CompilerParams(vmem_limit_bytes=VMEM_LIMIT),
        cost_estimate=took(3),
        name="late_out",
    )(own, *pieces)


def band_to_windows(band_values, win_count):
    trailing = band_values.shape[2:]
    blocks = band_values.reshape(
        (band_values.shape[0] // WIN_SIDE, WIN_SIDE, REG_SIDE, WIN_SIDE) + trailing
    )
    return jnp.swapaxes(blocks, 1, 2).reshape((win_count, WIN_SIDE * WIN_SIDE) + trailing)


def rank_of(keys):
    return jnp.sum(keys[None, :] < keys[:, None], axis=1)


def reduce_stages():
    img_bits = [("img", bit) for bit in range(lax.axis_size("img").bit_length() - 1)]
    dp_bits = [("dp", bit) for bit in range(lax.axis_size("dp").bit_length() - 1)]
    rest = img_bits[1:] + dp_bits
    return [img_bits[:1]] + [rest[at : at + 2] for at in range(0, len(rest), 2)]


def stage_masks(stage):
    img_size = lax.axis_size("img")
    return [(1 << bit) * (img_size if name == "dp" else 1) for name, bit in stage]


def stage_moves(stage):
    devices = lax.axis_size("dp") * lax.axis_size("img")
    moves = []
    for offset in range(1, 1 << len(stage)):
        flip = sum(mask for place, mask in enumerate(stage_masks(stage)) if offset >> place & 1)
        moves.append((offset, [(at, at ^ flip) for at in range(devices)]))
    return moves


def own_share(stages):
    flat = lax.axis_index("dp") * lax.axis_size("img") + lax.axis_index("img")
    share = 0
    for stage in stages:
        own = sum(((flat // mask) % 2) << place for place, mask in enumerate(stage_masks(stage)))
        share = (share << len(stage)) + own
    return share


def swap(rows, pairs):
    return lax.ppermute(rows, ("dp", "img"), pairs)


def add_up(pieces):
    return sum(piece.astype(f32) for piece in pieces).astype(bf16)


def split_sum(pieces, stage):
    parts = [piece.reshape((1 << len(stage), -1) + piece.shape[1:]) for piece in pieces]
    return [add_up([part[place] for part in parts]) for place in range(1 << len(stage))]


def sum_parts(parts, stage):
    return [parts[0]] + [swap(parts[offset], pairs) for offset, pairs in stage_moves(stage)]


def sum_stage(rows, stage):
    return add_up(sum_parts(rows.reshape((1 << len(stage), -1) + rows.shape[1:]), stage))


def gather_stage(rows, stage):
    return jnp.concatenate([rows] + [swap(rows, pairs) for _, pairs in stage_moves(stage)], axis=0)


def sum_stages(rows, stages):
    for stage in stages:
        rows = sum_stage(rows, stage)
    return rows


def deal_kernel(pick_ref, region_ref, local_ref, out_ref):
    groups = out_ref.shape[0]
    for pair in range(out_ref.shape[1] // 16):
        head = region_ref[...] if pair == 0 else local_ref[2 * pair - 1]
        rows = jnp.concatenate([head, local_ref[2 * pair]], axis=0)
        out_ref[:, 16 * pair : 16 * pair + 16, :] = (
            dot(pick_ref[...], rows).astype(bf16).reshape(groups, 16, WIDTH)
        )


def collect_kernel(pick_ref, came_ref, region_ref, local_ref):
    slots = region_ref.shape[0]
    for pair in range(came_ref.shape[1] // 16):
        rows = came_ref[:, 16 * pair : 16 * pair + 16, :].reshape(2 * slots, WIDTH)
        rows = dot(pick_ref[...], rows).astype(bf16)
        if pair == 0:
            region_ref[...] = rows[:slots]
        else:
            local_ref[2 * pair - 1] = rows[:slots]
        local_ref[2 * pair] = rows[slots:]


def run_deal(pick, region, local):
    count = region.shape[0] // TILE
    return pl.pallas_call(
        deal_kernel,
        out_shape=jax.ShapeDtypeStruct((count, (local.shape[0] + 1) * TILE, WIDTH), bf16),
        compiler_params=pltpu.CompilerParams(vmem_limit_bytes=VMEM_LIMIT),
        cost_estimate=took(5),
        name="deal",
    )(pick, region, local)


def run_collect(pick, came):
    slots = came.shape[0] * TILE
    return pl.pallas_call(
        collect_kernel,
        out_shape=[
            jax.ShapeDtypeStruct((slots, WIDTH), bf16),
            jax.ShapeDtypeStruct((came.shape[1] // TILE - 1, slots, WIDTH), bf16),
        ],
        compiler_params=pltpu.CompilerParams(vmem_limit_bytes=VMEM_LIMIT),
        cost_estimate=took(5),
        name="collect",
    )(pick, came)


def swap_tiles(tiles_sent, devices):
    count, rows, width = tiles_sent.shape
    share = count * TILE // devices
    if share == TILE:
        return lax.all_to_all(tiles_sent, "dp", split_axis=0, concat_axis=0, tiled=True)
    places = rows // TILE
    sent = tiles_sent.reshape(count, places, TILE, width).transpose(1, 0, 2, 3)
    sent = sent.reshape(places, devices, share, width).transpose(1, 0, 2, 3)
    came = lax.all_to_all(sent, "dp", split_axis=0, concat_axis=0, tiled=True)
    came = came.transpose(1, 0, 2, 3).reshape(places, count, TILE, width)
    return came.transpose(1, 0, 2, 3).reshape(count, rows, width)


def row_maps():
    window = np.arange(TILE)[:, None]
    place = np.arange(WIN_SIDE * WIN_SIDE)[None, :]
    raster = place // WIN_SIDE * (TILE * WIN_SIDE) + window * WIN_SIDE + place % WIN_SIDE
    band = TILE * WIN_SIDE * WIN_SIDE
    spread = np.zeros((TILE * SLOT, band), np.float32)
    spread[window * SLOT + 1 + place, raster] = 1
    gather = np.zeros((band, TILE * SLOT), np.float32)
    gather[raster, window * SLOT + 1 + place] = 1
    place = np.arange(WIN_SIDE * WIN_SIDE + 1)[None, :]
    squeeze = np.zeros(((WIN_SIDE * WIN_SIDE + 1) * TILE, TILE * TALL), np.float32)
    squeeze[place * TILE + window, window * TALL + place] = 1
    return [jnp.asarray(table, bf16) for table in (spread, gather, squeeze, squeeze.T)]


def shards(
    tokens,
    regional,
    pad_mask,
    keep_mask,
    window_slot,
    ln1_gain,
    ln1_bias,
    w_qkv,
    bias_q,
    bias_v,
    w_out,
    bias_out,
    ln2_gain,
    ln2_bias,
    w_fc1,
    bias_fc1,
    w_fc2,
    bias_fc2,
    cot_local,
    cot_regional,
):
    devices = lax.axis_size("dp")
    stages = reduce_stages()
    parts = devices * lax.axis_size("img")
    own_rank = lax.axis_index("dp")
    win_count = regional.shape[1]
    all_windows = window_slot.shape[1]
    slot_of = window_slot[0]
    places = jnp.arange(win_count)
    own_target = lax.dynamic_slice_in_dim(slot_of, own_rank * win_count, win_count) // win_count
    own_place = rank_of(own_target * win_count + places)
    order = jnp.sum(jnp.where(own_place[None, :] == places[:, None], places[None, :], 0), axis=1)
    slot_hit = slot_of[None, :] == (own_rank * win_count + places)[:, None]
    window_here = jnp.sum(jnp.where(slot_hit, jnp.arange(all_windows)[None, :], 0), axis=1)
    here_place = rank_of(window_here)
    deal_row = jnp.arange(2 * win_count)
    row_place = deal_row // (2 * TILE) * TILE + deal_row % TILE
    row_half = deal_row // TILE % 2
    column_hit = row_place[:, None] == jnp.concatenate([here_place, here_place])[None, :]
    pick = (column_hit & (row_half[:, None] == (deal_row // win_count)[None, :])).astype(bf16)
    pick_back = (column_hit & (row_half[:, None] == (deal_row // win_count)[None, :])).T.astype(bf16)
    cot = swap_tiles(
        run_deal(pick, cot_regional[0], jnp.swapaxes(cot_local[0], 0, 1)), devices
    )
    image = own_rank * win_count // REGIONS
    keep = lax.dynamic_slice_in_dim(keep_mask[0], image, 1).astype(f32) / survive
    live = band_to_windows(pad_mask[0], win_count) != 0
    allowed = jnp.concatenate(
        [jnp.ones((win_count, 1), bool), live, jnp.zeros((win_count, SLOT - 1 - live.shape[1]), bool)],
        axis=1,
    )
    window_bias = jnp.broadcast_to(
        jnp.where(allowed, 0.0, -1e30).astype(bf16)[:, :, None], (win_count, SLOT, LANES)
    )
    region_bias = jnp.broadcast_to(
        jnp.where(live[:, 0], 0.0, -1e30).astype(bf16)[:, None], (win_count, LANES)
    )
    spread, gather, squeeze, stretch = row_maps()
    plain, mixed_mask = head_masks()
    gain1, bias1, gain2, bias2 = ln1_gain[None], ln1_bias[None], ln2_gain[None], ln2_bias[None]
    out, qkv, probs, joined, mixed, after, hidden, slope, qkv_r, probs_r, mixed_r = run_forward(
        order, keep, tokens.reshape(REG_SIDE, -1, WIDTH), regional[0], window_bias, region_bias,
        spread, squeeze, plain, mixed_mask, gain1, bias1, w_qkv, bias_q[None], bias_v[None], w_out, bias_out[None],
        gain2, bias2, w_fc1, bias_fc1[None], w_fc2, bias_fc2[None],
    )
    came = swap_tiles(out, devices)
    own = own_share(stages)[None]
    grad_after, grad_mixed, early, early_sent, grad_out, small, row_fc1 = run_back_mlp(
        parts, keep, own, cot, after, mixed, hidden, slope, stretch, gain2, bias2, w_fc1, w_fc2, w_out
    )
    (_, pairs), = stage_moves(stages[0])
    early_came = swap(early_sent, pairs)
    attention = (
        order, keep, own, qkv, probs, joined, grad_mixed, grad_after, plain, mixed_mask, gain1, bias1
    )
    grad_qkv, *held = run_back_attention(*attention)
    early = split_sum([early, early_came], stages[1])
    held, early, came = lax.optimization_barrier((held, early, came))
    early = add_up(sum_parts(early, stages[1]))
    grad_qkv, late, late_sent, regional_out = run_back_attention(
        *attention,
        held=(*held, grad_qkv),
        ending=(grad_out, order[None], regional[0], qkv_r, probs_r, mixed_r, w_qkv, w_out, small, row_fc1),
        parts=parts,
    )
    late_came = swap(late_sent, pairs)
    grad_qkv, early = lax.optimization_barrier((grad_qkv, early))
    early = sum_stages(early, stages[2:])
    rows = (order, grad_qkv, joined, grad_after, gain1, w_qkv)
    windows = run_back_rows(*rows, 0, ROWS_FIRST)
    windows, late_came = lax.optimization_barrier((windows, late_came))
    late = add_up(sum_parts(split_sum([late, late_came], stages[1]), stages[1]))
    windows, early = lax.optimization_barrier((windows, early))
    for stage in reversed(stages[2:]):
        early = gather_stage(early, stage)
    windows = run_back_rows(*rows, ROWS_FIRST, win_count // TILE - ROWS_FIRST, held=windows)
    windows, early, late = lax.optimization_barrier((windows, early, late))
    late = sum_stages(late, stages[2:])
    moves = stage_moves(stages[1])
    early = [early] + [swap(early, moves[at][1]) for at in range(2)]
    early_far = [swap(early[0], pairs)]
    tokens_out = run_relay(gather, windows)
    tokens_out, came, early, early_far, late = lax.optimization_barrier(
        (tokens_out, came, early, early_far, late)
    )
    early += [swap(early[0], pairs) for _, pairs in moves[2:]]
    early_far += [swap(piece, pairs) for piece in early[1:3]]
    for stage in reversed(stages[2:]):
        late = gather_stage(late, stage)
    came, late = lax.optimization_barrier((came, late))
    late = [late] + [swap(late, pairs) for _, pairs in moves]
    early_far += [swap(piece, pairs) for piece in early[3:]]
    late_far = [swap(late[0], pairs)]
    grad_w_fc1, grad_w_fc2 = run_early_out(own, early + early_far, w_fc1.shape[1])
    out_regional, out_local = run_collect(pick_back, came)
    grad_w_fc1, grad_w_fc2, out_local, late, late_far = lax.optimization_barrier(
        (grad_w_fc1, grad_w_fc2, out_local, late, late_far)
    )
    late_far += [swap(piece, pairs) for piece in late[1:]]
    grad_w_qkv, grad_w_out, *vectors = run_late_out(own, late + late_far, w_fc1.shape[1])
    vectors = [vector[0] for vector in vectors]
    return (
        jnp.swapaxes(out_local, 0, 1)[None],
        out_regional[None],
        tokens_out.reshape(tokens.shape),
        regional_out[None],
        vectors[0],
        vectors[1],
        grad_w_qkv,
        vectors[2],
        vectors[3],
        grad_w_out,
        vectors[4],
        vectors[5],
        vectors[6],
        grad_w_fc1,
        vectors[8],
        grad_w_fc2,
        vectors[7],
    )


def solution(mesh):
    in_specs = (
        P("img", "dp", None, None),
        P("img", "dp", None),
        P("img", "dp", None),
        P("img", None),
        P("img", None),
        P(),
        P(),
        P(),
        P(),
        P(),
        P(),
        P(),
        P(),
        P(),
        P(),
        P(),
        P(),
        P(),
        P("img", "dp", None, None),
        P("img", "dp", None),
    )
    out_specs = (
        P("img", "dp", None, None),
        P("img", "dp", None),
        P("img", "dp", None, None),
        P("img", "dp", None),
        P(),
        P(),
        P(),
        P(),
        P(),
        P(),
        P(),
        P(),
        P(),
        P(),
        P(),
        P(),
        P(),
    )
    return jax.shard_map(shards, mesh=mesh, in_specs=in_specs, out_specs=out_specs, check_vma=False)
```

```python
import functools
import math
import jax
import jax.numpy as jnp
import numpy as np
from jax import lax
from jax.experimental import pallas as pl
from jax.experimental.pallas import tpu as pltpu
from jax.sharding import PartitionSpec as P

HEADS = 16
HDIM = 32
WIN_SIDE = 7
REG_SIDE = 8
REGIONS = 64

norm_eps = 1e-05
survive = 0.9

WIDTH = 512
SLOT = 64
TALL = 56
TILE = 8
GROUP = 4
GROUPS = HEADS // GROUP
TOGETHER = 8
LANES = 128
DEAL_PARTS = 5
ATTENTION_FIRST = 3
ROWS_FIRST = 2
ONES = 16
CHUNK = 512
MIB = 1024 * 1024
VMEM_LIMIT = 60 * MIB

f32 = jnp.float32


def took(micros):
    return pl.CostEstimate(flops=int(micros * 1.15e9), bytes_accessed=1_000_000, transcendentals=0)

bf16 = jnp.bfloat16


def dot(left, right):
    return lax.dot_general(left, right, (((1,), (0,)), ((), ())), preferred_element_type=f32)


def dot_nt(left, right):
    return lax.dot_general(left, right, (((1,), (1,)), ((), ())), preferred_element_type=f32)


def head_masks():
    lane_head = np.arange(LANES) // HDIM
    plain = np.repeat(np.arange(GROUP), SLOT)
    mixed = np.repeat(np.array([0, 2, 1, 3]), SLOT)
    return (
        jnp.asarray(plain[:, None] == lane_head[None, :], bf16),
        jnp.asarray(mixed[:, None] == lane_head[None, :], bf16),
    )


def spread_heads(rows, mask):
    return jnp.concatenate([rows] * GROUP, axis=0) * mask


def turn(blocks):
    stacked = jnp.concatenate([blocks[:, :LANES], blocks[:, LANES:]], axis=0)
    turned = stacked.T
    return jnp.concatenate([turned[:SLOT], turned[SLOT:]], axis=1)


def attend_scores(items, plain):
    return [dot_nt(key_rows, spread_heads(queries, plain)) for queries, key_rows, _, _ in items]


def attend_probs(items, scores):
    probs = []
    for rows, (_, _, _, bias) in zip(scores, items):
        rows = rows + bias
        highest = jnp.max(rows, axis=0, keepdims=True)
        weighted = jnp.exp2((rows - highest) * (HDIM**-0.5 * math.log2(math.e)))
        total = jnp.sum(weighted, axis=0, keepdims=True)
        probs.append((weighted * (1.0 / total)).astype(bf16))
    return probs


def attend_mix(items, turned, mixed):
    return [dot(rows, spread_heads(item[2], mixed)) for rows, item in zip(turned, items)]


def attend_back(items, plain, mixed):
    wide = [spread_heads(item[4], plain) for item in items]
    grad_probs = [dot_nt(item[2], rows) for item, rows in zip(items, wide)]
    grad_values = [dot(item[3], rows) for item, rows in zip(items, wide)]
    scores = []
    for rows, item in zip(grad_probs, items):
        soft = item[3].astype(f32)
        weighted = soft * rows
        inner = jnp.sum(weighted, axis=0, keepdims=True)
        scores.append((weighted - soft * inner).astype(bf16))
    turned = [turn(rows) for rows in scores]
    factor = HDIM**-0.5
    grad_keys = [dot(rows, spread_heads(item[0], plain)) * factor for rows, item in zip(scores, items)]
    grad_queries = [dot(rows, spread_heads(item[1], mixed)) * factor for rows, item in zip(turned, items)]
    return list(zip(grad_queries, grad_keys, grad_values))


def normalize(rows):
    centered = rows - jnp.mean(rows, axis=-1, keepdims=True)
    spread = jnp.mean(centered * centered, axis=-1, keepdims=True)
    scale = lax.rsqrt(spread + norm_eps)
    return centered * scale, scale


def normalize_back(grad_unit, unit, scale):
    first = jnp.mean(grad_unit, axis=-1, keepdims=True)
    second = jnp.mean(grad_unit * unit, axis=-1, keepdims=True)
    return scale * (grad_unit - first - unit * second)


def gelu_pair(values):
    below = 0.5 + 0.5 * lax.erf(values * 0.7071067811865476)
    bell = jnp.exp2(values * values * (-0.5 * math.log2(math.e)))
    return values * below, below + values * bell * 0.3989422804014327


def fold_lanes(rows):
    return sum(rows[:, at : at + LANES] for at in range(0, rows.shape[1], LANES))


def column_sum(rows):
    return jnp.sum(rows, axis=0, keepdims=True)


def window_items(qkv_of, bias):
    wide = jnp.concatenate([bias, bias], axis=1).astype(f32)
    return [
        (qkv_of(group), qkv_of(GROUPS + group), qkv_of(2 * GROUPS + group), wide) for group in range(GROUPS)
    ]


def attend_windows_back(windows, plain, mixed):
    items = []
    for qkv_of, probs_of, grad_of, _ in windows:
        for group in range(GROUPS):
            probs = jnp.concatenate([probs_of(2 * group), probs_of(2 * group + 1)], axis=1)
            items.append(
                (qkv_of(group), qkv_of(GROUPS + group), qkv_of(2 * GROUPS + group), probs, grad_of(group))
            )
    grads = attend_back(items, plain, mixed)
    for at, (_, _, _, put_grad) in enumerate(windows):
        for group in range(GROUPS):
            for part in range(3):
                put_grad(part * GROUPS + group, grads[at * GROUPS + group][part].astype(bf16))


def forward_kernel(
    order_ref, keep_ref,
    tokens_ref, regional_ref, window_bias_ref, region_bias_ref, spread_ref, squeeze_ref,
    plain_ref, mixed_mask_ref, gain1_ref, bias1_ref, w_qkv_ref, bias_q_ref, bias_v_ref, w_out_ref, bias_out_ref,
    gain2_ref, bias2_ref, w_fc1_ref, bias_fc1_ref, w_fc2_ref, bias_fc2_ref,
    out_ref, qkv_ref, probs_ref, joined_ref, mixed_ref, after_ref, hidden_ref, slope_ref,
    qkv_r_ref, probs_r_ref, mixed_r_ref,
    windows, normed, mixed_rows, joined_rows,
):
    step = pl.program_id(0)
    last = pl.num_programs(0) - 1
    keep = keep_ref[0]
    plain = plain_ref[...]
    mixed = mixed_mask_ref[...]
    count = TILE * TALL
    chunks = [slice(at, at + CHUNK) for at in range(0, w_fc1_ref.shape[1], CHUNK)]
    tile = {}

    @pl.when(step == 0)
    def first():
        region = regional_ref[...].astype(f32)
        unit, _ = normalize(region)
        region_norm = (unit * gain1_ref[...] + bias1_ref[...]).astype(bf16)
        region_qkv = dot(region_norm, w_qkv_ref[...])
        region_qkv = jnp.concatenate(
            [
                region_qkv[:, :WIDTH] + bias_q_ref[...],
                region_qkv[:, WIDTH : 2 * WIDTH],
                region_qkv[:, 2 * WIDTH :] + bias_v_ref[...],
            ],
            axis=1,
        ).astype(bf16)
        for at in range(3 * GROUPS):
            qkv_r_ref[at] = region_qkv[:, at * LANES : (at + 1) * LANES]
        items = window_items(lambda at: region_qkv[:, at * LANES : (at + 1) * LANES], region_bias_ref[...])
        probs = attend_probs(items, attend_scores(items, plain))
        for group in range(GROUPS):
            probs_r_ref[2 * group] = probs[group][:, :LANES]
            probs_r_ref[2 * group + 1] = probs[group][:, LANES:]
        outs = attend_mix(items, [turn(rows) for rows in probs], mixed)
        region_mixed = jnp.concatenate(outs, axis=1).astype(bf16)
        mixed_r_ref[...] = region_mixed
        region_mid = region + keep * (dot(region_mixed, w_out_ref[...]) + bias_out_ref[...])
        region_mid = region_mid.astype(bf16)
        row = lax.broadcasted_iota(jnp.int32, (TILE * SLOT, REGIONS), 0)
        column = lax.broadcasted_iota(jnp.int32, (TILE * SLOT, REGIONS), 1)

        def relay(line, carry):
            pick = (row == (column - line * TILE) * SLOT).astype(bf16)
            rows = dot(spread_ref[...], tokens_ref[line]) + dot(pick, region_mid)
            windows[pl.ds(line * TILE, TILE)] = rows.reshape(TILE, SLOT, WIDTH)
            return carry

        lax.fori_loop(0, REG_SIDE, relay, 0)


    def norm_rows():
        for at in range(TILE):
            rows = windows[order_ref[step * TILE + at]]
            joined_ref[at] = rows.astype(bf16)
            unit, _ = normalize(rows)
            normed[at * SLOT : (at + 1) * SLOT] = (unit * gain1_ref[...] + bias1_ref[...]).astype(bf16)

    def project(part):
        cols = slice(part * WIDTH, (part + 1) * WIDTH)
        qkv = dot(normed[...], w_qkv_ref[:, cols])
        if part != 1:
            qkv = qkv + (bias_q_ref if part == 0 else bias_v_ref)[...]
        qkv = qkv.astype(bf16).reshape(TILE, SLOT, WIDTH)
        for group in range(GROUPS):
            qkv_ref[:, part * GROUPS + group] = qkv[:, :, group * LANES : (group + 1) * LANES]

    def score(half):
        items = []
        for at in half:
            bias = window_bias_ref[order_ref[step * TILE + at]]
            items += window_items(lambda place, at=at: qkv_ref[at, place], bias)
        return items, attend_scores(items, plain)

    def soften(half, items, scores):
        probs = attend_probs(items, scores)
        for at, rows in enumerate(probs):
            window, group = half[at // GROUPS], at % GROUPS
            probs_ref[window, 2 * group] = rows[:, :LANES]
            probs_ref[window, 2 * group + 1] = rows[:, LANES:]
        return [turn(rows) for rows in probs]

    def mix(half, items, turned):
        outs = attend_mix(items, turned, mixed)
        for at, rows in enumerate(outs):
            window, group = half[at // GROUPS], at % GROUPS
            mixed_rows[window, :, group * LANES : (group + 1) * LANES] = rows

    def keep_joined():
        for at in range(TILE):
            joined_rows[at] = joined_ref[at].astype(f32)


    def branch():
        mixed_low = mixed_rows[:, :TALL].reshape(count, WIDTH).astype(bf16)
        mixed_ref[...] = mixed_low
        after = joined_rows[:, :TALL].reshape(count, WIDTH) + keep * (
            dot(mixed_low, w_out_ref[...]) + bias_out_ref[...]
        )
        after_ref[...] = after

    def norm_after():
        unit, _ = normalize(after_ref[...])
        tile["norm"] = (unit * gain2_ref[...] + bias2_ref[...]).astype(bf16)
        tile["total"] = jnp.zeros((count, WIDTH), f32)

    def widen(at):
        tile[at] = dot(tile["norm"], w_fc1_ref[:, chunks[at]])

    def bend(at):
        cols = chunks[at]
        hidden, slope = gelu_pair(tile[at] + bias_fc1_ref[:, cols])
        tile[at] = hidden.astype(bf16)
        hidden_ref[:, cols] = tile[at]
        slope_ref[:, cols] = slope.astype(bf16)

    def narrow(at):
        tile["total"] = tile["total"] + dot(tile[at], w_fc2_ref[chunks[at], :])

    def send():
        result = after_ref[...] + keep * (tile["total"] + bias_fc2_ref[...])
        out_ref[0] = dot(squeeze_ref[...], result.astype(bf16)).astype(bf16)

    halves = [list(range(TILE // 2)), list(range(TILE // 2, TILE))]

    @pl.when(step == 0)
    def attention_only():
        norm_rows()
        for part in range(3):
            project(part)
        scored = [score(half) for half in halves]
        turned = [soften(half, *pair) for half, pair in zip(halves, scored)]
        for half, pair, rows in zip(halves, scored, turned):
            mix(half, pair[0], rows)
        keep_joined()

    @pl.when((step > 0) & (step < last))
    def both():
        branch()
        norm_rows()
        project(0)
        norm_after()
        project(1)
        widen(0)
        project(2)
        widen(1)
        bend(0)
        scored = [score(halves[0]), None]
        narrow(0)
        bend(1)
        widen(2)
        scored[1] = score(halves[1])
        turned = [soften(halves[0], *scored[0]), None]
        narrow(1)
        widen(3)
        bend(2)
        mix(halves[0], scored[0][0], turned[0])
        turned[1] = soften(halves[1], *scored[1])
        narrow(2)
        bend(3)
        mix(halves[1], scored[1][0], turned[1])
        narrow(3)
        send()
        keep_joined()

    @pl.when(step == last)
    def feed_only():
        branch()
        norm_after()
        widen(0)
        for at in range(len(chunks)):
            if at + 1 < len(chunks):
                widen(at + 1)
            bend(at)
            narrow(at)
        send()


def whole(shape):
    return pl.BlockSpec(shape, lambda step, *_: (0,) * len(shape))


def tiles(shape):
    return pl.BlockSpec(shape, lambda step, *_: (step,) + (0,) * (len(shape) - 1))


def run_forward(order, keep, tokens, regional, window_bias, region_bias, spread, squeeze, plain, mixed,
                gain1, bias1, w_qkv, bias_q, bias_v, w_out, bias_out, gain2, bias2, w_fc1, bias_fc1, w_fc2, bias_fc2):
    windows = regional.shape[0]
    steps = windows // TILE
    rows = TILE * TALL
    hidden = w_fc1.shape[1]
    compact = squeeze.shape[0]
    args = (tokens, regional, window_bias, region_bias, spread, squeeze, plain, mixed,
            gain1, bias1, w_qkv, bias_q, bias_v, w_out, bias_out, gain2, bias2, w_fc1, bias_fc1, w_fc2, bias_fc2)
    def ahead(shape):
        return pl.BlockSpec(
            shape, lambda step, *_: (jnp.minimum(step, steps - 1),) + (0,) * (len(shape) - 1)
        )

    def behind(shape):
        return pl.BlockSpec(shape, lambda step, *_: (jnp.maximum(step - 1, 0),) + (0,) * (len(shape) - 1))

    outs = [
        ((steps, compact, WIDTH), bf16, behind((1, compact, WIDTH))),
        ((windows, 3 * GROUPS, SLOT, LANES), bf16, ahead((TILE, 3 * GROUPS, SLOT, LANES))),
        ((windows, 2 * GROUPS, SLOT, LANES), bf16, ahead((TILE, 2 * GROUPS, SLOT, LANES))),
        ((windows, SLOT, WIDTH), bf16, ahead((TILE, SLOT, WIDTH))),
        ((steps * rows, WIDTH), bf16, behind((rows, WIDTH))),
        ((steps * rows, WIDTH), f32, behind((rows, WIDTH))),
        ((steps * rows, hidden), bf16, behind((rows, hidden))),
        ((steps * rows, hidden), bf16, behind((rows, hidden))),
    ]
    fixed = [
        ((3 * GROUPS, REGIONS, LANES), bf16),
        ((2 * GROUPS, REGIONS, LANES), bf16),
        ((REGIONS, WIDTH), bf16),
    ]
    return pl.pallas_call(
        forward_kernel,
        grid_spec=pltpu.PrefetchScalarGridSpec(
            num_scalar_prefetch=2,
            grid=(steps + 1,),
            in_specs=[whole(a.shape) for a in args],
            out_specs=[spec for _, _, spec in outs] + [whole(s) for s, _ in fixed],
            scratch_shapes=[
                pltpu.VMEM((windows, SLOT, WIDTH), f32),
                pltpu.VMEM((TILE * SLOT, WIDTH), bf16),
                pltpu.VMEM((TILE, SLOT, WIDTH), f32),
                pltpu.VMEM((TILE, SLOT, WIDTH), f32),
            ],
        ),
        out_shape=[jax.ShapeDtypeStruct(s, d) for s, d, _ in outs]
        + [jax.ShapeDtypeStruct(s, d) for s, d in fixed],
        compiler_params=pltpu.CompilerParams(
            dimension_semantics=("arbitrary",), vmem_limit_bytes=62 * MIB
        ),
        cost_estimate=took(61),
        name="forward",
    )(order, keep, *args)


def put_shares(own, keep_ref, send_ref, chunk_of):
    half = keep_ref.shape[0]

    def fill(refs):
        for which, ref in enumerate(refs):
            for at in range(half):
                ref[at ^ (own % half)] = chunk_of(which * half + at)

    @pl.when(own < half)
    def low():
        fill((keep_ref, send_ref))

    @pl.when(own >= half)
    def high():
        fill((send_ref, keep_ref))


def back_mlp_kernel(
    keep_ref, own_ref, cot_ref, after_ref, mixed_ref, hidden_ref, slope_ref, stretch_ref,
    gain2_ref, bias2_ref, w_fc1_ref, w_fc2_ref, w_out_ref,
    grad_after_ref, grad_mixed_ref, stay_ref, send_ref, grad_out_ref, small_ref, bias_row_ref,
    sum_fc1, sum_fc2, sum_out, sums, sum_hidden, early_rows,
):
    step = pl.program_id(0)
    last = pl.num_programs(0) - 1
    keep = keep_ref[0]

    @pl.when(step == 0)
    def clear():
        for ref in (sum_fc1, sum_fc2, sum_out, sums, sum_hidden):
            ref[...] = jnp.zeros_like(ref)

    unit, scale = normalize(after_ref[...])
    mlp_norm = (unit * gain2_ref[...] + bias2_ref[...]).astype(bf16)
    norm_turned = mlp_norm.T
    cot = dot(stretch_ref[...], cot_ref[0])
    grad_mlp = (keep * cot).astype(bf16)
    grad_turned = grad_mlp.T
    sums[0:1] += column_sum(grad_mlp.astype(f32))
    grad_norm = jnp.zeros(after_ref.shape, f32)
    chunks = [slice(at, at + CHUNK) for at in range(0, w_fc1_ref.shape[1], CHUNK)]
    ahead = dot_nt(grad_mlp, w_fc2_ref[chunks[0], :])
    for at, cols in enumerate(chunks):
        grad_hidden = ahead
        if at + 1 < len(chunks):
            ahead = dot_nt(grad_mlp, w_fc2_ref[chunks[at + 1], :])
        sum_fc2[:, cols] += dot(grad_turned, hidden_ref[:, cols])
        grad_pre = (slope_ref[:, cols].astype(f32) * grad_hidden).astype(bf16)
        sum_fc1[:, cols] += dot(norm_turned, grad_pre)
        sum_hidden[0:1, cols] += column_sum(grad_pre.astype(f32))
        grad_norm = grad_norm + dot_nt(grad_pre, w_fc1_ref[:, cols])
    sums[1:2] += column_sum(grad_norm * unit)
    sums[2:3] += column_sum(grad_norm)
    grad_after = cot + normalize_back(grad_norm * gain2_ref[...], unit, scale)
    grad_after_ref[...] = grad_after
    grad_branch = (keep * grad_after).astype(bf16)
    sums[3:4] += column_sum(grad_branch.astype(f32))
    sum_out[...] += dot(mixed_ref[...].T, grad_branch)
    grad_mixed = dot_nt(grad_branch, w_out_ref[...]).reshape(TILE, TALL, WIDTH)
    empty = jnp.zeros((TILE, SLOT - TALL, WIDTH), f32)
    grad_mixed = jnp.concatenate([grad_mixed, empty], axis=1).astype(bf16)
    for group in range(GROUPS):
        grad_mixed_ref[:, group] = grad_mixed[:, :, group * LANES : (group + 1) * LANES]

    @pl.when(step == last)
    def finish():
        for at in range(4):
            cols = slice(at * WIDTH, (at + 1) * WIDTH)
            early_rows[cols, :] = sum_fc1[:, cols].astype(bf16)
            early_rows[4 * WIDTH + at * WIDTH : 4 * WIDTH + (at + 1) * WIDTH, :] = (
                sum_fc2[:, cols].T.astype(bf16)
            )
        rows = stay_ref.shape[1]
        put_shares(
            own_ref[0], stay_ref, send_ref, lambda at: early_rows[at * rows : (at + 1) * rows, :]
        )
        grad_out_ref[...] = sum_out[...]
        small_ref[...] = sums[...]
        bias_row_ref[...] = sum_hidden[...]


def run_back_mlp(parts, keep, own, cot, after, mixed, hidden, slope, stretch, gain2, bias2, w_fc1, w_fc2, w_out):
    steps, compact, _ = cot.shape
    rows = TILE * TALL
    units = w_fc1.shape[1]
    tiled = [(1, compact, WIDTH), (rows, WIDTH), (rows, WIDTH), (rows, units), (rows, units)]
    fixed = (stretch, gain2, bias2, w_fc1, w_fc2, w_out)
    outs = [
        ((steps * rows, WIDTH), f32, (rows, WIDTH)),
        ((steps * TILE, GROUPS, SLOT, LANES), bf16, (TILE, GROUPS, SLOT, LANES)),
    ]
    share = (parts // 2, 2 * units // parts, WIDTH)
    whole_outs = [(share, bf16), (share, bf16), ((WIDTH, WIDTH), f32), ((8, WIDTH), f32), ((8, units), f32)]
    return pl.pallas_call(
        back_mlp_kernel,
        grid_spec=pltpu.PrefetchScalarGridSpec(
            num_scalar_prefetch=2,
            grid=(steps,),
            in_specs=[tiles(b) for b in tiled] + [whole(a.shape) for a in fixed],
            out_specs=[tiles(block) for _, _, block in outs] + [whole(s) for s, _ in whole_outs],
            scratch_shapes=[
                pltpu.VMEM((WIDTH, units), f32),
                pltpu.VMEM((WIDTH, units), f32),
                pltpu.VMEM((WIDTH, WIDTH), f32),
                pltpu.VMEM((8, WIDTH), f32),
                pltpu.VMEM((8, units), f32),
                pltpu.VMEM((2 * units, WIDTH), bf16),
            ],
        ),
        out_shape=[jax.ShapeDtypeStruct(s, d) for s, d, _ in outs]
        + [jax.ShapeDtypeStruct(s, d) for s, d in whole_outs],
        compiler_params=pltpu.CompilerParams(
            dimension_semantics=("arbitrary",), vmem_limit_bytes=VMEM_LIMIT
        ),
        cost_estimate=took(55),
        name="back_mlp",
    )(keep, own, cot, after, mixed, hidden, slope, *fixed)


def back_attention_kernel(
    begin, last, order_ref, keep_ref, own_ref,
    qkv_ref, probs_ref, joined_ref, grad_mixed_ref, grad_after_ref,
    plain_ref, mixed_mask_ref, gain1_ref, bias1_ref, *refs,
):
    first = begin == 0
    held_in = ()
    if not first:
        held_in, refs = refs[:3], refs[4:]
    if last:
        ending, refs = refs[:10], refs[10:]
        grad_out_ref, order_row_ref, regional_ref, qkv_r_ref, probs_r_ref, mixed_r_ref = ending[:6]
        w_qkv_ref, w_out_ref, sums_mlp_ref, row_fc1_ref = ending[6:]
        grad_qkv_ref, stay_ref, send_ref, regional_out_ref, sum_qkv, heads, after_heads, late_rows = refs
    else:
        grad_qkv_ref, sum_qkv, heads, after_heads = refs
    step = pl.program_id(0)
    plain = plain_ref[...]
    mixed = mixed_mask_ref[...]

    @pl.when(step == 0)
    def open_sums():
        for at, ref in enumerate((sum_qkv, heads, after_heads)):
            ref[...] = jnp.zeros_like(ref) if first else held_in[at][...]

    def some(batch, carry):
        def window(at):
            rows = pl.ds(pl.multiple_of(at * SLOT, SLOT), SLOT)

            def put_grad(place, values):
                grad_qkv_ref[rows, place * LANES : (place + 1) * LANES] = values

            return (
                lambda place: qkv_ref[at, place],
                lambda place: probs_ref[at, place],
                lambda place: grad_mixed_ref[at, place],
                put_grad,
            )

        attend_windows_back([window(batch * TOGETHER + at) for at in range(TOGETHER)], plain, mixed)
        return carry

    lax.fori_loop(0, TILE // TOGETHER, some, 0)
    joined = joined_ref[...].reshape(TILE * SLOT, WIDTH).astype(f32)
    unit, _ = normalize(joined)
    normed = (unit * gain1_ref[...] + bias1_ref[...]).astype(bf16)
    turned = jnp.concatenate([normed.T, jnp.ones((ONES, TILE * SLOT), bf16)], axis=0)
    sum_qkv[...] += dot(turned, grad_qkv_ref[...])
    rows = pl.ds(pl.multiple_of((step + begin) * TILE, TILE), TILE)
    heads[rows, : 3 * WIDTH] = jnp.concatenate(
        [grad_qkv_ref[at * SLOT : at * SLOT + 16].astype(f32)[:1] for at in range(TILE)], axis=0
    )
    heads[rows, 3 * WIDTH :] = jnp.concatenate([joined_ref[at, :16].astype(f32)[:1] for at in range(TILE)], axis=0)
    after_heads[rows] = jnp.concatenate(
        [grad_after_ref[at * TALL : at * TALL + 1] for at in range(TILE)], axis=0
    )
    if not last:
        return

    @pl.when(step == pl.num_programs(0) - 1)
    def finish():
        keep = keep_ref[0]
        gain1 = gain1_ref[...]
        grad_normed = dot_nt(heads[:, : 3 * WIDTH].astype(bf16), w_qkv_ref[...])
        unit, scale = normalize(heads[:, 3 * WIDTH :])
        grad_mid = after_heads[...] + normalize_back(grad_normed * gain1, unit, scale)
        windows = grad_mid.shape[0]
        raster = lax.broadcasted_iota(jnp.int32, (windows, windows), 0)
        came = dot((raster == order_row_ref[...]).astype(bf16), grad_mid.astype(bf16))
        grad_branch = (keep * came).astype(bf16)
        grad_mixed = dot_nt(grad_branch, w_out_ref[...]).astype(bf16)
        parts = {}
        attend_windows_back(
            [
                (
                    lambda place: qkv_r_ref[place],
                    lambda place: probs_r_ref[place],
                    lambda place: grad_mixed[:, place * LANES : (place + 1) * LANES],
                    parts.__setitem__,
                )
            ],
            plain,
            mixed,
        )
        grad_qkv_r = jnp.concatenate([parts[place] for place in range(3 * GROUPS)], axis=1)
        unit_r, scale_r = normalize(regional_ref[...].astype(f32))
        normed_r = (unit_r * gain1 + bias1_ref[...]).astype(bf16)
        total = sum_qkv[:WIDTH] + dot(normed_r.T, grad_qkv_r)
        columns = sum_qkv[WIDTH : WIDTH + 1] + column_sum(grad_qkv_r.astype(f32))
        for part in range(3):
            cols = slice(part * WIDTH, (part + 1) * WIDTH)
            late_rows[cols, :] = total[:, cols].astype(bf16)
        late_rows[3 * WIDTH :, :] = (
            grad_out_ref[...] + dot(mixed_r_ref[...].T, grad_branch)
        ).astype(bf16)
        weights = w_qkv_ref[...].astype(f32)
        by_bias = weights * columns
        by_gain = weights * total
        turned_bias = fold_lanes(by_bias).T
        turned_gain = fold_lanes(by_gain).T
        grad_bias1 = column_sum(turned_bias)
        grad_gain1 = (column_sum(turned_gain) - bias1_ref[...] * grad_bias1) / gain1
        small = [
            grad_gain1,
            grad_bias1,
            columns[:, :WIDTH],
            columns[:, 2 * WIDTH :],
            sums_mlp_ref[3:4] + column_sum(grad_branch.astype(f32)),
            sums_mlp_ref[1:2],
            sums_mlp_ref[2:3],
            sums_mlp_ref[0:1],
        ]
        units = row_fc1_ref.shape[1] // WIDTH
        more = [row_fc1_ref[0:1, at * WIDTH : (at + 1) * WIDTH] for at in range(units)]
        more.append(jnp.zeros((8 - units, WIDTH), f32))
        share = stay_ref.shape[1] - 8

        def chunk_of(part):
            extra = jnp.zeros((8, WIDTH), f32)
            if part < 2:
                extra = jnp.concatenate(more if part else small, axis=0)
            rows = late_rows[part * share : (part + 1) * share]
            return jnp.concatenate([rows, extra.astype(bf16)], axis=0)

        put_shares(own_ref[0], stay_ref, send_ref, chunk_of)
        grad_normed_r = dot_nt(grad_qkv_r, w_qkv_ref[...])
        regional_out_ref[...] = (
            came + normalize_back(grad_normed_r * gain1, unit_r, scale_r)
        ).astype(bf16)


def run_back_attention(begin, count, order, keep, own, qkv, probs, joined, grad_mixed, grad_after, plain, mixed, gain1,
                       bias1, held=None, ending=None, parts=1):
    windows = qkv.shape[0]
    steps = windows // TILE
    rows = TILE * TALL

    def tile(shape):
        return pl.BlockSpec(shape, lambda step, *_: (step + begin,) + (0,) * (len(shape) - 1))

    tiled = [
        (TILE, 3 * GROUPS, SLOT, LANES),
        (TILE, 2 * GROUPS, SLOT, LANES),
        (TILE, SLOT, WIDTH),
        (TILE, GROUPS, SLOT, LANES),
        (rows, WIDTH),
    ]
    fixed = [plain, mixed, gain1, bias1]
    in_specs = [tile(b) for b in tiled] + [whole(a.shape) for a in fixed]
    args = [qkv, probs, joined, grad_mixed, grad_after] + fixed
    aliases = {}
    if held is not None:
        in_specs += [whole(a.shape) for a in held[:3]] + [pl.BlockSpec(memory_space=pl.ANY)]
        args += list(held)
        aliases = {3 + len(args) - 1: 0}
    if ending is not None:
        in_specs += [whole(a.shape) for a in ending]
        args += list(ending)
    held_shapes = [(WIDTH + ONES, 3 * WIDTH), (windows, 4 * WIDTH), (windows, WIDTH)]
    outs = [((steps * TILE * SLOT, 3 * WIDTH), bf16, tile((TILE * SLOT, 3 * WIDTH)))]
    scratch = []
    late_shape = (parts // 2, 4 * WIDTH // parts + 8, WIDTH)
    if ending is None:
        outs += [(s, f32, whole(s)) for s in held_shapes]
    else:
        outs += [
            (late_shape, bf16, whole(late_shape)),
            (late_shape, bf16, whole(late_shape)),
            ((windows, WIDTH), bf16, whole((windows, WIDTH))),
        ]
        scratch = [pltpu.VMEM(s, f32) for s in held_shapes] + [pltpu.VMEM((4 * WIDTH, WIDTH), bf16)]
    return pl.pallas_call(
        functools.partial(back_attention_kernel, begin, ending is not None),
        grid_spec=pltpu.PrefetchScalarGridSpec(
            num_scalar_prefetch=3,
            grid=(count,),
            in_specs=in_specs,
            out_specs=[spec for _, _, spec in outs],
            scratch_shapes=scratch,
        ),
        out_shape=[jax.ShapeDtypeStruct(s, d) for s, d, _ in outs],
        input_output_aliases=aliases,
        compiler_params=pltpu.CompilerParams(
            dimension_semantics=("arbitrary",), vmem_limit_bytes=VMEM_LIMIT
        ),
        cost_estimate=took(5 * count),
        name="back_attention",
    )(order, keep, own, *args)


def back_rows_kernel(begin, order_ref, grad_qkv_ref, joined_ref, grad_after_ref, gain1_ref, w_qkv_ref, *refs):
    windows_ref, rows_low, done = refs[-3:]
    step = pl.program_id(0)

    def copies(at_step):
        places = [order_ref[(begin + at_step) * TILE + at] for at in range(TILE)]
        return [
            pltpu.make_async_copy(rows_low.at[at], windows_ref.at[place], done.at[at])
            for at, place in enumerate(places)
        ]

    unit, scale = normalize(joined_ref[...].astype(f32).reshape(TILE * SLOT, WIDTH))
    grad_normed = dot_nt(grad_qkv_ref[...], w_qkv_ref[...])
    grad_in = normalize_back(grad_normed * gain1_ref[...], unit, scale)

    @pl.when(step > 0)
    def drain():
        for copy in copies(step - 1):
            copy.wait()

    empty = jnp.zeros((SLOT - TALL, WIDTH), f32)
    for at in range(TILE):
        rows = grad_in[at * SLOT : at * SLOT + TALL] + grad_after_ref[at * TALL : (at + 1) * TALL]
        rows_low[at] = jnp.concatenate([rows, empty], axis=0).astype(bf16)
    for copy in copies(step):
        copy.start()

    @pl.when(step == pl.num_programs(0) - 1)
    def finish():
        for copy in copies(step):
            copy.wait()


def run_back_rows(order, grad_qkv, joined, grad_after, gain1, w_qkv, begin, count, held=None):
    windows = joined.shape[0]

    def tile(shape):
        return pl.BlockSpec(shape, lambda step, *_: (step + begin,) + (0,) * (len(shape) - 1))

    tiled = [(TILE * SLOT, 3 * WIDTH), (TILE, SLOT, WIDTH), (TILE * TALL, WIDTH)]
    fixed = [gain1, w_qkv]
    in_specs = [tile(b) for b in tiled] + [whole(a.shape) for a in fixed]
    args = [grad_qkv, joined, grad_after] + fixed
    aliases = {}
    if held is not None:
        in_specs.append(pl.BlockSpec(memory_space=pl.ANY))
        args.append(held)
        aliases = {len(args): 0}
    return pl.pallas_call(
        functools.partial(back_rows_kernel, begin),
        grid_spec=pltpu.PrefetchScalarGridSpec(
            num_scalar_prefetch=1,
            grid=(count,),
            in_specs=in_specs,
            out_specs=pl.BlockSpec(memory_space=pl.ANY),
            scratch_shapes=[pltpu.VMEM((TILE, SLOT, WIDTH), bf16), pltpu.SemaphoreType.DMA((TILE,))],
        ),
        out_shape=jax.ShapeDtypeStruct((windows, SLOT, WIDTH), bf16),
        input_output_aliases=aliases,
        compiler_params=pltpu.CompilerParams(
            dimension_semantics=("arbitrary",), vmem_limit_bytes=VMEM_LIMIT
        ),
        cost_estimate=took(2.5 * count),
        name="back_rows",
    )(order, *args)


def relay_kernel(gather_ref, windows_ref, tokens_out_ref):
    for line in range(tokens_out_ref.shape[0]):
        rows = windows_ref[line * TILE : (line + 1) * TILE].reshape(TILE * SLOT, WIDTH)
        tokens_out_ref[line] = dot(gather_ref[...], rows).astype(bf16)


def run_relay(gather, windows):
    lines = windows.shape[0] // TILE
    return pl.pallas_call(
        relay_kernel,
        grid=(lines // 2,),
        in_specs=[whole(gather.shape), tiles((2 * TILE, SLOT, WIDTH))],
        out_specs=tiles((2, gather.shape[0], WIDTH)),
        out_shape=jax.ShapeDtypeStruct((lines, gather.shape[0], WIDTH), bf16),
        compiler_params=pltpu.CompilerParams(
            dimension_semantics=("arbitrary",), vmem_limit_bytes=VMEM_LIMIT
        ),
        cost_estimate=took(0.3),
        name="relay",
    )(gather, windows)


def widen_early(own, pieces, first, fc1_ref, fc2_ref, wide, done):
    half = 4

    def copies(place, slot):
        block = place ^ first
        columns = pl.ds(pl.multiple_of(block % half * WIDTH, WIDTH), WIDTH)
        copy_first = pltpu.make_async_copy(wide.at[slot], fc1_ref.at[:, columns], done.at[slot])
        copy_second = pltpu.make_async_copy(wide.at[slot], fc2_ref.at[columns, :], done.at[slot])
        return block, copy_first, copy_second

    for slot, (place, piece, low) in enumerate(pieces):
        share = piece.shape[1]
        per = WIDTH // share
        for chunk in range(per):
            row = pl.multiple_of((chunk ^ (own % per)) * share, share)
            wide[slot, pl.ds(row, share)] = piece[low + chunk].astype(f32)
        block, copy_first, copy_second = copies(place, slot)

        @pl.when(block < half)
        def start_first(copy=copy_first):
            copy.start()

        @pl.when(block >= half)
        def start_second(copy=copy_second):
            copy.start()

    def finish():
        for slot, (place, _, _) in enumerate(pieces):
            block, copy_first, copy_second = copies(place, slot)

            @pl.when(block < half)
            def wait_first(copy=copy_first):
                copy.wait()

            @pl.when(block >= half)
            def wait_second(copy=copy_second):
                copy.wait()

    return finish


def early_out_kernel(own_ref, near_ref, far_ref, fc1_ref, fc2_ref, wide, done):
    own = own_ref[0]
    per = near_ref.shape[0] // 3
    pieces = [(4 * half + at, ref, at * per) for half, ref in enumerate((near_ref, far_ref)) for at in range(3)]
    widen_early(own, pieces, own // per, fc1_ref, fc2_ref, wide, done)()


def run_early_out(own, near, far, units):
    return pl.pallas_call(
        early_out_kernel,
        in_specs=[pl.BlockSpec(memory_space=pltpu.SMEM)] + [pl.BlockSpec(memory_space=pltpu.VMEM)] * 2,
        out_specs=[pl.BlockSpec(memory_space=pl.ANY)] * 2,
        out_shape=[
            jax.ShapeDtypeStruct((WIDTH, units), f32),
            jax.ShapeDtypeStruct((units, WIDTH), f32),
        ],
        scratch_shapes=[pltpu.VMEM((6, WIDTH, WIDTH), f32), pltpu.SemaphoreType.DMA((6,))],
        compiler_params=pltpu.CompilerParams(vmem_limit_bytes=20 * MIB),
        cost_estimate=took(0.3),
        name="early_out",
    )(own, near, far)


def late_out_kernel(places, own_ref, *refs):
    pieces, refs = refs[:8], refs[8:]
    early, refs = refs[: len(places)], refs[len(places) + 2 :]
    (qkv_ref, out_ref), small_refs, (fc1_ref, fc2_ref, wide, wide_early, done, done_early) = refs[:2], refs[2:11], refs[11:]
    per, share, _ = pieces[0].shape
    share -= 8
    own = own_ref[0]
    count = len(pieces)
    height = per * share
    split = WIDTH // height
    finish = widen_early(
        own,
        [(place, piece, 0) for place, piece in zip(places, early)],
        own // early[0].shape[0],
        fc1_ref,
        fc2_ref,
        wide_early,
        done_early,
    )

    def copy_first(block):
        rows = pl.ds(pl.multiple_of(block % split * height, height), height)
        columns = pl.ds(pl.multiple_of(block // split * WIDTH, WIDTH), WIDTH)
        return pltpu.make_async_copy(wide.at[block], qkv_ref.at[rows, columns], done.at[block])

    def copy_second(block):
        rows = pl.ds(pl.multiple_of((block - 3 * split) * height, height), height)
        return pltpu.make_async_copy(wide.at[block], out_ref.at[rows, :], done.at[block])

    for at, piece in enumerate(pieces):
        block = at ^ (own // per)
        for chunk in range(per):
            row = pl.multiple_of((chunk ^ (own % per)) * share, share)
            wide[block, pl.ds(row, share)] = piece[chunk][:share].astype(f32)

        @pl.when(block < 3 * split)
        def first(block=block):
            copy_first(block).start()

        @pl.when(block >= 3 * split)
        def second(block=block):
            copy_second(block).start()

        @pl.when(block == 0)
        def vectors(piece=piece):
            lines = piece[own % per][share:].astype(f32)
            for line in range(8):
                small_refs[line][...] = lines[line : line + 1]
            lines = piece[1 ^ (own % per)][share:].astype(f32)
            for line in range(small_refs[8].shape[1] // WIDTH):
                small_refs[8][:, line * WIDTH : (line + 1) * WIDTH] = lines[line : line + 1]

    for block in range(count):
        (copy_first if block < 3 * split else copy_second)(block).wait()
    finish()


def run_late_out(own, pieces, early, grad_w_fc1, grad_w_fc2):
    places = (3, 7)
    count = len(pieces)
    per, share, _ = pieces[0].shape
    units = grad_w_fc1.shape[1]
    anywhere = pl.BlockSpec(memory_space=pl.ANY)
    kept = pl.BlockSpec(memory_space=pltpu.VMEM)
    inputs = [own, *pieces, *early, grad_w_fc1, grad_w_fc2]
    return pl.pallas_call(
        functools.partial(late_out_kernel, places),
        in_specs=[pl.BlockSpec(memory_space=pltpu.SMEM)] + [kept] * (count + len(places)) + [anywhere] * 2,
        out_specs=[anywhere] * 2 + [kept] * 9 + [anywhere] * 2,
        out_shape=[
            jax.ShapeDtypeStruct((WIDTH, 3 * WIDTH), f32),
            jax.ShapeDtypeStruct((WIDTH, WIDTH), f32),
            *[jax.ShapeDtypeStruct((1, WIDTH), f32)] * 8,
            jax.ShapeDtypeStruct((1, units), f32),
            jax.ShapeDtypeStruct((WIDTH, units), f32),
            jax.ShapeDtypeStruct((units, WIDTH), f32),
        ],
        input_output_aliases={len(inputs) - 2: 11, len(inputs) - 1: 12},
        scratch_shapes=[
            pltpu.VMEM((count, per * (share - 8), WIDTH), f32),
            pltpu.VMEM((len(places), WIDTH, WIDTH), f32),
            pltpu.SemaphoreType.DMA((count,)),
            pltpu.SemaphoreType.DMA((len(places),)),
        ],
        compiler_params=pltpu.CompilerParams(vmem_limit_bytes=20 * MIB),
        cost_estimate=took(3),
        name="late_out",
    )(*inputs)


def band_to_windows(band_values, win_count):
    trailing = band_values.shape[2:]
    blocks = band_values.reshape(
        (band_values.shape[0] // WIN_SIDE, WIN_SIDE, REG_SIDE, WIN_SIDE) + trailing
    )
    return jnp.swapaxes(blocks, 1, 2).reshape((win_count, WIN_SIDE * WIN_SIDE) + trailing)


def rank_of(keys):
    return jnp.sum(keys[None, :] < keys[:, None], axis=1)


def reduce_stages():
    img_bits = [("img", bit) for bit in range(lax.axis_size("img").bit_length() - 1)]
    dp_bits = [("dp", bit) for bit in range(lax.axis_size("dp").bit_length() - 1)]
    rest = img_bits[1:] + dp_bits
    return [img_bits[:1]] + [rest[at : at + 2] for at in range(0, len(rest), 2)]


def stage_masks(stage):
    img_size = lax.axis_size("img")
    return [(1 << bit) * (img_size if name == "dp" else 1) for name, bit in stage]


def stage_moves(stage):
    devices = lax.axis_size("dp") * lax.axis_size("img")
    moves = []
    for offset in range(1, 1 << len(stage)):
        flip = sum(mask for place, mask in enumerate(stage_masks(stage)) if offset >> place & 1)
        moves.append((offset, [(at, at ^ flip) for at in range(devices)]))
    return moves


def own_share(stages):
    flat = lax.axis_index("dp") * lax.axis_size("img") + lax.axis_index("img")
    share = 0
    for stage in stages:
        own = sum(((flat // mask) % 2) << place for place, mask in enumerate(stage_masks(stage)))
        share = (share << len(stage)) + own
    return share


def swap(rows, pairs):
    return lax.ppermute(rows, ("dp", "img"), pairs)


def add_up(pieces):
    return sum(piece.astype(f32) for piece in pieces).astype(bf16)


def split_sum(pieces, stage):
    parts = [piece.reshape((1 << len(stage), -1) + piece.shape[1:]) for piece in pieces]
    return [add_up([part[place] for part in parts]) for place in range(1 << len(stage))]


def sum_parts(parts, stage):
    return [parts[0]] + [swap(parts[offset], pairs) for offset, pairs in stage_moves(stage)]


def sum_stage(rows, stage):
    return add_up(sum_parts(rows.reshape((1 << len(stage), -1) + rows.shape[1:]), stage))


def gather_parts(rows, stage):
    return [rows] + [swap(rows, pairs) for _, pairs in stage_moves(stage)]


def gather_stage(rows, stage):
    return jnp.concatenate(gather_parts(rows, stage), axis=0)


def sum_stages(rows, stages):
    for stage in stages:
        rows = sum_stage(rows, stage)
    return rows


def deal_kernel(pick_ref, region_ref, local_ref, out_ref, rows_in, rows_out, came, gone):
    groups = out_ref.shape[0]
    positions = rows_in.shape[0]
    part = positions // DEAL_PARTS

    def copy_in(at):
        low = at * part
        if at == 0:
            return [
                pltpu.make_async_copy(region_ref, rows_in.at[0], came.at[DEAL_PARTS]),
                pltpu.make_async_copy(local_ref.at[: part - 1], rows_in.at[1:part], came.at[0]),
            ]
        return [
            pltpu.make_async_copy(local_ref.at[low - 1 : low + part - 1], rows_in.at[low : low + part], came.at[at])
        ]

    def copy_out(at):
        rows = slice(at * part * TILE, (at + 1) * part * TILE)
        return pltpu.make_async_copy(rows_out.at[:, rows, :], out_ref.at[:, rows, :], gone.at[at])

    for at in range(DEAL_PARTS):
        for copy in copy_in(at):
            copy.start()
    for at in range(DEAL_PARTS):
        for copy in copy_in(at):
            copy.wait()
        pairs = range(at * part // 2, (at + 1) * part // 2)
        dealt = [
            dot(pick_ref[...], jnp.concatenate([rows_in[2 * pair], rows_in[2 * pair + 1]], axis=0))
            for pair in pairs
        ]
        for pair, rows in zip(pairs, dealt):
            rows_out[:, 16 * pair : 16 * pair + 16, :] = rows.astype(bf16).reshape(groups, 16, WIDTH)
        copy_out(at).start()
    for at in range(DEAL_PARTS):
        copy_out(at).wait()


def collect_kernel(pick_ref, came_ref, region_ref, local_ref, rows_in, rows_out, came, gone):
    slots = region_ref.shape[0]
    positions = rows_out.shape[0]
    part = positions // DEAL_PARTS

    def copy_in(at):
        rows = slice(at * part * TILE, (at + 1) * part * TILE)
        return pltpu.make_async_copy(came_ref.at[:, rows, :], rows_in.at[:, rows, :], came.at[at])

    def copy_out(at):
        low = at * part
        if at == 0:
            return [
                pltpu.make_async_copy(rows_out.at[0], region_ref, gone.at[DEAL_PARTS]),
                pltpu.make_async_copy(rows_out.at[1:part], local_ref.at[: part - 1], gone.at[0]),
            ]
        return [
            pltpu.make_async_copy(rows_out.at[low : low + part], local_ref.at[low - 1 : low + part - 1], gone.at[at])
        ]

    for at in range(DEAL_PARTS):
        copy_in(at).start()
    for at in range(DEAL_PARTS):
        copy_in(at).wait()
        pairs = range(at * part // 2, (at + 1) * part // 2)
        dealt = [
            dot(pick_ref[...], rows_in[:, 16 * pair : 16 * pair + 16, :].reshape(2 * slots, WIDTH)) for pair in pairs
        ]
        for pair, rows in zip(pairs, dealt):
            rows = rows.astype(bf16)
            rows_out[2 * pair] = rows[:slots]
            rows_out[2 * pair + 1] = rows[slots:]
        for copy in copy_out(at):
            copy.start()
    for at in range(DEAL_PARTS):
        for copy in copy_out(at):
            copy.wait()


def run_deal(pick, region, local):
    slots = region.shape[0]
    count, positions = slots // TILE, local.shape[0] + 1
    return pl.pallas_call(
        deal_kernel,
        in_specs=[pl.BlockSpec(memory_space=pltpu.VMEM)] + [pl.BlockSpec(memory_space=pl.ANY)] * 2,
        out_specs=pl.BlockSpec(memory_space=pl.ANY),
        out_shape=jax.ShapeDtypeStruct((count, positions * TILE, WIDTH), bf16),
        scratch_shapes=[
            pltpu.VMEM((positions, slots, WIDTH), bf16),
            pltpu.VMEM((count, positions * TILE, WIDTH), bf16),
            pltpu.SemaphoreType.DMA((DEAL_PARTS + 1,)),
            pltpu.SemaphoreType.DMA((DEAL_PARTS,)),
        ],
        compiler_params=pltpu.CompilerParams(vmem_limit_bytes=VMEM_LIMIT),
        cost_estimate=took(4),
        name="deal",
    )(pick, region, local)


def run_collect(pick, came):
    count, rows, _ = came.shape
    slots, positions = count * TILE, rows // TILE
    anywhere = pl.BlockSpec(memory_space=pl.ANY)
    return pl.pallas_call(
        collect_kernel,
        in_specs=[pl.BlockSpec(memory_space=pltpu.VMEM), anywhere],
        out_specs=[anywhere] * 2,
        out_shape=[
            jax.ShapeDtypeStruct((slots, WIDTH), bf16),
            jax.ShapeDtypeStruct((positions - 1, slots, WIDTH), bf16),
        ],
        scratch_shapes=[
            pltpu.VMEM((count, rows, WIDTH), bf16),
            pltpu.VMEM((positions, slots, WIDTH), bf16),
            pltpu.SemaphoreType.DMA((DEAL_PARTS,)),
            pltpu.SemaphoreType.DMA((DEAL_PARTS + 1,)),
        ],
        compiler_params=pltpu.CompilerParams(vmem_limit_bytes=VMEM_LIMIT),
        cost_estimate=took(0.3),
        name="collect",
    )(pick, came)


def swap_tiles(tiles_sent, devices):
    count, rows, width = tiles_sent.shape
    share = count * TILE // devices
    if share == TILE:
        return lax.all_to_all(tiles_sent, "dp", split_axis=0, concat_axis=0, tiled=True)
    places = rows // TILE
    sent = tiles_sent.reshape(count, places, TILE, width).transpose(1, 0, 2, 3)
    sent = sent.reshape(places, devices, share, width).transpose(1, 0, 2, 3)
    came = lax.all_to_all(sent, "dp", split_axis=0, concat_axis=0, tiled=True)
    came = came.transpose(1, 0, 2, 3).reshape(places, count, TILE, width)
    return came.transpose(1, 0, 2, 3).reshape(count, rows, width)


def row_maps():
    window = np.arange(TILE)[:, None]
    place = np.arange(WIN_SIDE * WIN_SIDE)[None, :]
    raster = place // WIN_SIDE * (TILE * WIN_SIDE) + window * WIN_SIDE + place % WIN_SIDE
    band = TILE * WIN_SIDE * WIN_SIDE
    spread = np.zeros((TILE * SLOT, band), np.float32)
    spread[window * SLOT + 1 + place, raster] = 1
    gather = np.zeros((band, TILE * SLOT), np.float32)
    gather[raster, window * SLOT + 1 + place] = 1
    place = np.arange(WIN_SIDE * WIN_SIDE + 1)[None, :]
    squeeze = np.zeros(((WIN_SIDE * WIN_SIDE + 1) * TILE, TILE * TALL), np.float32)
    squeeze[place * TILE + window, window * TALL + place] = 1
    return [jnp.asarray(table, bf16) for table in (spread, gather, squeeze, squeeze.T)]


def shards(
    tokens,
    regional,
    pad_mask,
    keep_mask,
    window_slot,
    ln1_gain,
    ln1_bias,
    w_qkv,
    bias_q,
    bias_v,
    w_out,
    bias_out,
    ln2_gain,
    ln2_bias,
    w_fc1,
    bias_fc1,
    w_fc2,
    bias_fc2,
    cot_local,
    cot_regional,
):
    devices = lax.axis_size("dp")
    stages = reduce_stages()
    parts = devices * lax.axis_size("img")
    own_rank = lax.axis_index("dp")
    win_count = regional.shape[1]
    all_windows = window_slot.shape[1]
    slot_of = window_slot[0]
    places = jnp.arange(win_count)
    own_target = lax.dynamic_slice_in_dim(slot_of, own_rank * win_count, win_count) // win_count
    own_place = rank_of(own_target * win_count + places)
    order = jnp.sum(jnp.where(own_place[None, :] == places[:, None], places[None, :], 0), axis=1)
    slot_hit = slot_of[None, :] == (own_rank * win_count + places)[:, None]
    window_here = jnp.sum(jnp.where(slot_hit, jnp.arange(all_windows)[None, :], 0), axis=1)
    here_place = rank_of(window_here)
    deal_row = jnp.arange(2 * win_count)
    row_place = deal_row // (2 * TILE) * TILE + deal_row % TILE
    row_half = deal_row // TILE % 2
    column_hit = row_place[:, None] == jnp.concatenate([here_place, here_place])[None, :]
    pick = (column_hit & (row_half[:, None] == (deal_row // win_count)[None, :])).astype(bf16)
    pick_back = (column_hit & (row_half[:, None] == (deal_row // win_count)[None, :])).T.astype(bf16)
    cot = swap_tiles(
        run_deal(pick, cot_regional[0], jnp.swapaxes(cot_local[0], 0, 1)), devices
    )
    image = own_rank * win_count // REGIONS
    keep = lax.dynamic_slice_in_dim(keep_mask[0], image, 1).astype(f32) / survive
    live = band_to_windows(pad_mask[0], win_count) != 0
    allowed = jnp.concatenate(
        [jnp.ones((win_count, 1), bool), live, jnp.zeros((win_count, SLOT - 1 - live.shape[1]), bool)],
        axis=1,
    )
    window_bias = jnp.broadcast_to(
        jnp.where(allowed, 0.0, -1e30).astype(bf16)[:, :, None], (win_count, SLOT, LANES)
    )
    region_bias = jnp.broadcast_to(
        jnp.where(live[:, 0], 0.0, -1e30).astype(bf16)[:, None], (win_count, LANES)
    )
    spread, gather, squeeze, stretch = row_maps()
    plain, mixed_mask = head_masks()
    gain1, bias1, gain2, bias2 = ln1_gain[None], ln1_bias[None], ln2_gain[None], ln2_bias[None]
    out, qkv, probs, joined, mixed, after, hidden, slope, qkv_r, probs_r, mixed_r = run_forward(
        order, keep, tokens.reshape(REG_SIDE, -1, WIDTH), regional[0], window_bias, region_bias,
        spread, squeeze, plain, mixed_mask, gain1, bias1, w_qkv, bias_q[None], bias_v[None], w_out, bias_out[None],
        gain2, bias2, w_fc1, bias_fc1[None], w_fc2, bias_fc2[None],
    )
    came = swap_tiles(out, devices)
    own = own_share(stages)[None]
    grad_after, grad_mixed, early, early_sent, grad_out, small, row_fc1 = run_back_mlp(
        parts, keep, own, cot, after, mixed, hidden, slope, stretch, gain2, bias2, w_fc1, w_fc2, w_out
    )
    (_, pairs), = stage_moves(stages[0])
    early_came = swap(early_sent, pairs)
    attention = (
        order, keep, own, qkv, probs, joined, grad_mixed, grad_after, plain, mixed_mask, gain1, bias1
    )
    tile_count = win_count // TILE
    xy_stage, (z_stage, *more) = stages[1], stages[2:]
    grad_qkv, *held = run_back_attention(0, ATTENTION_FIRST, *attention)
    early = split_sum([early, early_came], xy_stage)
    held, early, came = lax.optimization_barrier((held, early, came))
    early = add_up(sum_parts(early, xy_stage))
    grad_qkv, late, late_sent, regional_out = run_back_attention(
        ATTENTION_FIRST,
        tile_count - ATTENTION_FIRST,
        *attention,
        held=(*held, grad_qkv),
        ending=(grad_out, order[None], regional[0], qkv_r, probs_r, mixed_r, w_qkv, w_out, small, row_fc1),
        parts=parts,
    )
    late_came = swap(late_sent, pairs)
    grad_qkv, early = lax.optimization_barrier((grad_qkv, early))
    early = sum_parts(split_sum([early], z_stage), z_stage)
    rows = (order, grad_qkv, joined, grad_after, gain1, w_qkv)
    windows = run_back_rows(*rows, 0, ROWS_FIRST)
    windows, late_came = lax.optimization_barrier((windows, late_came))
    late = sum_parts(split_sum([late, late_came], xy_stage), xy_stage)
    windows, early = lax.optimization_barrier((windows, early))
    early = sum_stages(add_up(early), more)
    for stage in reversed(more):
        early = gather_stage(early, stage)
    early = gather_parts(early, z_stage)
    windows = run_back_rows(*rows, ROWS_FIRST, tile_count - ROWS_FIRST, held=windows)
    windows, early, late = lax.optimization_barrier((windows, early, late))
    late = sum_parts(split_sum([add_up(late)], z_stage), z_stage)
    early = jnp.concatenate(early, axis=0)
    moves = stage_moves(xy_stage)
    early = [early] + [swap(early, moves[at][1]) for at in range(2)]
    tokens_out = run_relay(gather, windows)
    tokens_out, came, early, late = lax.optimization_barrier((tokens_out, came, early, late))
    late = sum_stages(add_up(late), more)
    for stage in reversed(more):
        late = gather_stage(late, stage)
    late = gather_parts(late, z_stage)
    (_, across), = moves[2:]
    early_last = swap(early[0], across)
    early = jnp.concatenate(early, axis=0)
    early_far = swap(early, pairs)
    came, early_far, late = lax.optimization_barrier((came, early_far, late))
    late = gather_parts(jnp.concatenate(late, axis=0), xy_stage)
    grad_w_fc1, grad_w_fc2 = run_early_out(own, early, early_far, w_fc1.shape[1])
    out_regional, out_local = run_collect(pick_back, came)
    late_far = [swap(late[0], pairs)]
    grad_w_fc1, grad_w_fc2, out_local, early_last, late, late_far = lax.optimization_barrier(
        (grad_w_fc1, grad_w_fc2, out_local, early_last, late, late_far)
    )
    early_last = [early_last, swap(early_last, pairs)]
    late_far += [swap(piece, pairs) for piece in late[1:]]
    grad_w_qkv, grad_w_out, *vectors, grad_w_fc1, grad_w_fc2 = run_late_out(
        own, late + late_far, early_last, grad_w_fc1, grad_w_fc2
    )
    vectors = [vector[0] for vector in vectors]
    return (
        jnp.swapaxes(out_local, 0, 1)[None],
        out_regional[None],
        tokens_out.reshape(tokens.shape),
        regional_out[None],
        vectors[0],
        vectors[1],
        grad_w_qkv,
        vectors[2],
        vectors[3],
        grad_w_out,
        vectors[4],
        vectors[5],
        vectors[6],
        grad_w_fc1,
        vectors[8],
        grad_w_fc2,
        vectors[7],
    )


def solution(mesh):
    in_specs = (
        P("img", "dp", None, None),
        P("img", "dp", None),
        P("img", "dp", None),
        P("img", None),
        P("img", None),
        P(),
        P(),
        P(),
        P(),
        P(),
        P(),
        P(),
        P(),
        P(),
        P(),
        P(),
        P(),
        P(),
        P("img", "dp", None, None),
        P("img", "dp", None),
    )
    out_specs = (
        P("img", "dp", None, None),
        P("img", "dp", None),
        P("img", "dp", None, None),
        P("img", "dp", None),
        P(),
        P(),
        P(),
        P(),
        P(),
        P(),
        P(),
        P(),
        P(),
        P(),
        P(),
        P(),
        P(),
    )
    return jax.shard_map(shards, mesh=mesh, in_specs=in_specs, out_specs=out_specs, check_vma=False)
```

```python
import functools
import math
import jax
import jax.numpy as jnp
import numpy as np
from jax import lax
from jax.experimental import pallas as pl
from jax.experimental.pallas import tpu as pltpu
from jax.sharding import PartitionSpec as P

HEADS = 16
HDIM = 32
WIN_SIDE = 7
REG_SIDE = 8
REGIONS = 64

norm_eps = 1e-05
survive = 0.9

WIDTH = 512
SLOT = 64
TALL = 56
TILE = 8
GROUP = 4
GROUPS = HEADS // GROUP
TOGETHER = 8
LANES = 128
DEAL_PARTS = 5
ATTENTION_FIRST = 3
ROWS_FIRST = 2
ONES = 16
BACK_CHUNK = 1024
CHUNK = 512
MIB = 1024 * 1024
VMEM_LIMIT = 60 * MIB

f32 = jnp.float32


def took(micros):
    return pl.CostEstimate(flops=int(micros * 1.15e9), bytes_accessed=1_000_000, transcendentals=0)

bf16 = jnp.bfloat16


def dot(left, right):
    return lax.dot_general(left, right, (((1,), (0,)), ((), ())), preferred_element_type=f32)


def dot_nt(left, right):
    return lax.dot_general(left, right, (((1,), (1,)), ((), ())), preferred_element_type=f32)


def head_masks():
    lane_head = np.arange(LANES) // HDIM
    plain = np.repeat(np.arange(GROUP), SLOT)
    mixed = np.repeat(np.array([0, 2, 1, 3]), SLOT)
    return (
        jnp.asarray(plain[:, None] == lane_head[None, :], bf16),
        jnp.asarray(mixed[:, None] == lane_head[None, :], bf16),
    )


def spread_heads(rows, mask):
    return jnp.concatenate([rows] * GROUP, axis=0) * mask


def turn(blocks):
    stacked = jnp.concatenate([blocks[:, :LANES], blocks[:, LANES:]], axis=0)
    turned = stacked.T
    return jnp.concatenate([turned[:SLOT], turned[SLOT:]], axis=1)


def attend_scores(items, plain):
    return [dot_nt(key_rows, spread_heads(queries, plain)) for queries, key_rows, _, _ in items]


def attend_probs(items, scores):
    probs = []
    for rows, (_, _, _, bias) in zip(scores, items):
        rows = rows + bias
        highest = jnp.max(rows, axis=0, keepdims=True)
        weighted = jnp.exp2((rows - highest) * (HDIM**-0.5 * math.log2(math.e)))
        total = jnp.sum(weighted, axis=0, keepdims=True)
        probs.append((weighted * (1.0 / total)).astype(bf16))
    return probs


def attend_mix(items, turned, mixed):
    return [dot(rows, spread_heads(item[2], mixed)) for rows, item in zip(turned, items)]


def attend_back(items, plain, mixed):
    wide = [spread_heads(item[4], plain) for item in items]
    grad_probs = [dot_nt(item[2], rows) for item, rows in zip(items, wide)]
    grad_values = [dot(item[3], rows) for item, rows in zip(items, wide)]
    scores = []
    for rows, item in zip(grad_probs, items):
        soft = item[3].astype(f32)
        weighted = soft * rows
        inner = jnp.sum(weighted, axis=0, keepdims=True)
        scores.append((weighted - soft * inner).astype(bf16))
    turned = [turn(rows) for rows in scores]
    factor = HDIM**-0.5
    grad_keys = [dot(rows, spread_heads(item[0], plain)) * factor for rows, item in zip(scores, items)]
    grad_queries = [dot(rows, spread_heads(item[1], mixed)) * factor for rows, item in zip(turned, items)]
    return list(zip(grad_queries, grad_keys, grad_values))


def normalize(rows):
    centered = rows - jnp.mean(rows, axis=-1, keepdims=True)
    spread = jnp.mean(centered * centered, axis=-1, keepdims=True)
    scale = lax.rsqrt(spread + norm_eps)
    return centered * scale, scale


def normalize_back(grad_unit, unit, scale):
    first = jnp.mean(grad_unit, axis=-1, keepdims=True)
    second = jnp.mean(grad_unit * unit, axis=-1, keepdims=True)
    return scale * (grad_unit - first - unit * second)


def gelu_pair(values):
    below = 0.5 + 0.5 * lax.erf(values * 0.7071067811865476)
    bell = jnp.exp2(values * values * (-0.5 * math.log2(math.e)))
    return values * below, below + values * bell * 0.3989422804014327


def fold_lanes(rows):
    return sum(rows[:, at : at + LANES] for at in range(0, rows.shape[1], LANES))


def column_sum(rows):
    return jnp.sum(rows, axis=0, keepdims=True)


def window_items(qkv_of, bias):
    wide = jnp.concatenate([bias, bias], axis=1).astype(f32)
    return [
        (qkv_of(group), qkv_of(GROUPS + group), qkv_of(2 * GROUPS + group), wide) for group in range(GROUPS)
    ]


def attend_windows_back(windows, plain, mixed):
    items = []
    for qkv_of, probs_of, grad_of, _ in windows:
        for group in range(GROUPS):
            probs = jnp.concatenate([probs_of(2 * group), probs_of(2 * group + 1)], axis=1)
            items.append(
                (qkv_of(group), qkv_of(GROUPS + group), qkv_of(2 * GROUPS + group), probs, grad_of(group))
            )
    grads = attend_back(items, plain, mixed)
    for at, (_, _, _, put_grad) in enumerate(windows):
        for group in range(GROUPS):
            for part in range(3):
                put_grad(part * GROUPS + group, grads[at * GROUPS + group][part].astype(bf16))


def forward_kernel(
    order_ref, keep_ref,
    tokens_ref, regional_ref, window_bias_ref, region_bias_ref, spread_ref, squeeze_ref,
    plain_ref, mixed_mask_ref, gain1_ref, bias1_ref, w_qkv_ref, bias_q_ref, bias_v_ref, w_out_ref, bias_out_ref,
    gain2_ref, bias2_ref, w_fc1_ref, bias_fc1_ref, w_fc2_ref, bias_fc2_ref,
    out_ref, qkv_ref, probs_ref, joined_ref, mixed_ref, after_ref, hidden_ref, slope_ref,
    qkv_r_ref, probs_r_ref, mixed_r_ref,
    windows, normed, mixed_rows, joined_rows,
):
    step = pl.program_id(0)
    last = pl.num_programs(0) - 1
    keep = keep_ref[0]
    plain = plain_ref[...]
    mixed = mixed_mask_ref[...]
    count = TILE * TALL
    chunks = [slice(at, at + CHUNK) for at in range(0, w_fc1_ref.shape[1], CHUNK)]
    tile = {}

    @pl.when(step == 0)
    def first():
        region = regional_ref[...].astype(f32)
        unit, _ = normalize(region)
        region_norm = (unit * gain1_ref[...] + bias1_ref[...]).astype(bf16)
        region_qkv = dot(region_norm, w_qkv_ref[...])
        region_qkv = jnp.concatenate(
            [
                region_qkv[:, :WIDTH] + bias_q_ref[...],
                region_qkv[:, WIDTH : 2 * WIDTH],
                region_qkv[:, 2 * WIDTH :] + bias_v_ref[...],
            ],
            axis=1,
        ).astype(bf16)
        for at in range(3 * GROUPS):
            qkv_r_ref[at] = region_qkv[:, at * LANES : (at + 1) * LANES]
        items = window_items(lambda at: region_qkv[:, at * LANES : (at + 1) * LANES], region_bias_ref[...])
        probs = attend_probs(items, attend_scores(items, plain))
        for group in range(GROUPS):
            probs_r_ref[2 * group] = probs[group][:, :LANES]
            probs_r_ref[2 * group + 1] = probs[group][:, LANES:]
        outs = attend_mix(items, [turn(rows) for rows in probs], mixed)
        region_mixed = jnp.concatenate(outs, axis=1).astype(bf16)
        mixed_r_ref[...] = region_mixed
        region_mid = region + keep * (dot(region_mixed, w_out_ref[...]) + bias_out_ref[...])
        region_mid = region_mid.astype(bf16)
        row = lax.broadcasted_iota(jnp.int32, (TILE * SLOT, REGIONS), 0)
        column = lax.broadcasted_iota(jnp.int32, (TILE * SLOT, REGIONS), 1)

        def relay(line, carry):
            pick = (row == (column - line * TILE) * SLOT).astype(bf16)
            rows = dot(spread_ref[...], tokens_ref[line]) + dot(pick, region_mid)
            windows[pl.ds(line * TILE, TILE)] = rows.reshape(TILE, SLOT, WIDTH)
            return carry

        lax.fori_loop(0, REG_SIDE, relay, 0)


    def norm_rows():
        for at in range(TILE):
            rows = windows[order_ref[step * TILE + at]]
            joined_ref[at] = rows.astype(bf16)
            unit, _ = normalize(rows)
            normed[at * SLOT : (at + 1) * SLOT] = (unit * gain1_ref[...] + bias1_ref[...]).astype(bf16)

    def project(part):
        cols = slice(part * WIDTH, (part + 1) * WIDTH)
        qkv = dot(normed[...], w_qkv_ref[:, cols])
        if part != 1:
            qkv = qkv + (bias_q_ref if part == 0 else bias_v_ref)[...]
        qkv = qkv.astype(bf16).reshape(TILE, SLOT, WIDTH)
        for group in range(GROUPS):
            qkv_ref[:, part * GROUPS + group] = qkv[:, :, group * LANES : (group + 1) * LANES]

    def score(half):
        items = []
        for at in half:
            bias = window_bias_ref[order_ref[step * TILE + at]]
            items += window_items(lambda place, at=at: qkv_ref[at, place], bias)
        return items, attend_scores(items, plain)

    def soften(half, items, scores):
        probs = attend_probs(items, scores)
        for at, rows in enumerate(probs):
            window, group = half[at // GROUPS], at % GROUPS
            probs_ref[window, 2 * group] = rows[:, :LANES]
            probs_ref[window, 2 * group + 1] = rows[:, LANES:]
        return [turn(rows) for rows in probs]

    def mix(half, items, turned):
        outs = attend_mix(items, turned, mixed)
        for at, rows in enumerate(outs):
            window, group = half[at // GROUPS], at % GROUPS
            mixed_rows[window, :, group * LANES : (group + 1) * LANES] = rows

    def keep_joined():
        for at in range(TILE):
            joined_rows[at] = joined_ref[at].astype(f32)


    def branch():
        mixed_low = mixed_rows[:, :TALL].reshape(count, WIDTH).astype(bf16)
        mixed_ref[...] = mixed_low
        after = joined_rows[:, :TALL].reshape(count, WIDTH) + keep * (
            dot(mixed_low, w_out_ref[...]) + bias_out_ref[...]
        )
        after_ref[...] = after

    def norm_after():
        unit, _ = normalize(after_ref[...])
        tile["norm"] = (unit * gain2_ref[...] + bias2_ref[...]).astype(bf16)
        tile["total"] = jnp.zeros((count, WIDTH), f32)

    def widen(at):
        tile[at] = dot(tile["norm"], w_fc1_ref[:, chunks[at]])

    def bend(at):
        cols = chunks[at]
        hidden, slope = gelu_pair(tile[at] + bias_fc1_ref[:, cols])
        tile[at] = hidden.astype(bf16)
        hidden_ref[:, cols] = tile[at]
        slope_ref[:, cols] = slope.astype(bf16)

    def narrow(at):
        tile["total"] = tile["total"] + dot(tile[at], w_fc2_ref[chunks[at], :])

    def send():
        result = after_ref[...] + keep * (tile["total"] + bias_fc2_ref[...])
        out_ref[0] = dot(squeeze_ref[...], result.astype(bf16)).astype(bf16)

    halves = [list(range(TILE // 2)), list(range(TILE // 2, TILE))]

    @pl.when(step == 0)
    def attention_only():
        norm_rows()
        for part in range(3):
            project(part)
        scored = [score(half) for half in halves]
        turned = [soften(half, *pair) for half, pair in zip(halves, scored)]
        for half, pair, rows in zip(halves, scored, turned):
            mix(half, pair[0], rows)
        keep_joined()

    @pl.when((step > 0) & (step < last))
    def both():
        branch()
        norm_rows()
        project(0)
        norm_after()
        project(1)
        widen(0)
        project(2)
        widen(1)
        bend(0)
        scored = [score(halves[0]), None]
        narrow(0)
        bend(1)
        widen(2)
        scored[1] = score(halves[1])
        turned = [soften(halves[0], *scored[0]), None]
        narrow(1)
        widen(3)
        bend(2)
        mix(halves[0], scored[0][0], turned[0])
        turned[1] = soften(halves[1], *scored[1])
        narrow(2)
        bend(3)
        mix(halves[1], scored[1][0], turned[1])
        narrow(3)
        send()
        keep_joined()

    @pl.when(step == last)
    def feed_only():
        branch()
        norm_after()
        widen(0)
        for at in range(len(chunks)):
            if at + 1 < len(chunks):
                widen(at + 1)
            bend(at)
            narrow(at)
        send()


def whole(shape):
    return pl.BlockSpec(shape, lambda step, *_: (0,) * len(shape))


def tiles(shape):
    return pl.BlockSpec(shape, lambda step, *_: (step,) + (0,) * (len(shape) - 1))


def run_forward(order, keep, tokens, regional, window_bias, region_bias, spread, squeeze, plain, mixed,
                gain1, bias1, w_qkv, bias_q, bias_v, w_out, bias_out, gain2, bias2, w_fc1, bias_fc1, w_fc2, bias_fc2):
    windows = regional.shape[0]
    steps = windows // TILE
    rows = TILE * TALL
    hidden = w_fc1.shape[1]
    compact = squeeze.shape[0]
    args = (tokens, regional, window_bias, region_bias, spread, squeeze, plain, mixed,
            gain1, bias1, w_qkv, bias_q, bias_v, w_out, bias_out, gain2, bias2, w_fc1, bias_fc1, w_fc2, bias_fc2)
    def ahead(shape):
        return pl.BlockSpec(
            shape, lambda step, *_: (jnp.minimum(step, steps - 1),) + (0,) * (len(shape) - 1)
        )

    def behind(shape):
        return pl.BlockSpec(shape, lambda step, *_: (jnp.maximum(step - 1, 0),) + (0,) * (len(shape) - 1))

    outs = [
        ((steps, compact, WIDTH), bf16, behind((1, compact, WIDTH))),
        ((windows, 3 * GROUPS, SLOT, LANES), bf16, ahead((TILE, 3 * GROUPS, SLOT, LANES))),
        ((windows, 2 * GROUPS, SLOT, LANES), bf16, ahead((TILE, 2 * GROUPS, SLOT, LANES))),
        ((windows, SLOT, WIDTH), bf16, ahead((TILE, SLOT, WIDTH))),
        ((steps * rows, WIDTH), bf16, behind((rows, WIDTH))),
        ((steps * rows, WIDTH), f32, behind((rows, WIDTH))),
        ((steps * rows, hidden), bf16, behind((rows, hidden))),
        ((steps * rows, hidden), bf16, behind((rows, hidden))),
    ]
    fixed = [
        ((3 * GROUPS, REGIONS, LANES), bf16),
        ((2 * GROUPS, REGIONS, LANES), bf16),
        ((REGIONS, WIDTH), bf16),
    ]
    return pl.pallas_call(
        forward_kernel,
        grid_spec=pltpu.PrefetchScalarGridSpec(
            num_scalar_prefetch=2,
            grid=(steps + 1,),
            in_specs=[whole(a.shape) for a in args],
            out_specs=[spec for _, _, spec in outs] + [whole(s) for s, _ in fixed],
            scratch_shapes=[
                pltpu.VMEM((windows, SLOT, WIDTH), f32),
                pltpu.VMEM((TILE * SLOT, WIDTH), bf16),
                pltpu.VMEM((TILE, SLOT, WIDTH), f32),
                pltpu.VMEM((TILE, SLOT, WIDTH), f32),
            ],
        ),
        out_shape=[jax.ShapeDtypeStruct(s, d) for s, d, _ in outs]
        + [jax.ShapeDtypeStruct(s, d) for s, d in fixed],
        compiler_params=pltpu.CompilerParams(
            dimension_semantics=("arbitrary",), vmem_limit_bytes=62 * MIB
        ),
        cost_estimate=took(61),
        name="forward",
    )(order, keep, *args)


def put_shares(own, keep_ref, send_ref, chunk_of):
    half = keep_ref.shape[0]

    def fill(refs):
        for which, ref in enumerate(refs):
            for at in range(half):
                ref[at ^ (own % half)] = chunk_of(which * half + at)

    @pl.when(own < half)
    def low():
        fill((keep_ref, send_ref))

    @pl.when(own >= half)
    def high():
        fill((send_ref, keep_ref))


def back_mlp_kernel(
    keep_ref, own_ref, cot_ref, after_ref, mixed_ref, hidden_ref, slope_ref, stretch_ref,
    gain2_ref, bias2_ref, w_fc1_ref, w_fc2_ref, w_out_ref,
    grad_after_ref, grad_mixed_ref, stay_ref, send_ref, grad_out_ref, small_ref, bias_row_ref,
    sum_fc1, sum_fc2, sum_out, sums, sum_hidden, early_rows,
):
    step = pl.program_id(0)
    last = pl.num_programs(0) - 1
    keep = keep_ref[0]

    @pl.when(step == 0)
    def clear():
        for ref in (sum_fc1, sum_fc2, sum_out, sums, sum_hidden):
            ref[...] = jnp.zeros_like(ref)

    unit, scale = normalize(after_ref[...])
    mlp_norm = (unit * gain2_ref[...] + bias2_ref[...]).astype(bf16)
    norm_turned = mlp_norm.T
    cot = dot(stretch_ref[...], cot_ref[0])
    grad_mlp = (keep * cot).astype(bf16)
    grad_turned = grad_mlp.T
    sums[0:1] += column_sum(grad_mlp.astype(f32))
    grad_norm = jnp.zeros(after_ref.shape, f32)
    chunks = [slice(at, at + BACK_CHUNK) for at in range(0, w_fc1_ref.shape[1], BACK_CHUNK)]
    ahead = dot_nt(grad_mlp, w_fc2_ref[chunks[0], :])
    for at, cols in enumerate(chunks):
        grad_hidden = ahead
        if at + 1 < len(chunks):
            ahead = dot_nt(grad_mlp, w_fc2_ref[chunks[at + 1], :])
        sum_fc2[:, cols] += dot(grad_turned, hidden_ref[:, cols])
        grad_pre = (slope_ref[:, cols].astype(f32) * grad_hidden).astype(bf16)
        sum_fc1[:, cols] += dot(norm_turned, grad_pre)
        sum_hidden[0:1, cols] += column_sum(grad_pre.astype(f32))
        grad_norm = grad_norm + dot_nt(grad_pre, w_fc1_ref[:, cols])
    sums[1:2] += column_sum(grad_norm * unit)
    sums[2:3] += column_sum(grad_norm)
    grad_after = cot + normalize_back(grad_norm * gain2_ref[...], unit, scale)
    grad_after_ref[...] = grad_after
    grad_branch = (keep * grad_after).astype(bf16)
    sums[3:4] += column_sum(grad_branch.astype(f32))
    sum_out[...] += dot(mixed_ref[...].T, grad_branch)
    grad_mixed = dot_nt(grad_branch, w_out_ref[...]).reshape(TILE, TALL, WIDTH)
    empty = jnp.zeros((TILE, SLOT - TALL, WIDTH), f32)
    grad_mixed = jnp.concatenate([grad_mixed, empty], axis=1).astype(bf16)
    for group in range(GROUPS):
        grad_mixed_ref[:, group] = grad_mixed[:, :, group * LANES : (group + 1) * LANES]

    @pl.when(step == last)
    def finish():
        for at in range(4):
            cols = slice(at * WIDTH, (at + 1) * WIDTH)
            early_rows[cols, :] = sum_fc1[:, cols].astype(bf16)
            early_rows[4 * WIDTH + at * WIDTH : 4 * WIDTH + (at + 1) * WIDTH, :] = (
                sum_fc2[:, cols].T.astype(bf16)
            )
        rows = stay_ref.shape[1]
        put_shares(
            own_ref[0], stay_ref, send_ref, lambda at: early_rows[at * rows : (at + 1) * rows, :]
        )
        grad_out_ref[...] = sum_out[...]
        small_ref[...] = sums[...]
        bias_row_ref[...] = sum_hidden[...]


def run_back_mlp(parts, keep, own, cot, after, mixed, hidden, slope, stretch, gain2, bias2, w_fc1, w_fc2, w_out):
    steps, compact, _ = cot.shape
    rows = TILE * TALL
    units = w_fc1.shape[1]
    tiled = [(1, compact, WIDTH), (rows, WIDTH), (rows, WIDTH), (rows, units), (rows, units)]
    fixed = (stretch, gain2, bias2, w_fc1, w_fc2, w_out)
    outs = [
        ((steps * rows, WIDTH), f32, (rows, WIDTH)),
        ((steps * TILE, GROUPS, SLOT, LANES), bf16, (TILE, GROUPS, SLOT, LANES)),
    ]
    share = (parts // 2, 2 * units // parts, WIDTH)
    whole_outs = [(share, bf16), (share, bf16), ((WIDTH, WIDTH), f32), ((8, WIDTH), f32), ((8, units), f32)]
    return pl.pallas_call(
        back_mlp_kernel,
        grid_spec=pltpu.PrefetchScalarGridSpec(
            num_scalar_prefetch=2,
            grid=(steps,),
            in_specs=[tiles(b) for b in tiled] + [whole(a.shape) for a in fixed],
            out_specs=[tiles(block) for _, _, block in outs] + [whole(s) for s, _ in whole_outs],
            scratch_shapes=[
                pltpu.VMEM((WIDTH, units), f32),
                pltpu.VMEM((WIDTH, units), f32),
                pltpu.VMEM((WIDTH, WIDTH), f32),
                pltpu.VMEM((8, WIDTH), f32),
                pltpu.VMEM((8, units), f32),
                pltpu.VMEM((2 * units, WIDTH), bf16),
            ],
        ),
        out_shape=[jax.ShapeDtypeStruct(s, d) for s, d, _ in outs]
        + [jax.ShapeDtypeStruct(s, d) for s, d in whole_outs],
        compiler_params=pltpu.CompilerParams(
            dimension_semantics=("arbitrary",), vmem_limit_bytes=VMEM_LIMIT
        ),
        cost_estimate=took(55),
        name="back_mlp",
    )(keep, own, cot, after, mixed, hidden, slope, *fixed)


def back_attention_kernel(
    begin, last, order_ref, keep_ref, own_ref,
    qkv_ref, probs_ref, joined_ref, grad_mixed_ref, grad_after_ref,
    plain_ref, mixed_mask_ref, gain1_ref, bias1_ref, *refs,
):
    first = begin == 0
    held_in = ()
    if not first:
        held_in, refs = refs[:3], refs[4:]
    if last:
        ending, refs = refs[:10], refs[10:]
        grad_out_ref, order_row_ref, regional_ref, qkv_r_ref, probs_r_ref, mixed_r_ref = ending[:6]
        w_qkv_ref, w_out_ref, sums_mlp_ref, row_fc1_ref = ending[6:]
        grad_qkv_ref, stay_ref, send_ref, regional_out_ref, sum_qkv, heads, after_heads, late_rows = refs
    else:
        grad_qkv_ref, sum_qkv, heads, after_heads = refs
    step = pl.program_id(0)
    plain = plain_ref[...]
    mixed = mixed_mask_ref[...]

    @pl.when(step == 0)
    def open_sums():
        for at, ref in enumerate((sum_qkv, heads, after_heads)):
            ref[...] = jnp.zeros_like(ref) if first else held_in[at][...]

    def some(batch, carry):
        def window(at):
            rows = pl.ds(pl.multiple_of(at * SLOT, SLOT), SLOT)

            def put_grad(place, values):
                grad_qkv_ref[rows, place * LANES : (place + 1) * LANES] = values

            return (
                lambda place: qkv_ref[at, place],
                lambda place: probs_ref[at, place],
                lambda place: grad_mixed_ref[at, place],
                put_grad,
            )

        attend_windows_back([window(batch * TOGETHER + at) for at in range(TOGETHER)], plain, mixed)
        return carry

    lax.fori_loop(0, TILE // TOGETHER, some, 0)
    joined = joined_ref[...].reshape(TILE * SLOT, WIDTH).astype(f32)
    unit, _ = normalize(joined)
    normed = (unit * gain1_ref[...] + bias1_ref[...]).astype(bf16)
    turned = jnp.concatenate([normed.T, jnp.ones((ONES, TILE * SLOT), bf16)], axis=0)
    sum_qkv[...] += dot(turned, grad_qkv_ref[...])
    rows = pl.ds(pl.multiple_of((step + begin) * TILE, TILE), TILE)
    heads[rows, : 3 * WIDTH] = jnp.concatenate(
        [grad_qkv_ref[at * SLOT : at * SLOT + 16].astype(f32)[:1] for at in range(TILE)], axis=0
    )
    heads[rows, 3 * WIDTH :] = jnp.concatenate([joined_ref[at, :16].astype(f32)[:1] for at in range(TILE)], axis=0)
    after_heads[rows] = jnp.concatenate(
        [grad_after_ref[at * TALL : at * TALL + 1] for at in range(TILE)], axis=0
    )
    if not last:
        return

    @pl.when(step == pl.num_programs(0) - 1)
    def finish():
        keep = keep_ref[0]
        gain1 = gain1_ref[...]
        grad_normed = dot_nt(heads[:, : 3 * WIDTH].astype(bf16), w_qkv_ref[...])
        unit, scale = normalize(heads[:, 3 * WIDTH :])
        grad_mid = after_heads[...] + normalize_back(grad_normed * gain1, unit, scale)
        windows = grad_mid.shape[0]
        raster = lax.broadcasted_iota(jnp.int32, (windows, windows), 0)
        came = dot((raster == order_row_ref[...]).astype(bf16), grad_mid.astype(bf16))
        grad_branch = (keep * came).astype(bf16)
        grad_mixed = dot_nt(grad_branch, w_out_ref[...]).astype(bf16)
        parts = {}
        attend_windows_back(
            [
                (
                    lambda place: qkv_r_ref[place],
                    lambda place: probs_r_ref[place],
                    lambda place: grad_mixed[:, place * LANES : (place + 1) * LANES],
                    parts.__setitem__,
                )
            ],
            plain,
            mixed,
        )
        grad_qkv_r = jnp.concatenate([parts[place] for place in range(3 * GROUPS)], axis=1)
        unit_r, scale_r = normalize(regional_ref[...].astype(f32))
        normed_r = (unit_r * gain1 + bias1_ref[...]).astype(bf16)
        total = sum_qkv[:WIDTH] + dot(normed_r.T, grad_qkv_r)
        columns = sum_qkv[WIDTH : WIDTH + 1] + column_sum(grad_qkv_r.astype(f32))
        for part in range(3):
            cols = slice(part * WIDTH, (part + 1) * WIDTH)
            late_rows[cols, :] = total[:, cols].astype(bf16)
        late_rows[3 * WIDTH :, :] = (
            grad_out_ref[...] + dot(mixed_r_ref[...].T, grad_branch)
        ).astype(bf16)
        weights = w_qkv_ref[...].astype(f32)
        by_bias = weights * columns
        by_gain = weights * total
        turned_bias = fold_lanes(by_bias).T
        turned_gain = fold_lanes(by_gain).T
        grad_bias1 = column_sum(turned_bias)
        grad_gain1 = (column_sum(turned_gain) - bias1_ref[...] * grad_bias1) / gain1
        small = [
            grad_gain1,
            grad_bias1,
            columns[:, :WIDTH],
            columns[:, 2 * WIDTH :],
            sums_mlp_ref[3:4] + column_sum(grad_branch.astype(f32)),
            sums_mlp_ref[1:2],
            sums_mlp_ref[2:3],
            sums_mlp_ref[0:1],
        ]
        units = row_fc1_ref.shape[1] // WIDTH
        more = [row_fc1_ref[0:1, at * WIDTH : (at + 1) * WIDTH] for at in range(units)]
        more.append(jnp.zeros((8 - units, WIDTH), f32))
        share = stay_ref.shape[1] - 8

        def chunk_of(part):
            extra = jnp.zeros((8, WIDTH), f32)
            if part < 2:
                extra = jnp.concatenate(more if part else small, axis=0)
            rows = late_rows[part * share : (part + 1) * share]
            return jnp.concatenate([rows, extra.astype(bf16)], axis=0)

        put_shares(own_ref[0], stay_ref, send_ref, chunk_of)
        grad_normed_r = dot_nt(grad_qkv_r, w_qkv_ref[...])
        regional_out_ref[...] = (
            came + normalize_back(grad_normed_r * gain1, unit_r, scale_r)
        ).astype(bf16)


def run_back_attention(begin, count, order, keep, own, qkv, probs, joined, grad_mixed, grad_after, plain, mixed, gain1,
                       bias1, held=None, ending=None, parts=1):
    windows = qkv.shape[0]
    steps = windows // TILE
    rows = TILE * TALL

    def tile(shape):
        return pl.BlockSpec(shape, lambda step, *_: (step + begin,) + (0,) * (len(shape) - 1))

    tiled = [
        (TILE, 3 * GROUPS, SLOT, LANES),
        (TILE, 2 * GROUPS, SLOT, LANES),
        (TILE, SLOT, WIDTH),
        (TILE, GROUPS, SLOT, LANES),
        (rows, WIDTH),
    ]
    fixed = [plain, mixed, gain1, bias1]
    in_specs = [tile(b) for b in tiled] + [whole(a.shape) for a in fixed]
    args = [qkv, probs, joined, grad_mixed, grad_after] + fixed
    aliases = {}
    if held is not None:
        in_specs += [whole(a.shape) for a in held[:3]] + [pl.BlockSpec(memory_space=pl.ANY)]
        args += list(held)
        aliases = {3 + len(args) - 1: 0}
    if ending is not None:
        in_specs += [whole(a.shape) for a in ending]
        args += list(ending)
    held_shapes = [(WIDTH + ONES, 3 * WIDTH), (windows, 4 * WIDTH), (windows, WIDTH)]
    outs = [((steps * TILE * SLOT, 3 * WIDTH), bf16, tile((TILE * SLOT, 3 * WIDTH)))]
    scratch = []
    late_shape = (parts // 2, 4 * WIDTH // parts + 8, WIDTH)
    if ending is None:
        outs += [(s, f32, whole(s)) for s in held_shapes]
    else:
        outs += [
            (late_shape, bf16, whole(late_shape)),
            (late_shape, bf16, whole(late_shape)),
            ((windows, WIDTH), bf16, whole((windows, WIDTH))),
        ]
        scratch = [pltpu.VMEM(s, f32) for s in held_shapes] + [pltpu.VMEM((4 * WIDTH, WIDTH), bf16)]
    return pl.pallas_call(
        functools.partial(back_attention_kernel, begin, ending is not None),
        grid_spec=pltpu.PrefetchScalarGridSpec(
            num_scalar_prefetch=3,
            grid=(count,),
            in_specs=in_specs,
            out_specs=[spec for _, _, spec in outs],
            scratch_shapes=scratch,
        ),
        out_shape=[jax.ShapeDtypeStruct(s, d) for s, d, _ in outs],
        input_output_aliases=aliases,
        compiler_params=pltpu.CompilerParams(
            dimension_semantics=("arbitrary",), vmem_limit_bytes=VMEM_LIMIT
        ),
        cost_estimate=took(5 * count),
        name="back_attention",
    )(order, keep, own, *args)


def back_rows_kernel(begin, order_ref, grad_qkv_ref, joined_ref, grad_after_ref, gain1_ref, w_qkv_ref, *refs):
    windows_ref, rows_low, done = refs[-3:]
    step = pl.program_id(0)

    def copies(at_step):
        places = [order_ref[(begin + at_step) * TILE + at] for at in range(TILE)]
        return [
            pltpu.make_async_copy(rows_low.at[at], windows_ref.at[place], done.at[at])
            for at, place in enumerate(places)
        ]

    unit, scale = normalize(joined_ref[...].astype(f32).reshape(TILE * SLOT, WIDTH))
    grad_normed = dot_nt(grad_qkv_ref[...], w_qkv_ref[...])
    grad_in = normalize_back(grad_normed * gain1_ref[...], unit, scale)

    @pl.when(step > 0)
    def drain():
        for copy in copies(step - 1):
            copy.wait()

    empty = jnp.zeros((SLOT - TALL, WIDTH), f32)
    for at in range(TILE):
        rows = grad_in[at * SLOT : at * SLOT + TALL] + grad_after_ref[at * TALL : (at + 1) * TALL]
        rows_low[at] = jnp.concatenate([rows, empty], axis=0).astype(bf16)
    for copy in copies(step):
        copy.start()

    @pl.when(step == pl.num_programs(0) - 1)
    def finish():
        for copy in copies(step):
            copy.wait()


def run_back_rows(order, grad_qkv, joined, grad_after, gain1, w_qkv, begin, count, held=None):
    windows = joined.shape[0]

    def tile(shape):
        return pl.BlockSpec(shape, lambda step, *_: (step + begin,) + (0,) * (len(shape) - 1))

    tiled = [(TILE * SLOT, 3 * WIDTH), (TILE, SLOT, WIDTH), (TILE * TALL, WIDTH)]
    fixed = [gain1, w_qkv]
    in_specs = [tile(b) for b in tiled] + [whole(a.shape) for a in fixed]
    args = [grad_qkv, joined, grad_after] + fixed
    aliases = {}
    if held is not None:
        in_specs.append(pl.BlockSpec(memory_space=pl.ANY))
        args.append(held)
        aliases = {len(args): 0}
    return pl.pallas_call(
        functools.partial(back_rows_kernel, begin),
        grid_spec=pltpu.PrefetchScalarGridSpec(
            num_scalar_prefetch=1,
            grid=(count,),
            in_specs=in_specs,
            out_specs=pl.BlockSpec(memory_space=pl.ANY),
            scratch_shapes=[pltpu.VMEM((TILE, SLOT, WIDTH), bf16), pltpu.SemaphoreType.DMA((TILE,))],
        ),
        out_shape=jax.ShapeDtypeStruct((windows, SLOT, WIDTH), bf16),
        input_output_aliases=aliases,
        compiler_params=pltpu.CompilerParams(
            dimension_semantics=("arbitrary",), vmem_limit_bytes=VMEM_LIMIT
        ),
        cost_estimate=took(2.5 * count),
        name="back_rows",
    )(order, *args)


def relay_kernel(gather_ref, windows_ref, tokens_out_ref):
    for line in range(tokens_out_ref.shape[0]):
        rows = windows_ref[line * TILE : (line + 1) * TILE].reshape(TILE * SLOT, WIDTH)
        tokens_out_ref[line] = dot(gather_ref[...], rows).astype(bf16)


def run_relay(gather, windows):
    lines = windows.shape[0] // TILE
    return pl.pallas_call(
        relay_kernel,
        grid=(lines // 2,),
        in_specs=[whole(gather.shape), tiles((2 * TILE, SLOT, WIDTH))],
        out_specs=tiles((2, gather.shape[0], WIDTH)),
        out_shape=jax.ShapeDtypeStruct((lines, gather.shape[0], WIDTH), bf16),
        compiler_params=pltpu.CompilerParams(
            dimension_semantics=("arbitrary",), vmem_limit_bytes=VMEM_LIMIT
        ),
        cost_estimate=took(0.3),
        name="relay",
    )(gather, windows)


def widen_early(own, pieces, first, fc1_ref, fc2_ref, wide, done):
    half = 4

    def copies(place, slot):
        block = place ^ first
        columns = pl.ds(pl.multiple_of(block % half * WIDTH, WIDTH), WIDTH)
        copy_first = pltpu.make_async_copy(wide.at[slot], fc1_ref.at[:, columns], done.at[slot])
        copy_second = pltpu.make_async_copy(wide.at[slot], fc2_ref.at[columns, :], done.at[slot])
        return block, copy_first, copy_second

    for slot, (place, piece, low) in enumerate(pieces):
        share = piece.shape[1]
        per = WIDTH // share
        for chunk in range(per):
            row = pl.multiple_of((chunk ^ (own % per)) * share, share)
            wide[slot, pl.ds(row, share)] = piece[low + chunk].astype(f32)
        block, copy_first, copy_second = copies(place, slot)

        @pl.when(block < half)
        def start_first(copy=copy_first):
            copy.start()

        @pl.when(block >= half)
        def start_second(copy=copy_second):
            copy.start()

    def finish():
        for slot, (place, _, _) in enumerate(pieces):
            block, copy_first, copy_second = copies(place, slot)

            @pl.when(block < half)
            def wait_first(copy=copy_first):
                copy.wait()

            @pl.when(block >= half)
            def wait_second(copy=copy_second):
                copy.wait()

    return finish


def early_out_kernel(own_ref, near_ref, far_ref, fc1_ref, fc2_ref, wide, done):
    own = own_ref[0]
    per = near_ref.shape[0] // 3
    pieces = [(4 * half + at, ref, at * per) for half, ref in enumerate((near_ref, far_ref)) for at in range(3)]
    widen_early(own, pieces, own // per, fc1_ref, fc2_ref, wide, done)()


def run_early_out(own, near, far, units):
    return pl.pallas_call(
        early_out_kernel,
        in_specs=[pl.BlockSpec(memory_space=pltpu.SMEM)] + [pl.BlockSpec(memory_space=pltpu.VMEM)] * 2,
        out_specs=[pl.BlockSpec(memory_space=pl.ANY)] * 2,
        out_shape=[
            jax.ShapeDtypeStruct((WIDTH, units), f32),
            jax.ShapeDtypeStruct((units, WIDTH), f32),
        ],
        scratch_shapes=[pltpu.VMEM((6, WIDTH, WIDTH), f32), pltpu.SemaphoreType.DMA((6,))],
        compiler_params=pltpu.CompilerParams(vmem_limit_bytes=20 * MIB),
        cost_estimate=took(0.3),
        name="early_out",
    )(own, near, far)


def late_out_kernel(places, own_ref, *refs):
    pieces, refs = refs[:8], refs[8:]
    early, refs = refs[: len(places)], refs[len(places) + 2 :]
    (qkv_ref, out_ref), small_refs, (fc1_ref, fc2_ref, wide, wide_early, done, done_early) = refs[:2], refs[2:11], refs[11:]
    per, share, _ = pieces[0].shape
    share -= 8
    own = own_ref[0]
    count = len(pieces)
    height = per * share
    split = WIDTH // height
    finish = widen_early(
        own,
        [(place, piece, 0) for place, piece in zip(places, early)],
        own // early[0].shape[0],
        fc1_ref,
        fc2_ref,
        wide_early,
        done_early,
    )

    def copy_first(block):
        rows = pl.ds(pl.multiple_of(block % split * height, height), height)
        columns = pl.ds(pl.multiple_of(block // split * WIDTH, WIDTH), WIDTH)
        return pltpu.make_async_copy(wide.at[block], qkv_ref.at[rows, columns], done.at[block])

    def copy_second(block):
        rows = pl.ds(pl.multiple_of((block - 3 * split) * height, height), height)
        return pltpu.make_async_copy(wide.at[block], out_ref.at[rows, :], done.at[block])

    for at, piece in enumerate(pieces):
        block = at ^ (own // per)
        for chunk in range(per):
            row = pl.multiple_of((chunk ^ (own % per)) * share, share)
            wide[block, pl.ds(row, share)] = piece[chunk][:share].astype(f32)

        @pl.when(block < 3 * split)
        def first(block=block):
            copy_first(block).start()

        @pl.when(block >= 3 * split)
        def second(block=block):
            copy_second(block).start()

        @pl.when(block == 0)
        def vectors(piece=piece):
            lines = piece[own % per][share:].astype(f32)
            for line in range(8):
                small_refs[line][...] = lines[line : line + 1]
            lines = piece[1 ^ (own % per)][share:].astype(f32)
            for line in range(small_refs[8].shape[1] // WIDTH):
                small_refs[8][:, line * WIDTH : (line + 1) * WIDTH] = lines[line : line + 1]

    for block in range(count):
        (copy_first if block < 3 * split else copy_second)(block).wait()
    finish()


def run_late_out(own, pieces, early, grad_w_fc1, grad_w_fc2):
    places = (3, 7)
    count = len(pieces)
    per, share, _ = pieces[0].shape
    units = grad_w_fc1.shape[1]
    anywhere = pl.BlockSpec(memory_space=pl.ANY)
    kept = pl.BlockSpec(memory_space=pltpu.VMEM)
    inputs = [own, *pieces, *early, grad_w_fc1, grad_w_fc2]
    return pl.pallas_call(
        functools.partial(late_out_kernel, places),
        in_specs=[pl.BlockSpec(memory_space=pltpu.SMEM)] + [kept] * (count + len(places)) + [anywhere] * 2,
        out_specs=[anywhere] * 2 + [kept] * 9 + [anywhere] * 2,
        out_shape=[
            jax.ShapeDtypeStruct((WIDTH, 3 * WIDTH), f32),
            jax.ShapeDtypeStruct((WIDTH, WIDTH), f32),
            *[jax.ShapeDtypeStruct((1, WIDTH), f32)] * 8,
            jax.ShapeDtypeStruct((1, units), f32),
            jax.ShapeDtypeStruct((WIDTH, units), f32),
            jax.ShapeDtypeStruct((units, WIDTH), f32),
        ],
        input_output_aliases={len(inputs) - 2: 11, len(inputs) - 1: 12},
        scratch_shapes=[
            pltpu.VMEM((count, per * (share - 8), WIDTH), f32),
            pltpu.VMEM((len(places), WIDTH, WIDTH), f32),
            pltpu.SemaphoreType.DMA((count,)),
            pltpu.SemaphoreType.DMA((len(places),)),
        ],
        compiler_params=pltpu.CompilerParams(vmem_limit_bytes=20 * MIB),
        cost_estimate=took(3),
        name="late_out",
    )(*inputs)


def band_to_windows(band_values, win_count):
    trailing = band_values.shape[2:]
    blocks = band_values.reshape(
        (band_values.shape[0] // WIN_SIDE, WIN_SIDE, REG_SIDE, WIN_SIDE) + trailing
    )
    return jnp.swapaxes(blocks, 1, 2).reshape((win_count, WIN_SIDE * WIN_SIDE) + trailing)


def rank_of(keys):
    return jnp.sum(keys[None, :] < keys[:, None], axis=1)


def reduce_stages():
    img_bits = [("img", bit) for bit in range(lax.axis_size("img").bit_length() - 1)]
    dp_bits = [("dp", bit) for bit in range(lax.axis_size("dp").bit_length() - 1)]
    rest = img_bits[1:] + dp_bits
    return [img_bits[:1]] + [rest[at : at + 2] for at in range(0, len(rest), 2)]


def stage_masks(stage):
    img_size = lax.axis_size("img")
    return [(1 << bit) * (img_size if name == "dp" else 1) for name, bit in stage]


def stage_moves(stage):
    devices = lax.axis_size("dp") * lax.axis_size("img")
    moves = []
    for offset in range(1, 1 << len(stage)):
        flip = sum(mask for place, mask in enumerate(stage_masks(stage)) if offset >> place & 1)
        moves.append((offset, [(at, at ^ flip) for at in range(devices)]))
    return moves


def own_share(stages):
    flat = lax.axis_index("dp") * lax.axis_size("img") + lax.axis_index("img")
    share = 0
    for stage in stages:
        own = sum(((flat // mask) % 2) << place for place, mask in enumerate(stage_masks(stage)))
        share = (share << len(stage)) + own
    return share


def swap(rows, pairs):
    return lax.ppermute(rows, ("dp", "img"), pairs)


def add_up(pieces):
    return sum(piece.astype(f32) for piece in pieces).astype(bf16)


def split_sum(pieces, stage):
    parts = [piece.reshape((1 << len(stage), -1) + piece.shape[1:]) for piece in pieces]
    return [add_up([part[place] for part in parts]) for place in range(1 << len(stage))]


def sum_parts(parts, stage):
    return [parts[0]] + [swap(parts[offset], pairs) for offset, pairs in stage_moves(stage)]


def sum_stage(rows, stage):
    return add_up(sum_parts(rows.reshape((1 << len(stage), -1) + rows.shape[1:]), stage))


def gather_parts(rows, stage):
    return [rows] + [swap(rows, pairs) for _, pairs in stage_moves(stage)]


def gather_stage(rows, stage):
    return jnp.concatenate(gather_parts(rows, stage), axis=0)


def sum_stages(rows, stages):
    for stage in stages:
        rows = sum_stage(rows, stage)
    return rows


def deal_kernel(pick_ref, region_ref, local_ref, out_ref, rows_in, rows_out, came, gone):
    groups = out_ref.shape[0]
    positions = rows_in.shape[0]
    part = positions // DEAL_PARTS

    def copy_in(at):
        low = at * part
        if at == 0:
            return [
                pltpu.make_async_copy(region_ref, rows_in.at[0], came.at[DEAL_PARTS]),
                pltpu.make_async_copy(local_ref.at[: part - 1], rows_in.at[1:part], came.at[0]),
            ]
        return [
            pltpu.make_async_copy(local_ref.at[low - 1 : low + part - 1], rows_in.at[low : low + part], came.at[at])
        ]

    def copy_out(at):
        rows = slice(at * part * TILE, (at + 1) * part * TILE)
        return pltpu.make_async_copy(rows_out.at[:, rows, :], out_ref.at[:, rows, :], gone.at[at])

    for at in range(DEAL_PARTS):
        for copy in copy_in(at):
            copy.start()
    for at in range(DEAL_PARTS):
        for copy in copy_in(at):
            copy.wait()
        pairs = range(at * part // 2, (at + 1) * part // 2)
        dealt = [
            dot(pick_ref[...], jnp.concatenate([rows_in[2 * pair], rows_in[2 * pair + 1]], axis=0))
            for pair in pairs
        ]
        for pair, rows in zip(pairs, dealt):
            rows_out[:, 16 * pair : 16 * pair + 16, :] = rows.astype(bf16).reshape(groups, 16, WIDTH)
        copy_out(at).start()
    for at in range(DEAL_PARTS):
        copy_out(at).wait()


def collect_kernel(pick_ref, came_ref, region_ref, local_ref, rows_in, rows_out, came, gone):
    slots = region_ref.shape[0]
    positions = rows_out.shape[0]
    part = positions // DEAL_PARTS

    def copy_in(at):
        rows = slice(at * part * TILE, (at + 1) * part * TILE)
        return pltpu.make_async_copy(came_ref.at[:, rows, :], rows_in.at[:, rows, :], came.at[at])

    def copy_out(at):
        low = at * part
        if at == 0:
            return [
                pltpu.make_async_copy(rows_out.at[0], region_ref, gone.at[DEAL_PARTS]),
                pltpu.make_async_copy(rows_out.at[1:part], local_ref.at[: part - 1], gone.at[0]),
            ]
        return [
            pltpu.make_async_copy(rows_out.at[low : low + part], local_ref.at[low - 1 : low + part - 1], gone.at[at])
        ]

    for at in range(DEAL_PARTS):
        copy_in(at).start()
    for at in range(DEAL_PARTS):
        copy_in(at).wait()
        pairs = range(at * part // 2, (at + 1) * part // 2)
        dealt = [
            dot(pick_ref[...], rows_in[:, 16 * pair : 16 * pair + 16, :].reshape(2 * slots, WIDTH)) for pair in pairs
        ]
        for pair, rows in zip(pairs, dealt):
            rows = rows.astype(bf16)
            rows_out[2 * pair] = rows[:slots]
            rows_out[2 * pair + 1] = rows[slots:]
        for copy in copy_out(at):
            copy.start()
    for at in range(DEAL_PARTS):
        for copy in copy_out(at):
            copy.wait()


def run_deal(pick, region, local):
    slots = region.shape[0]
    count, positions = slots // TILE, local.shape[0] + 1
    return pl.pallas_call(
        deal_kernel,
        in_specs=[pl.BlockSpec(memory_space=pltpu.VMEM)] + [pl.BlockSpec(memory_space=pl.ANY)] * 2,
        out_specs=pl.BlockSpec(memory_space=pl.ANY),
        out_shape=jax.ShapeDtypeStruct((count, positions * TILE, WIDTH), bf16),
        scratch_shapes=[
            pltpu.VMEM((positions, slots, WIDTH), bf16),
            pltpu.VMEM((count, positions * TILE, WIDTH), bf16),
            pltpu.SemaphoreType.DMA((DEAL_PARTS + 1,)),
            pltpu.SemaphoreType.DMA((DEAL_PARTS,)),
        ],
        compiler_params=pltpu.CompilerParams(vmem_limit_bytes=VMEM_LIMIT),
        cost_estimate=took(4),
        name="deal",
    )(pick, region, local)


def run_collect(pick, came):
    count, rows, _ = came.shape
    slots, positions = count * TILE, rows // TILE
    anywhere = pl.BlockSpec(memory_space=pl.ANY)
    return pl.pallas_call(
        collect_kernel,
        in_specs=[pl.BlockSpec(memory_space=pltpu.VMEM), anywhere],
        out_specs=[anywhere] * 2,
        out_shape=[
            jax.ShapeDtypeStruct((slots, WIDTH), bf16),
            jax.ShapeDtypeStruct((positions - 1, slots, WIDTH), bf16),
        ],
        scratch_shapes=[
            pltpu.VMEM((count, rows, WIDTH), bf16),
            pltpu.VMEM((positions, slots, WIDTH), bf16),
            pltpu.SemaphoreType.DMA((DEAL_PARTS,)),
            pltpu.SemaphoreType.DMA((DEAL_PARTS + 1,)),
        ],
        compiler_params=pltpu.CompilerParams(vmem_limit_bytes=VMEM_LIMIT),
        cost_estimate=took(0.3),
        name="collect",
    )(pick, came)


def swap_tiles(tiles_sent, devices):
    count, rows, width = tiles_sent.shape
    share = count * TILE // devices
    if share == TILE:
        return lax.all_to_all(tiles_sent, "dp", split_axis=0, concat_axis=0, tiled=True)
    places = rows // TILE
    sent = tiles_sent.reshape(count, places, TILE, width).transpose(1, 0, 2, 3)
    sent = sent.reshape(places, devices, share, width).transpose(1, 0, 2, 3)
    came = lax.all_to_all(sent, "dp", split_axis=0, concat_axis=0, tiled=True)
    came = came.transpose(1, 0, 2, 3).reshape(places, count, TILE, width)
    return came.transpose(1, 0, 2, 3).reshape(count, rows, width)


def row_maps():
    window = np.arange(TILE)[:, None]
    place = np.arange(WIN_SIDE * WIN_SIDE)[None, :]
    raster = place // WIN_SIDE * (TILE * WIN_SIDE) + window * WIN_SIDE + place % WIN_SIDE
    band = TILE * WIN_SIDE * WIN_SIDE
    spread = np.zeros((TILE * SLOT, band), np.float32)
    spread[window * SLOT + 1 + place, raster] = 1
    gather = np.zeros((band, TILE * SLOT), np.float32)
    gather[raster, window * SLOT + 1 + place] = 1
    place = np.arange(WIN_SIDE * WIN_SIDE + 1)[None, :]
    squeeze = np.zeros(((WIN_SIDE * WIN_SIDE + 1) * TILE, TILE * TALL), np.float32)
    squeeze[place * TILE + window, window * TALL + place] = 1
    return [jnp.asarray(table, bf16) for table in (spread, gather, squeeze, squeeze.T)]


def shards(
    tokens,
    regional,
    pad_mask,
    keep_mask,
    window_slot,
    ln1_gain,
    ln1_bias,
    w_qkv,
    bias_q,
    bias_v,
    w_out,
    bias_out,
    ln2_gain,
    ln2_bias,
    w_fc1,
    bias_fc1,
    w_fc2,
    bias_fc2,
    cot_local,
    cot_regional,
):
    devices = lax.axis_size("dp")
    stages = reduce_stages()
    parts = devices * lax.axis_size("img")
    own_rank = lax.axis_index("dp")
    win_count = regional.shape[1]
    all_windows = window_slot.shape[1]
    slot_of = window_slot[0]
    places = jnp.arange(win_count)
    own_target = lax.dynamic_slice_in_dim(slot_of, own_rank * win_count, win_count) // win_count
    own_place = rank_of(own_target * win_count + places)
    order = jnp.sum(jnp.where(own_place[None, :] == places[:, None], places[None, :], 0), axis=1)
    slot_hit = slot_of[None, :] == (own_rank * win_count + places)[:, None]
    window_here = jnp.sum(jnp.where(slot_hit, jnp.arange(all_windows)[None, :], 0), axis=1)
    here_place = rank_of(window_here)
    deal_row = jnp.arange(2 * win_count)
    row_place = deal_row // (2 * TILE) * TILE + deal_row % TILE
    row_half = deal_row // TILE % 2
    column_hit = row_place[:, None] == jnp.concatenate([here_place, here_place])[None, :]
    pick = (column_hit & (row_half[:, None] == (deal_row // win_count)[None, :])).astype(bf16)
    pick_back = (column_hit & (row_half[:, None] == (deal_row // win_count)[None, :])).T.astype(bf16)
    cot = swap_tiles(
        run_deal(pick, cot_regional[0], jnp.swapaxes(cot_local[0], 0, 1)), devices
    )
    image = own_rank * win_count // REGIONS
    keep = lax.dynamic_slice_in_dim(keep_mask[0], image, 1).astype(f32) / survive
    live = band_to_windows(pad_mask[0], win_count) != 0
    allowed = jnp.concatenate(
        [jnp.ones((win_count, 1), bool), live, jnp.zeros((win_count, SLOT - 1 - live.shape[1]), bool)],
        axis=1,
    )
    window_bias = jnp.broadcast_to(
        jnp.where(allowed, 0.0, -1e30).astype(bf16)[:, :, None], (win_count, SLOT, LANES)
    )
    region_bias = jnp.broadcast_to(
        jnp.where(live[:, 0], 0.0, -1e30).astype(bf16)[:, None], (win_count, LANES)
    )
    spread, gather, squeeze, stretch = row_maps()
    plain, mixed_mask = head_masks()
    gain1, bias1, gain2, bias2 = ln1_gain[None], ln1_bias[None], ln2_gain[None], ln2_bias[None]
    out, qkv, probs, joined, mixed, after, hidden, slope, qkv_r, probs_r, mixed_r = run_forward(
        order, keep, tokens.reshape(REG_SIDE, -1, WIDTH), regional[0], window_bias, region_bias,
        spread, squeeze, plain, mixed_mask, gain1, bias1, w_qkv, bias_q[None], bias_v[None], w_out, bias_out[None],
        gain2, bias2, w_fc1, bias_fc1[None], w_fc2, bias_fc2[None],
    )
    came = swap_tiles(out, devices)
    own = own_share(stages)[None]
    grad_after, grad_mixed, early, early_sent, grad_out, small, row_fc1 = run_back_mlp(
        parts, keep, own, cot, after, mixed, hidden, slope, stretch, gain2, bias2, w_fc1, w_fc2, w_out
    )
    (_, pairs), = stage_moves(stages[0])
    early_came = swap(early_sent, pairs)
    attention = (
        order, keep, own, qkv, probs, joined, grad_mixed, grad_after, plain, mixed_mask, gain1, bias1
    )
    tile_count = win_count // TILE
    xy_stage, (z_stage, *more) = stages[1], stages[2:]
    grad_qkv, *held = run_back_attention(0, ATTENTION_FIRST, *attention)
    early = split_sum([early, early_came], xy_stage)
    held, early, came = lax.optimization_barrier((held, early, came))
    early = add_up(sum_parts(early, xy_stage))
    grad_qkv, late, late_sent, regional_out = run_back_attention(
        ATTENTION_FIRST,
        tile_count - ATTENTION_FIRST,
        *attention,
        held=(*held, grad_qkv),
        ending=(grad_out, order[None], regional[0], qkv_r, probs_r, mixed_r, w_qkv, w_out, small, row_fc1),
        parts=parts,
    )
    late_came = swap(late_sent, pairs)
    grad_qkv, early = lax.optimization_barrier((grad_qkv, early))
    early = sum_parts(split_sum([early], z_stage), z_stage)
    rows = (order, grad_qkv, joined, grad_after, gain1, w_qkv)
    windows = run_back_rows(*rows, 0, ROWS_FIRST)
    windows, late_came = lax.optimization_barrier((windows, late_came))
    late = sum_parts(split_sum([late, late_came], xy_stage), xy_stage)
    windows, early = lax.optimization_barrier((windows, early))
    early = sum_stages(add_up(early), more)
    for stage in reversed(more):
        early = gather_stage(early, stage)
    early = gather_parts(early, z_stage)
    windows = run_back_rows(*rows, ROWS_FIRST, tile_count - ROWS_FIRST, held=windows)
    windows, early, late = lax.optimization_barrier((windows, early, late))
    late = sum_parts(split_sum([add_up(late)], z_stage), z_stage)
    early = jnp.concatenate(early, axis=0)
    moves = stage_moves(xy_stage)
    early = [early] + [swap(early, moves[at][1]) for at in range(2)]
    tokens_out = run_relay(gather, windows)
    tokens_out, came, early, late = lax.optimization_barrier((tokens_out, came, early, late))
    late = sum_stages(add_up(late), more)
    for stage in reversed(more):
        late = gather_stage(late, stage)
    late = gather_parts(late, z_stage)
    (_, across), = moves[2:]
    early_last = swap(early[0], across)
    early = jnp.concatenate(early, axis=0)
    early_far = swap(early, pairs)
    came, early_far, late = lax.optimization_barrier((came, early_far, late))
    late = gather_parts(jnp.concatenate(late, axis=0), xy_stage)
    grad_w_fc1, grad_w_fc2 = run_early_out(own, early, early_far, w_fc1.shape[1])
    out_regional, out_local = run_collect(pick_back, came)
    late_far = [swap(late[0], pairs)]
    grad_w_fc1, grad_w_fc2, out_local, early_last, late, late_far = lax.optimization_barrier(
        (grad_w_fc1, grad_w_fc2, out_local, early_last, late, late_far)
    )
    early_last = [early_last, swap(early_last, pairs)]
    late_far += [swap(piece, pairs) for piece in late[1:]]
    grad_w_qkv, grad_w_out, *vectors, grad_w_fc1, grad_w_fc2 = run_late_out(
        own, late + late_far, early_last, grad_w_fc1, grad_w_fc2
    )
    vectors = [vector[0] for vector in vectors]
    return (
        jnp.swapaxes(out_local, 0, 1)[None],
        out_regional[None],
        tokens_out.reshape(tokens.shape),
        regional_out[None],
        vectors[0],
        vectors[1],
        grad_w_qkv,
        vectors[2],
        vectors[3],
        grad_w_out,
        vectors[4],
        vectors[5],
        vectors[6],
        grad_w_fc1,
        vectors[8],
        grad_w_fc2,
        vectors[7],
    )


def solution(mesh):
    in_specs = (
        P("img", "dp", None, None),
        P("img", "dp", None),
        P("img", "dp", None),
        P("img", None),
        P("img", None),
        P(),
        P(),
        P(),
        P(),
        P(),
        P(),
        P(),
        P(),
        P(),
        P(),
        P(),
        P(),
        P(),
        P("img", "dp", None, None),
        P("img", "dp", None),
    )
    out_specs = (
        P("img", "dp", None, None),
        P("img", "dp", None),
        P("img", "dp", None, None),
        P("img", "dp", None),
        P(),
        P(),
        P(),
        P(),
        P(),
        P(),
        P(),
        P(),
        P(),
        P(),
        P(),
        P(),
        P(),
    )
    return jax.shard_map(shards, mesh=mesh, in_specs=in_specs, out_specs=out_specs, check_vma=False)
```
